32 devices in a mesh: wide: 8 (over y, x, core), narrow: 4 (over z).
Axes of the slice: x: 2, y: 2, z: 4, core: 2. Of those that a mesh axis runs over, the one named last changes fastest.
Arguments:
- loads: float32 [24576, 512], P('wide', 'narrow'), may hold values from -6 to 6
- start: float32 [24576, 512], P('wide', 'narrow'), may hold values from -6 to 6
- stiffness: bfloat16 [32, 1024, 1024], P('wide')
- local_inverse: bfloat16 [32, 1024, 1024], P('wide')
- modes: bfloat16 [32, 1024, 32], P('wide'), may hold values from -0.1875 to 0.1875
- coarse_inverse: float32 [1024, 1024], P('wide', 'narrow'), as said below
- margin_rows: int32 [32, 256], P('wide'), may hold values from 0 to 24575, as said below
Outputs:
- displacement: float32 [24576, 512], P('wide', 'narrow')
- final_residual: float32 [24576, 512], P('wide', 'narrow')
The draws below stay inside these ranges and needn't reach their ends.
Inputs may be any that keep to these rules, and one draw needn't show every extreme that they name: Row s lists 256 distinct rows of loads, none of them rows s * 768 to s * 768 + 767. Call rows i * 4 * 768 to (i + 1) * 4 * 768 - 1 block i. For every i, the entries of rows i * 4 to (i + 1) * 4 - 1 of margin_rows fall at most 192 times into any one block, and exactly 192 times into some block. coarse_inverse equals its transpose.
All inputs are finite; a program needn't handle non-finite values.
Results may differ from the reference program's by a relative error of at most 0.0062.
Values may be sent and summed in bfloat16 or wider, within the bound.
No kernel may reach another device: no remote copies, remote signals or barrier semaphores. Data moves between devices by JAX's collectives and lax.ppermute only.
A program may use at most 128 MiB of HBM per device.

```python
import math
import jax
import jax.numpy as jnp
from jax import lax

SUBN = 1024
OVL = 256
MODES = 32
SUB_DEV = 4
COLS = 512
ITERS = 2
CORE = 768
NSUB = 32
NC = 1024
NDOF = 24576


def with_diagonal(random_part, key_diag, lowest, highest):
    lead_shape = random_part.shape[:-1]
    matrix_order = random_part.shape[-1]
    log_diag = jax.random.uniform(key_diag, lead_shape, jnp.float32, math.log(lowest), math.log(highest))
    identity = jnp.eye(matrix_order, dtype=jnp.float32)
    return random_part * (1.0 - identity) + identity * jnp.exp(log_diag)[..., None]


def draw_stiffness(key, part):
    key_off, key_diag = jax.random.split(jax.random.fold_in(key, 11))
    random_part = jax.random.normal(key_off, (NSUB, SUBN, SUBN), jnp.float32)
    return with_diagonal(random_part * (0.6 / math.sqrt(SUBN)), key_diag, 1.0, 2.0).astype(jnp.bfloat16)


def draw_local_inverse(key, part):
    key_off, key_diag = jax.random.split(jax.random.fold_in(key, 23))
    random_part = jax.random.normal(key_off, (NSUB, SUBN, SUBN), jnp.float32)
    return with_diagonal(random_part * (0.3 / math.sqrt(SUBN)), key_diag, 0.5, 1.0).astype(jnp.bfloat16)


def draw_coarse_inverse(key, part):
    key_off, key_diag = jax.random.split(jax.random.fold_in(key, 37))
    random_part = jax.random.normal(key_off, (NC, NC), jnp.float32)
    symmetric = (random_part + random_part.T) * 0.70710678
    return with_diagonal(symmetric * (2.0 / math.sqrt(NC)), key_diag, 0.5, 1.0)


def pick_from(table, block_of):
    return jnp.take_along_axis(table, block_of, axis=1)


def draw_margin_rows(key, part):
    owners = NSUB // SUB_DEV
    average = SUB_DEV * OVL // owners
    spread_most = average // 2
    halves = owners // 2
    core_count = SUBN - OVL
    key_lift, key_pick, key_sign, key_slot, key_self, key_start = jax.random.split(jax.random.fold_in(key, 51), 6)
    deviation = jax.random.randint(key_lift, (owners, halves), 0, spread_most + 1)
    chosen = jax.random.randint(key_pick, (owners, 1), 0, halves)
    deviation = jnp.where(jnp.arange(halves, dtype=jnp.int32)[None, :] == chosen, spread_most, deviation)
    direction = jax.random.randint(key_sign, (owners, halves), 0, 2) * 2 - 1
    counts = jnp.stack([average + direction * deviation, average - direction * deviation], axis=2).reshape(owners, owners)
    block_end = jnp.cumsum(counts, axis=1)
    starts = block_end - counts
    source_slot = jax.random.randint(key_slot, (owners, owners), 0, SUB_DEV)
    self_slot = jax.random.randint(key_self, (owners, 1), 1, SUB_DEV)
    source_slot = jnp.where(jnp.arange(owners, dtype=jnp.int32)[None, :] == 0, self_slot, source_slot)
    window = jax.random.randint(key_start, (owners, owners), 0, core_count - counts + 1)
    positions = jnp.arange(SUB_DEV * OVL, dtype=jnp.int32)
    block_of = jnp.sum((block_end[:, None, :] <= positions[None, :, None]).astype(jnp.int32), axis=2)
    source = (jnp.arange(owners, dtype=jnp.int32)[:, None] + block_of) % owners
    global_rows = source * (SUB_DEV * core_count) + pick_from(source_slot, block_of) * core_count
    global_rows = global_rows + pick_from(window, block_of) + positions[None, :] - pick_from(starts, block_of)
    return global_rows.reshape(NSUB, OVL).astype(jnp.int32)


def level_of(stream_key, dims, cuts, least, top_value):
    loudness, own = 1.0, jax.random.fold_in(stream_key, 6)
    for axis_at, blocks in cuts:
        steps = jnp.exp(jax.random.uniform(jax.random.fold_in(own, axis_at), (blocks,), jnp.float32, least / len(cuts), top_value / len(cuts)))
        loudness = loudness * jnp.repeat(steps, dims[axis_at] // blocks).reshape([-1 if axis == axis_at else 1 for axis in range(len(dims))])
    return loudness


def scatter_about(key, shape, scale, most, pieces=(), kind=jnp.bfloat16):
    values = jax.random.normal(key, shape, jnp.float32) * scale
    if len(pieces) > 0:
        values = level_of(key, shape, pieces, -0.22, 0.18) * values
    return jnp.clip(values, min=-most, max=most).astype(kind)


def setup_inputs(seed: int = 0) -> dict:
    arg_keys = jax.random.split(jax.random.key(seed), 8)
    return {
        "loads": scatter_about(arg_keys[0], (NDOF, COLS), 1.0, 6.0, ((0, 8), (1, 4)), jnp.float32),
        "start": scatter_about(arg_keys[1], (NDOF, COLS), 1.0, 6.0, ((0, 8), (1, 4)), jnp.float32),
        "stiffness": draw_stiffness(jax.random.fold_in(arg_keys[7], 71), 0),
        "local_inverse": draw_local_inverse(jax.random.fold_in(arg_keys[7], 71), 0),
        "modes": scatter_about(arg_keys[4], (NSUB, SUBN, MODES), SUBN ** -0.5, 0.1875, ((0, 8),)),
        "coarse_inverse": draw_coarse_inverse(jax.random.fold_in(arg_keys[7], 71), 0),
        "margin_rows": draw_margin_rows(jax.random.fold_in(arg_keys[7], 71), 0),
    }


damping = 0.5


def gather_local(field, margin_rows):
    core_part = field.reshape(NSUB, CORE, COLS)
    outer_part = field[margin_rows.reshape(-1)].reshape(NSUB, OVL, COLS)
    return jnp.concatenate([core_part, outer_part], axis=1).astype(jnp.bfloat16)


def assemble_parts(parts, margin_rows):
    summed = parts[:, :CORE, :].reshape(NSUB * CORE, COLS)
    return summed.at[margin_rows.reshape(-1)].add(parts[:, CORE:, :].reshape(NSUB * OVL, COLS))


def apply_each(matrices, vectors):
    def single(operands):
        return jnp.dot(operands[0].astype(jnp.float32), operands[1].astype(jnp.float32), precision=lax.Precision.HIGHEST)
    return lax.map(single, (matrices, vectors))


def project_modes(modes, vectors):
    def single(operands):
        return jnp.dot(operands[0].astype(jnp.float32).T, operands[1].astype(jnp.float32), precision=lax.Precision.HIGHEST)
    return lax.map(single, (modes, vectors))


def residual_of(field, loads, stiffness, margin_rows):
    return loads - assemble_parts(apply_each(stiffness, gather_local(field, margin_rows)), margin_rows)


def reference(loads, start, stiffness, local_inverse, modes, coarse_inverse, margin_rows):
    field = start
    for iteration in range(ITERS):
        residual = residual_of(field, loads, stiffness, margin_rows)
        restricted = gather_local(residual, margin_rows)
        solved_local = apply_each(local_inverse, restricted)
        projection = project_modes(modes, restricted).reshape(NC, COLS)
        coarse = jnp.dot(coarse_inverse, projection, precision=lax.Precision.HIGHEST).reshape(NSUB, MODES, COLS)
        lifted = apply_each(modes, coarse)
        field = field + assemble_parts(damping * solved_local + lifted, margin_rows)
    return field, residual_of(field, loads, stiffness, margin_rows)
```

```python
import jax
import jax.numpy as jnp
from jax import lax
from jax.sharding import PartitionSpec as P

ITERS = 2
damping = 0.5


def dot(a, b, **kw):
    return jnp.dot(a, b, preferred_element_type=jnp.float32, **kw)


def swap(blocks, owners):
    out = [blocks[0]]
    for k in range(1, owners):
        out.append(lax.ppermute(blocks[k], "wide", [(i, i ^ k) for i in range(owners)]))
    return out


def shards(loads, start, stiffness, local_inverse, modes, coarse_inverse, margin_rows):
    owners = lax.axis_size("wide")
    me = lax.axis_index("wide")
    subs, margins = margin_rows.shape
    order = stiffness.shape[1]
    core = order - margins
    held, cols = loads.shape
    mode_count = modes.shape[2]
    coarse_rows = subs * mode_count
    capacity = 3 * subs * margins // (2 * owners)
    slots = owners * capacity

    flat = margin_rows.reshape(-1)
    source = flat // held
    row = flat - source * held
    relative = source ^ me
    onehot = (relative[:, None] == jnp.arange(owners, dtype=jnp.int32)[None, :]).astype(jnp.bfloat16)
    many = subs * margins
    earlier = (jnp.arange(many)[:, None] > jnp.arange(many)[None, :]).astype(jnp.bfloat16)
    rank = jnp.sum(dot(earlier, onehot) * onehot.astype(jnp.float32), axis=1).astype(jnp.int32)
    place = relative * capacity + rank
    hit = place[:, None] == jnp.arange(slots, dtype=jnp.int32)[None, :]
    to_slots = hit.astype(jnp.bfloat16)
    asked = jnp.sum(jnp.where(hit, row[:, None] + 1, 0), axis=0) - 1
    asked = asked.reshape(owners, capacity)
    wanted = jnp.concatenate(swap([asked[k] for k in range(owners)], owners))
    pick = (wanted[:, None] == jnp.arange(held, dtype=jnp.int32)[None, :]).astype(jnp.bfloat16)
    put = (jnp.arange(held, dtype=jnp.int32)[:, None] == wanted[None, :]).astype(jnp.bfloat16)

    full_rows = lax.all_gather(coarse_inverse, "narrow", axis=1, tiled=True)
    coarse_block = [
        lax.dynamic_slice_in_dim(full_rows, (me ^ k) * coarse_rows, coarse_rows, 1) for k in range(owners)
    ]

    def exchange(x):
        got = swap([x[k * capacity : (k + 1) * capacity] for k in range(owners)], owners)
        return jnp.concatenate(got, axis=0)

    def gather_local(field_low):
        outgoing = dot(pick, field_low).astype(jnp.bfloat16)
        incoming = exchange(outgoing)
        outer = dot(to_slots, incoming).astype(jnp.bfloat16).reshape(subs, margins, cols)
        return jnp.concatenate([field_low.reshape(subs, core, cols), outer], axis=1)

    def assemble(parts):
        outer = parts[:, core:, :].reshape(many, cols).astype(jnp.bfloat16)
        outgoing = lax.dot_general(
            to_slots, outer, (((0,), (0,)), ((), ())), preferred_element_type=jnp.float32
        ).astype(jnp.bfloat16)
        incoming = exchange(outgoing)
        return parts[:, :core, :].reshape(held, cols) + dot(put, incoming)

    def apply_each(matrices, vectors):
        return jnp.einsum("sij,sjc->sic", matrices, vectors, preferred_element_type=jnp.float32)

    def residual_of(field):
        return loads - assemble(apply_each(stiffness, gather_local(field.astype(jnp.bfloat16))))

    field = start
    for _ in range(ITERS):
        restricted = gather_local(residual_of(field).astype(jnp.bfloat16))
        projection = jnp.einsum(
            "sim,sic->smc", modes, restricted, preferred_element_type=jnp.float32
        ).reshape(coarse_rows, cols)
        everyone = swap([projection] * owners, owners)
        solved = apply_each(local_inverse, restricted)
        coarse = sum(
            dot(coarse_block[k], everyone[k], precision=lax.Precision.HIGHEST) for k in range(owners)
        ).reshape(subs, mode_count, cols)
        lifted = jnp.einsum(
            "sim,smc->sic", modes.astype(jnp.float32), coarse, precision=lax.Precision.HIGHEST
        )
        field = field + assemble(damping * solved + lifted)
    return field, residual_of(field)


def solution(mesh):
    placed = (
        P("wide", "narrow"),
        P("wide", "narrow"),
        P("wide", None, None),
        P("wide", None, None),
        P("wide", None, None),
        P("wide", "narrow"),
        P("wide", None),
    )
    return jax.shard_map(
        shards,
        mesh=mesh,
        in_specs=placed,
        out_specs=(P("wide", "narrow"), P("wide", "narrow")),
        check_vma=False,
    )
```

```python
import functools

import jax
import jax.numpy as jnp
from jax import lax
from jax.experimental import pallas as pl
from jax.experimental.pallas import tpu as pltpu
from jax.sharding import PartitionSpec as P

ITERS = 2
damping = 0.5
LANES = 128
CHUNK = 256
VMEM_LIMIT = 24 * 1024 * 1024
f32, bf16, i32 = jnp.float32, jnp.bfloat16, jnp.int32


def dot(a, b):
    return jnp.dot(a, b, preferred_element_type=f32)


def hot_rows(column, first, width):
    offset = column - lax.broadcasted_iota(i32, column.shape, 1)
    tiles = [(offset == first + t).astype(f32).astype(bf16) for t in range(0, width, LANES)]
    return jnp.concatenate(tiles, axis=1)


def hot_cols(row, first, height):
    numbers = lax.broadcasted_iota(i32, (height, row.shape[1]), 0) + first
    return (numbers == row).astype(f32).astype(bf16)


def hot_pairs(column, row):
    tiles = [
        (column == row[:, t : t + LANES]).astype(f32).astype(bf16) for t in range(0, row.shape[1], LANES)
    ]
    return jnp.concatenate(tiles, axis=1)


def chunks(count, body, size=CHUNK):
    def step(c, carry):
        body(pl.ds(pl.multiple_of(c * size, size), size), c * size)
        return carry

    lax.fori_loop(0, count // size, step, 0)


def call(body, grid, in_specs, out_specs, out_shape, scratch, flops, moved):
    return pl.pallas_call(
        body,
        grid=grid,
        in_specs=in_specs,
        out_specs=out_specs,
        out_shape=out_shape,
        scratch_shapes=scratch,
        compiler_params=pltpu.CompilerParams(vmem_limit_bytes=VMEM_LIMIT),
        cost_estimate=pl.CostEstimate(flops=int(flops), bytes_accessed=int(moved), transcendentals=0),
    )


def whole(shape):
    return pl.BlockSpec(shape, lambda s: (0,) * len(shape))


def open_body(field_ref, matrix_ref, low_ref, part_ref):
    low_ref[...] = field_ref[...].astype(bf16)

    def rows(at, _):
        part_ref[0, at, :] = dot(matrix_ref[0, at, :], low_ref[...])

    chunks(part_ref.shape[1], rows)


def first_body(low_ref, column_ref, out_ref):
    def rows(at, _):
        out_ref[at, :] = dot(hot_rows(column_ref[at, :], 0, low_ref.shape[0]), low_ref[...]).astype(bf16)

    chunks(out_ref.shape[0], rows)


def settle_body(sign, has_modes, base_ref, in_ref, row_ref, matrix_ref, *rest):
    if has_modes:
        modes_ref, field_ref, part_ref, proj_ref, low = rest
    else:
        field_ref, part_ref, low = rest
    core = field_ref.shape[0]
    first = pl.program_id(0) * core

    def fields(at, c):
        added = dot(hot_cols(row_ref[...], first + c, CHUNK), in_ref[...])
        value = base_ref[at, :] + sign * added
        field_ref[at, :] = value
        low[at, :] = value.astype(bf16)

    chunks(core, fields)
    if has_modes:
        proj_ref[...] = dot(modes_ref[0], low[...])

    def rows(at, _):
        part_ref[0, at, :] = dot(matrix_ref[0, at, :], low[...])

    chunks(part_ref.shape[1], rows)


def finish_body(sign, base_ref, in_ref, row_ref, field_ref):
    core = field_ref.shape[0]
    first = pl.program_id(0) * core

    def fields(at, c):
        added = dot(hot_cols(row_ref[...], first + c, CHUNK), in_ref[...])
        field_ref[at, :] = base_ref[at, :] + sign * added

    chunks(core, fields)


def take_margin(in_ref, column_ref, margin_ref, s, margins):
    at = pl.ds(s * margins, margins)
    taken = dot(hot_rows(column_ref[at, :], 0, in_ref.shape[0]), in_ref[...]).astype(bf16)
    margin_ref[at, :] = taken
    return taken


def pack(place_ref, outer, out_ref):
    def rows(at, c):
        out_ref[at, :] = dot(hot_cols(place_ref[...], c, CHUNK), outer[...]).astype(bf16)

    chunks(out_ref.shape[0], rows)


def outer_body(in_ref, column_ref, place_ref, matrix_ref, part_ref, margin_ref, out_ref, outer):
    subs, margins, _ = matrix_ref.shape
    for s in range(subs):
        taken = take_margin(in_ref, column_ref, margin_ref, s, margins)
        outer[pl.ds(s * margins, margins), :] = (part_ref[s] + dot(matrix_ref[s], taken)).astype(bf16)
    pack(place_ref, outer, out_ref)


def project_body(in_ref, column_ref, modes_ref, proj_ref, margin_ref, out_ref):
    subs, count, margins = modes_ref.shape
    for s in range(subs):
        taken = take_margin(in_ref, column_ref, margin_ref, s, margins)
        at = pl.ds(s * count, count)
        out_ref[at, :] = (proj_ref[at, :] + dot(modes_ref[s], taken)).astype(bf16)


def split(x):
    high = x.astype(bf16)
    return jnp.concatenate([high, (x - high.astype(f32)).astype(bf16)], axis=1)


def both(x):
    half = x.shape[1] // 2
    return x[:, :half] + x[:, half:]


def coarse_body(all_ref, inverse_ref, margin_ref, place_ref, matrix_ref, part_ref, modes_ref, coarse_ref, out_ref, outer):
    subs, margins, count = modes_ref.shape
    made = dot(inverse_ref[0], all_ref[...]) + dot(inverse_ref[1], all_ref[...])
    coarse_ref[...] = made
    halves = split(made)
    for s in range(subs):
        at = pl.ds(s * margins, margins)
        solved = part_ref[s] + dot(matrix_ref[s], margin_ref[at, :])
        lifted = both(dot(modes_ref[s], halves[s * count : (s + 1) * count]))
        outer[at, :] = (damping * solved + lifted).astype(bf16)
    pack(place_ref, outer, out_ref)


def inner_body(sign, has_modes, part_ref, matrix_ref, margin_ref, base_ref, column_ref, *rest):
    if has_modes:
        coarse_ref, modes_ref, new_ref, sent_ref, halves, total = rest
    else:
        new_ref, sent_ref, halves, total = rest
    s = pl.program_id(0)
    core = new_ref.shape[0]
    made = part_ref[0] + dot(matrix_ref[0], margin_ref[...])
    if has_modes:
        made = damping * made + both(dot(modes_ref[0], split(coarse_ref[...])))
    value = base_ref[...] + sign * made
    new_ref[...] = value
    halves[...] = split(value)

    @pl.when(s == 0)
    def _():
        total[...] = jnp.zeros_like(total)

    def rows(at, _):
        total[at, :] += dot(hot_rows(column_ref[at, :], s * core, core), halves[...])

    chunks(total.shape[0], rows)

    @pl.when(s == pl.num_programs(0) - 1)
    def _():
        sent_ref[...] = both(total[...])


def relay_body(sign, sent_ref, in_ref, column_ref, row_ref, out_ref):
    def rows(at, _):
        added = dot(hot_pairs(column_ref[at, :], row_ref[...]), in_ref[...])
        out_ref[at, :] = (sent_ref[at, :] + sign * added).astype(bf16)

    chunks(out_ref.shape[0], rows)


def shards(loads, start, stiffness, local_inverse, modes, coarse_inverse, margin_rows):
    owners = lax.axis_size("wide")
    subs, margins = margin_rows.shape
    order = stiffness.shape[1]
    core = order - margins
    held, cols = loads.shape
    count = modes.shape[2]
    coarse_rows = subs * count
    capacity = 3 * subs * margins // (2 * owners)
    slots = owners * capacity
    many = subs * margins
    m_at = core // margins

    flat = margin_rows.reshape(-1)
    source = flat // held
    row = flat - source * held
    onehot = (source[:, None] == jnp.arange(owners, dtype=i32)[None, :]).astype(bf16)
    earlier = (jnp.arange(many)[:, None] > jnp.arange(many)[None, :]).astype(bf16)
    rank = jnp.sum(dot(earlier, onehot) * onehot.astype(f32), axis=1).astype(i32)
    place = source * capacity + rank
    hit = place[:, None] == jnp.arange(slots, dtype=i32)[None, :]
    asked = jnp.sum(jnp.where(hit, row[:, None] + 1, 0), axis=0) - 1

    def trade(x):
        blocks = x.reshape((owners, x.shape[0] // owners) + x.shape[1:])
        got = lax.all_to_all(blocks, "wide", split_axis=0, concat_axis=0, tiled=True)
        return got.reshape(x.shape)

    wanted = trade(asked)
    wanted_row = wanted[None, :]
    wanted_column = jnp.broadcast_to(jnp.where(wanted < 0, -2, wanted)[:, None], (slots, LANES))
    place_row = place[None, :]
    place_column = jnp.broadcast_to(place[:, None], (many, LANES))
    modes_turned = jnp.swapaxes(modes, 1, 2)

    side = lax.axis_size("narrow")
    here = lax.axis_index("narrow")
    width = coarse_inverse.shape[1]
    coarse_full = jnp.zeros((coarse_rows, side * width), f32)
    for k in range(side):
        piece = coarse_inverse
        if k > 0:
            piece = lax.ppermute(coarse_inverse, "narrow", [(i, i ^ k) for i in range(side)])
        coarse_full = lax.dynamic_update_slice(coarse_full, piece, (0, (here ^ k) * width))
    high = coarse_full.astype(bf16)
    coarse_pair = jnp.stack([high, (coarse_full - high.astype(f32)).astype(bf16)])

    rows_spec = pl.BlockSpec((core, cols), lambda s: (s, 0))
    left_spec = pl.BlockSpec((1, order, core), lambda s: (s, 0, 0))
    part_spec = pl.BlockSpec((1, order, cols), lambda s: (s, 0, 0))
    slots_spec = whole((slots, cols))
    held_shape = jax.ShapeDtypeStruct((held, cols), f32)
    part_shape = jax.ShapeDtypeStruct((subs, order, cols), f32)
    slots_low = jax.ShapeDtypeStruct((slots, cols), bf16)
    margin_shape = jax.ShapeDtypeStruct((many, cols), bf16)
    matrix_flops = 2 * subs * order * core * cols
    slot_flops = 2 * held * slots * cols

    low, part = call(
        open_body, (subs,), [rows_spec, left_spec], [rows_spec, part_spec],
        [jax.ShapeDtypeStruct((held, cols), bf16), part_shape], [], matrix_flops, 10e6,
    )(start, stiffness)
    going = call(
        first_body, (1,), [whole((held, cols)), whole((slots, LANES))], slots_spec, slots_low, [], slot_flops, 2e6,
    )(low, wanted_column)

    def settle(sign, base, came, matrices, has_modes):
        specs = [rows_spec, slots_spec, whole((1, slots)), left_spec]
        args = [base, came, wanted_row, matrices]
        outs, shapes = [rows_spec, part_spec], [held_shape, part_shape]
        if has_modes:
            specs.append(pl.BlockSpec((1, count, core), lambda s: (s, 0, 0)))
            args.append(modes_turned[:, :, :core])
            outs.append(pl.BlockSpec((count, cols), lambda s: (s, 0)))
            shapes.append(jax.ShapeDtypeStruct((coarse_rows, cols), f32))
        return call(
            functools.partial(settle_body, sign, has_modes), (subs,), specs, outs, shapes,
            [pltpu.VMEM((core, cols), bf16)], slot_flops + matrix_flops, 14e6,
        )(*args)

    corner_spec = pl.BlockSpec((subs, margins, margins), lambda s: (0, m_at, m_at))
    part_outer_spec = pl.BlockSpec((subs, margins, cols), lambda s: (0, m_at, 0))
    outer_scratch = [pltpu.VMEM((many, cols), bf16)]

    def inner(sign, base, margin, part, matrices, coarse):
        specs = [
            pl.BlockSpec((1, core, cols), lambda s: (s, 0, 0)),
            pl.BlockSpec((1, core, margins), lambda s: (s, 0, m_at)),
            pl.BlockSpec((margins, cols), lambda s: (s, 0)),
            rows_spec,
            whole((slots, LANES)),
        ]
        args = [part, matrices, margin, base, wanted_column]
        if coarse is not None:
            specs += [
                pl.BlockSpec((count, cols), lambda s: (s, 0)),
                pl.BlockSpec((1, core, count), lambda s: (s, 0, 0)),
            ]
            args += [coarse, modes]
        return call(
            functools.partial(inner_body, sign, coarse is not None), (subs,), specs, [rows_spec, slots_spec],
            [held_shape, jax.ShapeDtypeStruct((slots, cols), f32)],
            [pltpu.VMEM((core, 2 * cols), bf16), pltpu.VMEM((slots, 2 * cols), f32)], 2 * slot_flops, 8e6,
        )(*args)

    def relay(sign, sent, came):
        return call(
            functools.partial(relay_body, sign), (1,),
            [slots_spec, slots_spec, whole((slots, LANES)), whole((1, slots))], slots_spec, slots_low, [],
            slot_flops // 2, 3e6,
        )(sent, came, wanted_column, wanted_row)

    def stiffness_outer(came, part):
        return call(
            outer_body, (1,),
            [slots_spec, whole((many, LANES)), whole((1, many)), corner_spec, part_outer_spec],
            [whole((many, cols)), slots_spec], [margin_shape, slots_low], outer_scratch, slot_flops, 3e6,
        )(came, place_column, place_row, stiffness, part)

    field = start
    for step in range(ITERS + 1):
        came = trade(going)
        if step > 0:
            field, part = settle(1.0, base, back, stiffness, False)
        margin, going = stiffness_outer(came, part)
        back = trade(going)
        base, sent = inner(-1.0, loads, margin, part, stiffness, None)
        if step == ITERS:
            break

        going = relay(-1.0, sent, back)
        came = trade(going)
        _, part, proj = settle(-1.0, base, back, local_inverse, True)
        projection, margin = None, None
        margin, projection = call(
            project_body, (1,),
            [slots_spec, whole((many, LANES)), whole((subs, count, margins)), whole((coarse_rows, cols))],
            [whole((many, cols)), whole((coarse_rows, cols))],
            [margin_shape, jax.ShapeDtypeStruct((coarse_rows, cols), bf16)], [], slot_flops // 2, 2e6,
        )(came, place_column, modes_turned[:, :, core:], proj)
        everyone = trade(jnp.tile(projection, (owners, 1)))
        coarse, going = call(
            coarse_body, (1,),
            [
                whole((owners * coarse_rows, cols)),
                whole((2, coarse_rows, owners * coarse_rows)),
                whole((many, cols)),
                whole((1, many)),
                corner_spec,
                part_outer_spec,
                whole((subs, margins, count)),
            ],
            [whole((coarse_rows, cols)), slots_spec],
            [jax.ShapeDtypeStruct((coarse_rows, cols), f32), slots_low], outer_scratch, slot_flops, 3e6,
        )(everyone, coarse_pair, margin, place_row, local_inverse, part, modes[:, core:, :])
        back = trade(going)
        base, sent = inner(1.0, field, margin, part, local_inverse, coarse)
        going = relay(1.0, sent, back)

    final = call(
        functools.partial(finish_body, -1.0), (subs,), [rows_spec, slots_spec, whole((1, slots))], rows_spec,
        held_shape, [], slot_flops, 4e6,
    )(base, back, wanted_row)
    return field, final


def solution(mesh):
    placed = (
        P("wide", "narrow"),
        P("wide", "narrow"),
        P("wide", None, None),
        P("wide", None, None),
        P("wide", None, None),
        P("wide", "narrow"),
        P("wide", None),
    )
    return jax.shard_map(
        shards,
        mesh=mesh,
        in_specs=placed,
        out_specs=(P("wide", "narrow"), P("wide", "narrow")),
        check_vma=False,
    )
```

```python
import functools

import jax
import jax.numpy as jnp
from jax import lax
from jax.experimental import pallas as pl
from jax.experimental.pallas import tpu as pltpu
from jax.sharding import PartitionSpec as P

ITERS = 2
damping = 0.5
LANES = 128
CHUNK = 256
VMEM_LIMIT = 58 * 1024 * 1024
f32, bf16, i32 = jnp.float32, jnp.bfloat16, jnp.int32


def dot(a, b):
    return jnp.dot(a, b, preferred_element_type=f32)


def hot_rows(column, first, width):
    offset = column - lax.broadcasted_iota(i32, column.shape, 1)
    tiles = [(offset == first + t).astype(f32).astype(bf16) for t in range(0, width, LANES)]
    return jnp.concatenate(tiles, axis=1)


def hot_cols(row, first, height):
    numbers = lax.broadcasted_iota(i32, (height, row.shape[1]), 0) + first
    return (numbers == row).astype(f32).astype(bf16)


def hot_pairs(column, row):
    tiles = [
        (column == row[:, t : t + LANES]).astype(f32).astype(bf16) for t in range(0, row.shape[1], LANES)
    ]
    return jnp.concatenate(tiles, axis=1)


def chunks(count, body, size=CHUNK):
    for first in range(0, count, size):
        body(pl.ds(first, size), first)


def turned_dot(a, b):
    return lax.dot_general(a, b, (((0,), (0,)), ((), ())), preferred_element_type=f32)


def call(body, grid, in_specs, out_specs, out_shape, scratch, flops, moved):
    return pl.pallas_call(
        body,
        grid=grid,
        in_specs=in_specs,
        out_specs=out_specs,
        out_shape=out_shape,
        scratch_shapes=scratch,
        compiler_params=pltpu.CompilerParams(vmem_limit_bytes=VMEM_LIMIT),
        cost_estimate=pl.CostEstimate(flops=int(flops), bytes_accessed=int(moved), transcendentals=0),
    )


def whole(shape):
    return pl.BlockSpec(shape, lambda s: (0,) * len(shape))


def open_body(field_ref, matrix_ref, low_ref, part_ref):
    low_ref[...] = field_ref[...].astype(bf16)
    part_ref[0] = dot(matrix_ref[0], low_ref[...])


def first_body(low_ref, column_ref, out_ref):
    def rows(at, _):
        out_ref[at, :] = dot(hot_rows(column_ref[at, :], 0, low_ref.shape[0]), low_ref[...]).astype(bf16)

    chunks(out_ref.shape[0], rows)


def settle_body(sign, has_modes, base_ref, in_ref, row_ref, matrix_ref, *rest):
    if has_modes:
        modes_ref, part_ref, proj_ref, low = rest
    else:
        field_ref, part_ref, low = rest
    core = base_ref.shape[0]
    first = pl.program_id(0) * core

    def fields(at, c):
        added = dot(hot_cols(row_ref[...], first + c, CHUNK), in_ref[...])
        value = base_ref[at, :] + sign * added
        if not has_modes:
            field_ref[at, :] = value
        low[at, :] = value.astype(bf16)

    chunks(core, fields)
    if has_modes:
        proj_ref[...] = dot(modes_ref[0], low[...])
    part_ref[0] = dot(matrix_ref[0], low[...])


def finish_body(sign, base_ref, in_ref, row_ref, field_ref):
    core = field_ref.shape[0]
    first = pl.program_id(0) * core

    def fields(at, c):
        added = dot(hot_cols(row_ref[...], first + c, CHUNK), in_ref[...])
        field_ref[at, :] = base_ref[at, :] + sign * added

    chunks(core, fields)


def take_margin(in_ref, column_ref, margin_ref, s, margins):
    at = pl.ds(s * margins, margins)
    taken = dot(hot_rows(column_ref[at, :], 0, in_ref.shape[0]), in_ref[...]).astype(bf16)
    margin_ref[at, :] = taken
    return taken


def pack(place_ref, outer, out_ref):
    def rows(at, c):
        out_ref[at, :] = dot(hot_cols(place_ref[...], c, CHUNK), outer[...]).astype(bf16)

    chunks(out_ref.shape[0], rows)


def outer_body(in_ref, column_ref, place_ref, matrix_ref, part_ref, margin_ref, out_ref, outer):
    subs, margins, _ = matrix_ref.shape
    for s in range(subs):
        taken = take_margin(in_ref, column_ref, margin_ref, s, margins)
        outer[pl.ds(s * margins, margins), :] = (part_ref[s] + dot(matrix_ref[s], taken)).astype(bf16)
    pack(place_ref, outer, out_ref)


def project_body(in_ref, column_ref, modes_ref, proj_ref, margin_ref, out_ref):
    subs, count, margins = modes_ref.shape
    for s in range(subs):
        taken = take_margin(in_ref, column_ref, margin_ref, s, margins)
        made = (proj_ref[pl.ds(s * count, count), :] + dot(modes_ref[s], taken)).astype(bf16)
        for first in range(0, out_ref.shape[0], subs * count):
            out_ref[pl.ds(first + s * count, count), :] = made


def split(x):
    high = x.astype(bf16)
    return jnp.concatenate([high, (x - high.astype(f32)).astype(bf16)], axis=1)


def both(x):
    half = x.shape[1] // 2
    return x[:, :half] + x[:, half:]


def coarse_body(side, here_ref, all_ref, *rest):
    inverse_refs = rest[:side]
    margin_ref, place_ref, matrix_ref, part_ref, modes_ref, coarse_ref, out_ref, outer = rest[side:]
    subs, count, margins = modes_ref.shape
    made = 0.0
    for k, inverse_ref in enumerate(inverse_refs):
        width = inverse_ref.shape[1]
        first = pl.multiple_of((here_ref[0] ^ k) * width, width)
        piece = inverse_ref[...]
        high = piece.astype(bf16)
        held = all_ref[pl.ds(first, width), :]
        made += dot(high, held) + dot((piece - high.astype(f32)).astype(bf16), held)
    coarse_ref[...] = made
    halves = split(made)
    for s in range(subs):
        at = pl.ds(s * margins, margins)
        solved = part_ref[s] + dot(matrix_ref[s], margin_ref[at, :])
        lifted = both(turned_dot(modes_ref[s], halves[s * count : (s + 1) * count]))
        outer[at, :] = (damping * solved + lifted).astype(bf16)
    pack(place_ref, outer, out_ref)


def inner_body(sign, has_modes, part_ref, matrix_ref, margin_ref, base_ref, column_ref, *rest):
    if has_modes:
        coarse_ref, modes_ref, new_ref, sent_ref, halves, total = rest
    else:
        new_ref, sent_ref, halves, total = rest
    s = pl.program_id(0)
    core = new_ref.shape[0]
    made = part_ref[0] + dot(matrix_ref[0], margin_ref[...])
    if has_modes:
        made = damping * made + both(turned_dot(modes_ref[0], split(coarse_ref[...])))
    value = base_ref[...] + sign * made
    new_ref[...] = value
    halves[...] = split(value)

    @pl.when(s == 0)
    def _():
        total[...] = jnp.zeros_like(total)

    def rows(at, _):
        total[at, :] += dot(hot_rows(column_ref[at, :], s * core, core), halves[...])

    chunks(total.shape[0], rows)

    @pl.when(s == pl.num_programs(0) - 1)
    def _():
        sent_ref[...] = both(total[...])


def relay_body(sign, sent_ref, in_ref, column_ref, row_ref, out_ref):
    def rows(at, _):
        added = dot(hot_pairs(column_ref[at, :], row_ref[...]), in_ref[...])
        out_ref[at, :] = (sent_ref[at, :] + sign * added).astype(bf16)

    chunks(out_ref.shape[0], rows)


def shards(loads, start, stiffness, local_inverse, modes, coarse_inverse, margin_rows):
    owners = lax.axis_size("wide")
    subs, margins = margin_rows.shape
    order = stiffness.shape[1]
    core = order - margins
    held, cols = loads.shape
    count = modes.shape[2]
    coarse_rows = subs * count
    capacity = 3 * subs * margins // (2 * owners)
    slots = owners * capacity
    many = subs * margins
    m_at = core // margins

    flat = margin_rows.reshape(-1)
    source = flat // held
    row = flat - source * held
    onehot = (source[:, None] == jnp.arange(owners, dtype=i32)[None, :]).astype(bf16)
    earlier = (jnp.arange(many)[:, None] > jnp.arange(many)[None, :]).astype(bf16)
    rank = jnp.sum(dot(earlier, onehot) * onehot.astype(f32), axis=1).astype(i32)
    place = source * capacity + rank
    hit = place[:, None] == jnp.arange(slots, dtype=i32)[None, :]
    asked = jnp.sum(jnp.where(hit, row[:, None] + 1, 0), axis=0) - 1

    def trade(x):
        blocks = x.reshape((owners, x.shape[0] // owners) + x.shape[1:])
        got = lax.all_to_all(blocks, "wide", split_axis=0, concat_axis=0, tiled=True)
        return got.reshape(x.shape)

    wanted = trade(asked)
    wanted_row = wanted[None, :]
    wanted_column = jnp.broadcast_to(jnp.where(wanted < 0, -2, wanted)[:, None], (slots, LANES))
    place_row = place[None, :]
    place_column = jnp.broadcast_to(place[:, None], (many, LANES))
    modes_turned = jnp.swapaxes(modes, 1, 2)

    rows_spec = pl.BlockSpec((core, cols), lambda s: (s, 0))
    left_spec = pl.BlockSpec((1, order, core), lambda s: (s, 0, 0))
    part_spec = pl.BlockSpec((1, order, cols), lambda s: (s, 0, 0))
    slots_spec = whole((slots, cols))
    held_shape = jax.ShapeDtypeStruct((held, cols), f32)
    part_shape = jax.ShapeDtypeStruct((subs, order, cols), f32)
    slots_low = jax.ShapeDtypeStruct((slots, cols), bf16)
    margin_shape = jax.ShapeDtypeStruct((many, cols), bf16)
    matrix_flops = 2 * subs * order * core * cols
    slot_flops = 2 * held * slots * cols

    low, part = call(
        open_body, (subs,), [rows_spec, left_spec], [rows_spec, part_spec],
        [jax.ShapeDtypeStruct((held, cols), bf16), part_shape], [], matrix_flops, 10e6,
    )(start, stiffness)
    going = call(
        first_body, (1,), [whole((held, cols)), whole((slots, LANES))], slots_spec, slots_low, [], slot_flops, 2e6,
    )(low, wanted_column)

    side = lax.axis_size("narrow")
    here = lax.axis_index("narrow").reshape(1).astype(i32)
    own, going = lax.optimization_barrier((coarse_inverse, going))
    pieces = [own] + [
        lax.ppermute(own, "narrow", [(i, i ^ k) for i in range(side)]) for k in range(1, side)
    ]
    core_modes_spec = pl.BlockSpec((1, count, core), lambda s: (s, 0, 0))
    outer_modes_spec = pl.BlockSpec((subs, count, margins), lambda s: (0, 0, m_at))

    def settle(sign, base, came, matrices, has_modes):
        specs = [rows_spec, slots_spec, whole((1, slots)), left_spec]
        args = [base, came, wanted_row, matrices]
        outs, shapes = [rows_spec, part_spec], [held_shape, part_shape]
        if has_modes:
            specs.append(core_modes_spec)
            args.append(modes_turned)
            outs = [part_spec, pl.BlockSpec((count, cols), lambda s: (s, 0))]
            shapes = [part_shape, jax.ShapeDtypeStruct((coarse_rows, cols), f32)]
        return call(
            functools.partial(settle_body, sign, has_modes), (subs,), specs, outs, shapes,
            [pltpu.VMEM((core, cols), bf16)], slot_flops + matrix_flops, 14e6,
        )(*args)

    corner_spec = pl.BlockSpec((subs, margins, margins), lambda s: (0, m_at, m_at))
    part_outer_spec = pl.BlockSpec((subs, margins, cols), lambda s: (0, m_at, 0))
    outer_scratch = [pltpu.VMEM((many, cols), bf16)]

    def inner(sign, base, margin, part, matrices, coarse):
        specs = [
            pl.BlockSpec((1, core, cols), lambda s: (s, 0, 0)),
            pl.BlockSpec((1, core, margins), lambda s: (s, 0, m_at)),
            pl.BlockSpec((margins, cols), lambda s: (s, 0)),
            rows_spec,
            whole((slots, LANES)),
        ]
        args = [part, matrices, margin, base, wanted_column]
        if coarse is not None:
            specs += [
                pl.BlockSpec((count, cols), lambda s: (s, 0)),
                core_modes_spec,
            ]
            args += [coarse, modes_turned]
        return call(
            functools.partial(inner_body, sign, coarse is not None), (subs,), specs, [rows_spec, slots_spec],
            [held_shape, jax.ShapeDtypeStruct((slots, cols), f32)],
            [pltpu.VMEM((core, 2 * cols), bf16), pltpu.VMEM((slots, 2 * cols), f32)], 2 * slot_flops, 8e6,
        )(*args)

    def relay(sign, sent, came):
        return call(
            functools.partial(relay_body, sign), (1,),
            [slots_spec, slots_spec, whole((slots, LANES)), whole((1, slots))], slots_spec, slots_low, [],
            slot_flops // 2, 3e6,
        )(sent, came, wanted_column, wanted_row)

    def stiffness_outer(came, part):
        return call(
            outer_body, (1,),
            [slots_spec, whole((many, LANES)), whole((1, many)), corner_spec, part_outer_spec],
            [whole((many, cols)), slots_spec], [margin_shape, slots_low], outer_scratch, slot_flops, 3e6,
        )(came, place_column, place_row, stiffness, part)

    field = start
    for step in range(ITERS + 1):
        came = trade(going)
        if step > 0:
            field, part = settle(1.0, base, back, stiffness, False)
        margin, going = stiffness_outer(came, part)
        back = trade(going)
        base, sent = inner(-1.0, loads, margin, part, stiffness, None)
        if step == ITERS:
            break

        going = relay(-1.0, sent, back)
        came = trade(going)
        part, proj = settle(-1.0, base, back, local_inverse, True)
        margin, projection = call(
            project_body, (1,),
            [slots_spec, whole((many, LANES)), outer_modes_spec, whole((coarse_rows, cols))],
            [whole((many, cols)), whole((owners * coarse_rows, cols))],
            [margin_shape, jax.ShapeDtypeStruct((owners * coarse_rows, cols), bf16)], [], slot_flops // 2, 2e6,
        )(came, place_column, modes_turned, proj)
        everyone = trade(projection)
        coarse, going = call(
            functools.partial(coarse_body, side), (1,),
            [pl.BlockSpec(memory_space=pltpu.SMEM), whole((owners * coarse_rows, cols))]
            + [whole(coarse_inverse.shape)] * side
            + [
                whole((many, cols)),
                whole((1, many)),
                corner_spec,
                part_outer_spec,
                outer_modes_spec,
            ],
            [whole((coarse_rows, cols)), slots_spec],
            [jax.ShapeDtypeStruct((coarse_rows, cols), f32), slots_low], outer_scratch, slot_flops, 3e6,
        )(here, everyone, *pieces, margin, place_row, local_inverse, part, modes_turned)
        back = trade(going)
        base, sent = inner(1.0, field, margin, part, local_inverse, coarse)
        going = relay(1.0, sent, back)

    final = call(
        functools.partial(finish_body, -1.0), (subs,), [rows_spec, slots_spec, whole((1, slots))], rows_spec,
        held_shape, [], slot_flops, 4e6,
    )(base, back, wanted_row)
    return field, final


def solution(mesh):
    placed = (
        P("wide", "narrow"),
        P("wide", "narrow"),
        P("wide", None, None),
        P("wide", None, None),
        P("wide", None, None),
        P("wide", "narrow"),
        P("wide", None),
    )
    return jax.shard_map(
        shards,
        mesh=mesh,
        in_specs=placed,
        out_specs=(P("wide", "narrow"), P("wide", "narrow")),
        check_vma=False,
    )
```

```python
import functools

import jax
import jax.numpy as jnp
from jax import lax
from jax.experimental import pallas as pl
from jax.experimental.pallas import tpu as pltpu
from jax.sharding import PartitionSpec as P

ITERS = 2
damping = 0.5
LANES = 128
CHUNK = 256
VMEM_LIMIT = 32 * 1024 * 1024
f32, bf16, i32 = jnp.float32, jnp.bfloat16, jnp.int32


def dot(a, b):
    return jnp.dot(a, b, preferred_element_type=f32)


def hot_rows(column, first, width):
    offset = column - lax.broadcasted_iota(i32, column.shape, 1)
    tiles = [(offset == first + t).astype(f32).astype(bf16) for t in range(0, width, LANES)]
    return jnp.concatenate(tiles, axis=1)


def hot_cols(row, first, height):
    numbers = lax.broadcasted_iota(i32, (height, row.shape[1]), 0) + first
    return (numbers == row).astype(f32).astype(bf16)


def hot_pairs(column, row):
    tiles = [
        (column == row[:, t : t + LANES]).astype(f32).astype(bf16) for t in range(0, row.shape[1], LANES)
    ]
    return jnp.concatenate(tiles, axis=1)


def chunks(count, body, size=CHUNK):
    for first in range(0, count, size):
        body(pl.ds(first, size), first)


def turned_dot(a, b):
    return lax.dot_general(a, b, (((0,), (0,)), ((), ())), preferred_element_type=f32)


def call(body, grid, in_specs, out_specs, out_shape, scratch, flops, moved, arrived=()):
    shapes = jax.tree.map(lambda x: pltpu.HBM(x.shape, x.dtype), out_shape)
    run = pl.pallas_call(
        body,
        grid=grid,
        in_specs=in_specs,
        out_specs=out_specs,
        out_shape=shapes,
        scratch_shapes=scratch,
        compiler_params=pltpu.CompilerParams(vmem_limit_bytes=VMEM_LIMIT),
        cost_estimate=pl.CostEstimate(flops=int(flops), bytes_accessed=int(moved), transcendentals=0),
    )

    def placed(i, x, spec):
        if spec.memory_space == pltpu.SMEM:
            return x
        return pltpu.with_memory_space_constraint(x, pltpu.VMEM if i in arrived else pltpu.HBM)

    return lambda *args: run(*(placed(i, x, spec) for i, (x, spec) in enumerate(zip(args, in_specs))))


def whole(shape):
    return pl.BlockSpec(shape, lambda s: (0,) * len(shape))


def open_body(field_ref, matrix_ref, low_ref, part_ref):
    low_ref[...] = field_ref[...].astype(bf16)
    part_ref[0] = dot(matrix_ref[0], low_ref[...])


def first_body(low_ref, column_ref, out_ref):
    def rows(at, _):
        out_ref[at, :] = dot(hot_rows(column_ref[at, :], 0, low_ref.shape[0]), low_ref[...]).astype(bf16)

    chunks(out_ref.shape[0], rows)


def settle_body(sign, has_modes, base_ref, in_ref, row_ref, matrix_ref, *rest):
    if has_modes:
        modes_ref, part_ref, proj_ref, low = rest
    else:
        field_ref, part_ref, low = rest
    core = base_ref.shape[0]
    first = pl.program_id(0) * core

    def fields(at, c):
        added = dot(hot_cols(row_ref[...], first + c, CHUNK), in_ref[...])
        value = base_ref[at, :] + sign * added
        if not has_modes:
            field_ref[at, :] = value
        low[at, :] = value.astype(bf16)

    chunks(core, fields)
    if has_modes:
        proj_ref[...] = dot(modes_ref[0], low[...])
    part_ref[0] = dot(matrix_ref[0], low[...])


def finish_body(sign, base_ref, in_ref, row_ref, field_ref):
    core = field_ref.shape[0]
    first = pl.program_id(0) * core

    def fields(at, c):
        added = dot(hot_cols(row_ref[...], first + c, CHUNK), in_ref[...])
        field_ref[at, :] = base_ref[at, :] + sign * added

    chunks(core, fields)


def take_margin(in_ref, column_ref, margin_ref, s, margins):
    at = pl.ds(s * margins, margins)
    taken = dot(hot_rows(column_ref[at, :], 0, in_ref.shape[0]), in_ref[...]).astype(bf16)
    margin_ref[at, :] = taken
    return taken


def pack(place_ref, outer, out_ref):
    def rows(at, c):
        out_ref[at, :] = dot(hot_cols(place_ref[...], c, CHUNK), outer[...]).astype(bf16)

    chunks(out_ref.shape[0], rows)


def outer_body(in_ref, column_ref, place_ref, matrix_ref, part_ref, margin_ref, out_ref, outer):
    subs, margins, _ = matrix_ref.shape
    for s in range(subs):
        taken = take_margin(in_ref, column_ref, margin_ref, s, margins)
        outer[pl.ds(s * margins, margins), :] = (part_ref[s] + dot(matrix_ref[s], taken)).astype(bf16)
    pack(place_ref, outer, out_ref)


def project_body(in_ref, column_ref, modes_ref, proj_ref, margin_ref, out_ref):
    subs, count, margins = modes_ref.shape
    for s in range(subs):
        taken = take_margin(in_ref, column_ref, margin_ref, s, margins)
        made = (proj_ref[pl.ds(s * count, count), :] + dot(modes_ref[s], taken)).astype(bf16)
        for first in range(0, out_ref.shape[0], subs * count):
            out_ref[pl.ds(first + s * count, count), :] = made


def split(x):
    high = x.astype(bf16)
    return jnp.concatenate([high, (x - high.astype(f32)).astype(bf16)], axis=1)


def both(x):
    half = x.shape[1] // 2
    return x[:, :half] + x[:, half:]


def coarse_body(side, here_ref, all_ref, *rest):
    inverse_refs = rest[:side]
    margin_ref, place_ref, matrix_ref, part_ref, modes_ref, coarse_ref, out_ref, outer = rest[side:]
    subs, count, margins = modes_ref.shape
    made = 0.0
    for k, inverse_ref in enumerate(inverse_refs):
        width = inverse_ref.shape[1]
        first = pl.multiple_of((here_ref[0] ^ k) * width, width)
        piece = inverse_ref[...]
        high = piece.astype(bf16)
        held = all_ref[pl.ds(first, width), :]
        made += dot(high, held) + dot((piece - high.astype(f32)).astype(bf16), held)
    coarse_ref[...] = made
    halves = split(made)
    for s in range(subs):
        at = pl.ds(s * margins, margins)
        solved = part_ref[s] + dot(matrix_ref[s], margin_ref[at, :])
        lifted = both(turned_dot(modes_ref[s], halves[s * count : (s + 1) * count]))
        outer[at, :] = (damping * solved + lifted).astype(bf16)
    pack(place_ref, outer, out_ref)


def inner_body(sign, has_modes, part_ref, matrix_ref, margin_ref, base_ref, column_ref, *rest):
    if has_modes:
        coarse_ref, modes_ref, new_ref, sent_ref, halves, total = rest
    else:
        new_ref, sent_ref, halves, total = rest
    s = pl.program_id(0)
    core = new_ref.shape[0]
    made = part_ref[0] + dot(matrix_ref[0], margin_ref[...])
    if has_modes:
        made = damping * made + both(turned_dot(modes_ref[0], split(coarse_ref[...])))
    value = base_ref[...] + sign * made
    new_ref[...] = value
    halves[...] = split(value)

    @pl.when(s == 0)
    def _():
        total[...] = jnp.zeros_like(total)

    def rows(at, _):
        total[at, :] += dot(hot_rows(column_ref[at, :], s * core, core), halves[...])

    chunks(total.shape[0], rows)

    @pl.when(s == pl.num_programs(0) - 1)
    def _():
        sent_ref[...] = both(total[...])


def relay_body(sign, sent_ref, in_ref, column_ref, row_ref, out_ref):
    def rows(at, _):
        added = dot(hot_pairs(column_ref[at, :], row_ref[...]), in_ref[...])
        out_ref[at, :] = (sent_ref[at, :] + sign * added).astype(bf16)

    chunks(out_ref.shape[0], rows)


def shards(loads, start, stiffness, local_inverse, modes, coarse_inverse, margin_rows):
    owners = lax.axis_size("wide")
    subs, margins = margin_rows.shape
    order = stiffness.shape[1]
    core = order - margins
    held, cols = loads.shape
    count = modes.shape[2]
    coarse_rows = subs * count
    capacity = 3 * subs * margins // (2 * owners)
    slots = owners * capacity
    many = subs * margins
    m_at = core // margins

    flat = margin_rows.reshape(-1)
    source = flat // held
    row = flat - source * held
    onehot = (source[:, None] == jnp.arange(owners, dtype=i32)[None, :]).astype(bf16)
    earlier = (jnp.arange(many)[:, None] > jnp.arange(many)[None, :]).astype(bf16)
    rank = jnp.sum(dot(earlier, onehot) * onehot.astype(f32), axis=1).astype(i32)
    place = source * capacity + rank
    hit = place[:, None] == jnp.arange(slots, dtype=i32)[None, :]
    asked = jnp.sum(jnp.where(hit, row[:, None] + 1, 0), axis=0) - 1

    def trade(x):
        blocks = x.reshape((owners, x.shape[0] // owners) + x.shape[1:])
        got = lax.all_to_all(blocks, "wide", split_axis=0, concat_axis=0, tiled=True)
        return got.reshape(x.shape)

    wanted = trade(asked)
    wanted_row = wanted[None, :]
    wanted_column = jnp.broadcast_to(jnp.where(wanted < 0, -2, wanted)[:, None], (slots, LANES))
    place_row = place[None, :]
    place_column = jnp.broadcast_to(place[:, None], (many, LANES))
    modes_turned = jnp.swapaxes(modes, 1, 2)

    rows_spec = pl.BlockSpec((core, cols), lambda s: (s, 0))
    left_spec = pl.BlockSpec((1, order, core), lambda s: (s, 0, 0))
    part_spec = pl.BlockSpec((1, order, cols), lambda s: (s, 0, 0))
    slots_spec = whole((slots, cols))
    held_shape = jax.ShapeDtypeStruct((held, cols), f32)
    part_shape = jax.ShapeDtypeStruct((subs, order, cols), f32)
    slots_low = jax.ShapeDtypeStruct((slots, cols), bf16)
    margin_shape = jax.ShapeDtypeStruct((many, cols), bf16)
    matrix_flops = 2 * subs * order * core * cols
    slot_flops = 2 * held * slots * cols

    low, part = call(
        open_body, (subs,), [rows_spec, left_spec], [rows_spec, part_spec],
        [jax.ShapeDtypeStruct((held, cols), bf16), part_shape], [], matrix_flops, 10e6,
    )(start, stiffness)
    going = call(
        first_body, (1,), [whole((held, cols)), whole((slots, LANES))], slots_spec, slots_low, [], slot_flops, 2e6,
    )(low, wanted_column)

    side = lax.axis_size("narrow")
    here = lax.axis_index("narrow").reshape(1).astype(i32)
    own, going = lax.optimization_barrier((coarse_inverse, going))
    pieces = [own] + [
        lax.ppermute(own, "narrow", [(i, i ^ k) for i in range(side)]) for k in range(1, side)
    ]
    core_modes_spec = pl.BlockSpec((1, count, core), lambda s: (s, 0, 0))
    outer_modes_spec = pl.BlockSpec((subs, count, margins), lambda s: (0, 0, m_at))

    def settle(sign, base, came, matrices, has_modes):
        specs = [rows_spec, slots_spec, whole((1, slots)), left_spec]
        args = [base, came, wanted_row, matrices]
        outs, shapes = [rows_spec, part_spec], [held_shape, part_shape]
        if has_modes:
            specs.append(core_modes_spec)
            args.append(modes_turned)
            outs = [part_spec, pl.BlockSpec((count, cols), lambda s: (s, 0))]
            shapes = [part_shape, jax.ShapeDtypeStruct((coarse_rows, cols), f32)]
        return call(
            functools.partial(settle_body, sign, has_modes), (subs,), specs, outs, shapes,
            [pltpu.VMEM((core, cols), bf16)], slot_flops + matrix_flops, 14e6, (1,),
        )(*args)

    corner_spec = pl.BlockSpec((subs, margins, margins), lambda s: (0, m_at, m_at))
    part_outer_spec = pl.BlockSpec((subs, margins, cols), lambda s: (0, m_at, 0))
    outer_scratch = [pltpu.VMEM((many, cols), bf16)]

    def inner(sign, base, margin, part, matrices, coarse):
        specs = [
            pl.BlockSpec((1, core, cols), lambda s: (s, 0, 0)),
            pl.BlockSpec((1, core, margins), lambda s: (s, 0, m_at)),
            pl.BlockSpec((margins, cols), lambda s: (s, 0)),
            rows_spec,
            whole((slots, LANES)),
        ]
        args = [part, matrices, margin, base, wanted_column]
        if coarse is not None:
            specs += [
                pl.BlockSpec((count, cols), lambda s: (s, 0)),
                core_modes_spec,
            ]
            args += [coarse, modes_turned]
        return call(
            functools.partial(inner_body, sign, coarse is not None), (subs,), specs, [rows_spec, slots_spec],
            [held_shape, jax.ShapeDtypeStruct((slots, cols), f32)],
            [pltpu.VMEM((core, 2 * cols), bf16), pltpu.VMEM((slots, 2 * cols), f32)], 2 * slot_flops, 8e6,
        )(*args)

    def relay(sign, sent, came):
        return call(
            functools.partial(relay_body, sign), (1,),
            [slots_spec, slots_spec, whole((slots, LANES)), whole((1, slots))], slots_spec, slots_low, [],
            slot_flops // 2, 3e6, (1,),
        )(sent, came, wanted_column, wanted_row)

    def stiffness_outer(came, part):
        return call(
            outer_body, (1,),
            [slots_spec, whole((many, LANES)), whole((1, many)), corner_spec, part_outer_spec],
            [whole((many, cols)), slots_spec], [margin_shape, slots_low], outer_scratch, slot_flops, 3e6, (0,),
        )(came, place_column, place_row, stiffness, part)

    field = start
    for step in range(ITERS + 1):
        came = trade(going)
        if step > 0:
            field, part = settle(1.0, base, back, stiffness, False)
        margin, going = stiffness_outer(came, part)
        back = trade(going)
        if step == 0:
            pieces, back = lax.optimization_barrier((pieces, back))
        base, sent = inner(-1.0, loads, margin, part, stiffness, None)
        if step == ITERS:
            break

        going = relay(-1.0, sent, back)
        came = trade(going)
        part, proj = settle(-1.0, base, back, local_inverse, True)
        margin, projection = call(
            project_body, (1,),
            [slots_spec, whole((many, LANES)), outer_modes_spec, whole((coarse_rows, cols))],
            [whole((many, cols)), whole((owners * coarse_rows, cols))],
            [margin_shape, jax.ShapeDtypeStruct((owners * coarse_rows, cols), bf16)], [], slot_flops // 2, 2e6, (0,),
        )(came, place_column, modes_turned, proj)
        everyone = trade(projection)
        coarse, going = call(
            functools.partial(coarse_body, side), (1,),
            [pl.BlockSpec(memory_space=pltpu.SMEM), whole((owners * coarse_rows, cols))]
            + [whole(coarse_inverse.shape)] * side
            + [
                whole((many, cols)),
                whole((1, many)),
                corner_spec,
                part_outer_spec,
                outer_modes_spec,
            ],
            [whole((coarse_rows, cols)), slots_spec],
            [jax.ShapeDtypeStruct((coarse_rows, cols), f32), slots_low], outer_scratch, slot_flops, 3e6, (1,),
        )(here, everyone, *pieces, margin, place_row, local_inverse, part, modes_turned)
        back = trade(going)
        base, sent = inner(1.0, field, margin, part, local_inverse, coarse)
        going = relay(1.0, sent, back)

    final = call(
        functools.partial(finish_body, -1.0), (subs,), [rows_spec, slots_spec, whole((1, slots))], rows_spec,
        held_shape, [], slot_flops, 4e6, (1,),
    )(base, back, wanted_row)
    return field, final


def solution(mesh):
    placed = (
        P("wide", "narrow"),
        P("wide", "narrow"),
        P("wide", None, None),
        P("wide", None, None),
        P("wide", None, None),
        P("wide", "narrow"),
        P("wide", None),
    )
    return jax.shard_map(
        shards,
        mesh=mesh,
        in_specs=placed,
        out_specs=(P("wide", "narrow"), P("wide", "narrow")),
        check_vma=False,
    )
```

```python
import functools

import jax
import jax.numpy as jnp
from jax import lax
from jax.experimental import pallas as pl
from jax.experimental.pallas import tpu as pltpu
from jax.sharding import PartitionSpec as P

ITERS = 2
damping = 0.5
LANES = 128
CHUNK = 256
VMEM_LIMIT = 32 * 1024 * 1024
f32, bf16, i32 = jnp.float32, jnp.bfloat16, jnp.int32


def dot(a, b):
    return jnp.dot(a, b, preferred_element_type=f32)


def hot_rows(column, first, width):
    offset = column - lax.broadcasted_iota(i32, column.shape, 1)
    tiles = [(offset == first + t).astype(f32).astype(bf16) for t in range(0, width, LANES)]
    return jnp.concatenate(tiles, axis=1)


def hot_cols(row, first, height):
    numbers = lax.broadcasted_iota(i32, (height, row.shape[1]), 0) + first
    return (numbers == row).astype(f32).astype(bf16)


def hot_pairs(column, row):
    tiles = [
        (column == row[:, t : t + LANES]).astype(f32).astype(bf16) for t in range(0, row.shape[1], LANES)
    ]
    return jnp.concatenate(tiles, axis=1)


def chunks(count, body, size=CHUNK):
    for first in range(0, count, size):
        body(pl.ds(first, size), first)


def turned_dot(a, b):
    return lax.dot_general(a, b, (((0,), (0,)), ((), ())), preferred_element_type=f32)


def call(body, grid, in_specs, out_specs, out_shape, scratch, flops, moved, near=(), near_out=()):
    listed = isinstance(out_shape, (list, tuple))
    shapes = [
        (pltpu.VMEM if i in near_out else pltpu.HBM)(x.shape, x.dtype)
        for i, x in enumerate(out_shape if listed else [out_shape])
    ]
    shapes = shapes if listed else shapes[0]
    run = pl.pallas_call(
        body,
        grid=grid,
        in_specs=in_specs,
        out_specs=out_specs,
        out_shape=shapes,
        scratch_shapes=scratch,
        compiler_params=pltpu.CompilerParams(vmem_limit_bytes=VMEM_LIMIT),
        cost_estimate=pl.CostEstimate(flops=int(flops), bytes_accessed=int(moved), transcendentals=0),
    )

    def placed(i, x, spec):
        if spec.memory_space == pltpu.SMEM:
            return x
        return pltpu.with_memory_space_constraint(x, pltpu.VMEM if i in near else pltpu.HBM)

    return lambda *args: run(*(placed(i, x, spec) for i, (x, spec) in enumerate(zip(args, in_specs))))


def whole(shape):
    return pl.BlockSpec(shape, lambda s: (0,) * len(shape))


def open_body(field_ref, matrix_ref, part_ref):
    part_ref[0] = dot(matrix_ref[0], field_ref[...].astype(bf16))


def first_body(row_ref, field_ref, out_ref, column_ref, low):
    same = (
        lax.broadcasted_iota(i32, (LANES, LANES), 0) == lax.broadcasted_iota(i32, (LANES, LANES), 1)
    ).astype(f32)
    ones = jnp.ones((LANES, LANES), bf16)
    for t in range(0, row_ref.shape[1], LANES):
        number = row_ref[:, t : t + LANES]
        number = jnp.where(number < 0, -2, number) + 2
        high = number // LANES
        column = dot((same * high.astype(f32)).astype(bf16), ones) * LANES
        column += dot((same * (number - high * LANES).astype(f32)).astype(bf16), ones)
        column_ref[pl.ds(t, LANES), :] = column.astype(i32) - 2
    low[...] = field_ref[...].astype(bf16)

    def rows(at, _):
        out_ref[at, :] = dot(hot_rows(column_ref[at, :], 0, low.shape[0]), low[...]).astype(bf16)

    chunks(out_ref.shape[0], rows)


def settle_body(sign, has_modes, base_ref, in_ref, row_ref, matrix_ref, *rest):
    if has_modes:
        modes_ref, part_ref, proj_ref, low = rest
    else:
        field_ref, part_ref, low = rest
    core = base_ref.shape[0]
    first = pl.program_id(0) * core

    def fields(at, c):
        added = dot(hot_cols(row_ref[...], first + c, CHUNK), in_ref[...])
        value = base_ref[at, :] + sign * added
        if not has_modes:
            field_ref[at, :] = value
        low[at, :] = value.astype(bf16)

    chunks(core, fields)
    if has_modes:
        proj_ref[...] = dot(modes_ref[0], low[...])
    part_ref[0] = dot(matrix_ref[0], low[...])


def finish_body(sign, base_ref, in_ref, row_ref, field_ref):
    core = field_ref.shape[0]
    first = pl.program_id(0) * core

    def fields(at, c):
        added = dot(hot_cols(row_ref[...], first + c, CHUNK), in_ref[...])
        field_ref[at, :] = base_ref[at, :] + sign * added

    chunks(core, fields)


def take_margin(in_ref, column_ref, margin_ref, s, margins):
    at = pl.ds(s * margins, margins)
    taken = dot(hot_rows(column_ref[at, :], 0, in_ref.shape[0]), in_ref[...]).astype(bf16)
    margin_ref[at, :] = taken
    return taken


def pack(place_ref, outer, out_ref):
    def rows(at, c):
        out_ref[at, :] = dot(hot_cols(place_ref[...], c, CHUNK), outer[...]).astype(bf16)

    chunks(out_ref.shape[0], rows)


def outer_body(in_ref, column_ref, place_ref, matrix_ref, part_ref, margin_ref, out_ref, outer):
    subs, margins, _ = matrix_ref.shape
    for s in range(subs):
        taken = take_margin(in_ref, column_ref, margin_ref, s, margins)
        outer[pl.ds(s * margins, margins), :] = (part_ref[s] + dot(matrix_ref[s], taken)).astype(bf16)
    pack(place_ref, outer, out_ref)


def project_body(in_ref, column_ref, modes_ref, proj_ref, margin_ref, out_ref):
    subs, count, margins = modes_ref.shape
    for s in range(subs):
        taken = take_margin(in_ref, column_ref, margin_ref, s, margins)
        made = (proj_ref[pl.ds(s * count, count), :] + dot(modes_ref[s], taken)).astype(bf16)
        for first in range(0, out_ref.shape[0], subs * count):
            out_ref[pl.ds(first + s * count, count), :] = made


def split(x):
    high = x.astype(bf16)
    return jnp.concatenate([high, (x - high.astype(f32)).astype(bf16)], axis=1)


def both(x):
    half = x.shape[1] // 2
    return x[:, :half] + x[:, half:]


def coarse_body(side, here_ref, all_ref, *rest):
    inverse_refs = rest[:side]
    margin_ref, place_ref, matrix_ref, part_ref, modes_ref, coarse_ref, out_ref, outer = rest[side:]
    subs, count, margins = modes_ref.shape
    made = 0.0
    for k, inverse_ref in enumerate(inverse_refs):
        width = inverse_ref.shape[1]
        first = pl.multiple_of((here_ref[0] ^ k) * width, width)
        piece = inverse_ref[...]
        high = piece.astype(bf16)
        held = all_ref[pl.ds(first, width), :]
        made += dot(high, held) + dot((piece - high.astype(f32)).astype(bf16), held)
    coarse_ref[...] = made
    halves = split(made)
    for s in range(subs):
        at = pl.ds(s * margins, margins)
        solved = part_ref[s] + dot(matrix_ref[s], margin_ref[at, :])
        lifted = both(turned_dot(modes_ref[s], halves[s * count : (s + 1) * count]))
        outer[at, :] = (damping * solved + lifted).astype(bf16)
    pack(place_ref, outer, out_ref)


def inner_body(sign, has_modes, part_ref, matrix_ref, margin_ref, base_ref, column_ref, *rest):
    if has_modes:
        coarse_ref, modes_ref, new_ref, sent_ref, halves, total = rest
    else:
        new_ref, sent_ref, halves, total = rest
    s = pl.program_id(0)
    core = new_ref.shape[0]
    made = part_ref[0] + dot(matrix_ref[0], margin_ref[...])
    if has_modes:
        made = damping * made + both(turned_dot(modes_ref[0], split(coarse_ref[...])))
    value = base_ref[...] + sign * made
    new_ref[...] = value
    halves[...] = split(value)

    @pl.when(s == 0)
    def _():
        total[...] = jnp.zeros_like(total)

    def rows(at, _):
        total[at, :] += dot(hot_rows(column_ref[at, :], s * core, core), halves[...])

    chunks(total.shape[0], rows)

    @pl.when(s == pl.num_programs(0) - 1)
    def _():
        sent_ref[...] = both(total[...])


def relay_body(sign, sent_ref, in_ref, column_ref, row_ref, out_ref):
    def rows(at, _):
        added = dot(hot_pairs(column_ref[at, :], row_ref[...]), in_ref[...])
        out_ref[at, :] = (sent_ref[at, :] + sign * added).astype(bf16)

    chunks(out_ref.shape[0], rows)


def shards(loads, start, stiffness, local_inverse, modes, coarse_inverse, margin_rows):
    owners = lax.axis_size("wide")
    subs, margins = margin_rows.shape
    order = stiffness.shape[1]
    core = order - margins
    held, cols = loads.shape
    count = modes.shape[2]
    coarse_rows = subs * count
    capacity = 3 * subs * margins // (2 * owners)
    slots = owners * capacity
    many = subs * margins
    m_at = core // margins

    flat = margin_rows.reshape(-1)
    source = flat // held
    row = flat - source * held
    onehot = (source[:, None] == jnp.arange(owners, dtype=i32)[None, :]).astype(bf16)
    earlier = (jnp.arange(many)[:, None] > jnp.arange(many)[None, :]).astype(bf16)
    rank = jnp.sum(dot(earlier, onehot) * onehot.astype(f32), axis=1).astype(i32)
    place = source * capacity + rank
    hit = place[:, None] == jnp.arange(slots, dtype=i32)[None, :]
    asked = jnp.sum(jnp.where(hit, row[:, None] + 1, 0), axis=0) - 1

    def trade(x):
        blocks = x.reshape((owners, x.shape[0] // owners) + x.shape[1:])
        got = lax.all_to_all(blocks, "wide", split_axis=0, concat_axis=0, tiled=True)
        return got.reshape(x.shape)

    wanted = trade(asked)
    wanted_row = wanted[None, :]
    place_row = place[None, :]
    place_column = jnp.broadcast_to(place[:, None], (many, LANES))
    modes_turned = jnp.swapaxes(modes, 1, 2)

    rows_spec = pl.BlockSpec((core, cols), lambda s: (s, 0))
    left_spec = pl.BlockSpec((1, order, core), lambda s: (s, 0, 0))
    part_spec = pl.BlockSpec((1, order, cols), lambda s: (s, 0, 0))
    slots_spec = whole((slots, cols))
    held_shape = jax.ShapeDtypeStruct((held, cols), f32)
    part_shape = jax.ShapeDtypeStruct((subs, order, cols), f32)
    slots_low = jax.ShapeDtypeStruct((slots, cols), bf16)
    margin_shape = jax.ShapeDtypeStruct((many, cols), bf16)
    matrix_flops = 2 * subs * order * core * cols
    slot_flops = 2 * held * slots * cols

    going, wanted_column = call(
        first_body, (1,), [whole((1, slots)), whole((held, cols))], [slots_spec, whole((slots, LANES))],
        [slots_low, jax.ShapeDtypeStruct((slots, LANES), i32)], [pltpu.VMEM((held, cols), bf16)],
        slot_flops, 2e6, (0,), (1,),
    )(wanted_row, start)
    begun, own, going = lax.optimization_barrier((start, coarse_inverse, going))
    part = call(
        open_body, (subs,), [rows_spec, left_spec], part_spec, part_shape, [], matrix_flops, 10e6, (), (0,),
    )(begun, stiffness)

    side = lax.axis_size("narrow")
    here = lax.axis_index("narrow").reshape(1).astype(i32)
    pieces = [own] + [
        lax.ppermute(own, "narrow", [(i, i ^ k) for i in range(side)]) for k in range(1, side)
    ]
    core_modes_spec = pl.BlockSpec((1, count, core), lambda s: (s, 0, 0))
    outer_modes_spec = pl.BlockSpec((subs, count, margins), lambda s: (0, 0, m_at))

    def settle(sign, base, came, matrices, has_modes):
        specs = [rows_spec, slots_spec, whole((1, slots)), left_spec]
        args = [base, came, wanted_row, matrices]
        outs, shapes = [rows_spec, part_spec], [held_shape, part_shape]
        if has_modes:
            specs.append(core_modes_spec)
            args.append(modes_turned)
            outs = [part_spec, pl.BlockSpec((count, cols), lambda s: (s, 0))]
            shapes = [part_shape, jax.ShapeDtypeStruct((coarse_rows, cols), f32)]
        return call(
            functools.partial(settle_body, sign, has_modes), (subs,), specs, outs, shapes,
            [pltpu.VMEM((core, cols), bf16)], slot_flops + matrix_flops, 14e6, (0, 1, 2),
            (0, 1) if has_modes else (1,),
        )(*args)

    corner_spec = whole((subs, margins, margins))
    stiffness_corner = stiffness[:, core:, core:]
    inverse_corner = local_inverse[:, core:, core:]
    part_outer_spec = pl.BlockSpec((subs, margins, cols), lambda s: (0, m_at, 0))
    outer_scratch = [pltpu.VMEM((many, cols), bf16)]

    def inner(sign, base, margin, part, matrices, coarse):
        specs = [
            pl.BlockSpec((1, core, cols), lambda s: (s, 0, 0)),
            pl.BlockSpec((1, core, margins), lambda s: (s, 0, m_at)),
            pl.BlockSpec((margins, cols), lambda s: (s, 0)),
            rows_spec,
            whole((slots, LANES)),
        ]
        args = [part, matrices, margin, base, wanted_column]
        if coarse is not None:
            specs += [
                pl.BlockSpec((count, cols), lambda s: (s, 0)),
                core_modes_spec,
            ]
            args += [coarse, modes_turned]
        return call(
            functools.partial(inner_body, sign, coarse is not None), (subs,), specs, [rows_spec, slots_spec],
            [held_shape, jax.ShapeDtypeStruct((slots, cols), f32)],
            [pltpu.VMEM((core, 2 * cols), bf16), pltpu.VMEM((slots, 2 * cols), f32)], 2 * slot_flops, 8e6,
            (0, 2, 4, 5), (0, 1),
        )(*args)

    def relay(sign, sent, came):
        return call(
            functools.partial(relay_body, sign), (1,),
            [slots_spec, slots_spec, whole((slots, LANES)), whole((1, slots))], slots_spec, slots_low, [],
            slot_flops // 2, 3e6, (0, 1, 2, 3),
        )(sent, came, wanted_column, wanted_row)

    def stiffness_outer(came, part):
        return call(
            outer_body, (1,),
            [slots_spec, whole((many, LANES)), whole((1, many)), corner_spec, part_outer_spec],
            [whole((many, cols)), slots_spec], [margin_shape, slots_low], outer_scratch, slot_flops, 3e6,
            (0, 1, 2, 3, 4), (0,),
        )(came, place_column, place_row, stiffness_corner, part)

    field = start
    for step in range(ITERS + 1):
        came = trade(going)
        if step > 0:
            field, part = settle(1.0, base, back, stiffness, False)
        margin, going = stiffness_outer(came, part)
        back = trade(going)
        if step == 0:
            pieces, back = lax.optimization_barrier((pieces, back))
        base, sent = inner(-1.0, loads, margin, part, stiffness, None)
        if step == ITERS:
            break

        going = relay(-1.0, sent, back)
        came = trade(going)
        part, proj = settle(-1.0, base, back, local_inverse, True)
        margin, projection = call(
            project_body, (1,),
            [slots_spec, whole((many, LANES)), outer_modes_spec, whole((coarse_rows, cols))],
            [whole((many, cols)), whole((owners * coarse_rows, cols))],
            [margin_shape, jax.ShapeDtypeStruct((owners * coarse_rows, cols), bf16)], [], slot_flops // 2, 2e6,
            (0, 1, 3), (0,),
        )(came, place_column, modes_turned, proj)
        everyone = trade(projection)
        coarse, going = call(
            functools.partial(coarse_body, side), (1,),
            [pl.BlockSpec(memory_space=pltpu.SMEM), whole((owners * coarse_rows, cols))]
            + [whole(coarse_inverse.shape)] * side
            + [
                whole((many, cols)),
                whole((1, many)),
                corner_spec,
                part_outer_spec,
                outer_modes_spec,
            ],
            [whole((coarse_rows, cols)), slots_spec],
            [jax.ShapeDtypeStruct((coarse_rows, cols), f32), slots_low], outer_scratch, slot_flops, 3e6,
            (1, side + 2, side + 3, side + 4, side + 5), (0,),
        )(here, everyone, *pieces, margin, place_row, inverse_corner, part, modes_turned)
        back = trade(going)
        base, sent = inner(1.0, field, margin, part, local_inverse, coarse)
        going = relay(1.0, sent, back)

    final = call(
        functools.partial(finish_body, -1.0), (subs,), [rows_spec, slots_spec, whole((1, slots))], rows_spec,
        held_shape, [], slot_flops, 4e6, (0, 1, 2),
    )(base, back, wanted_row)
    return field, final


def solution(mesh):
    placed = (
        P("wide", "narrow"),
        P("wide", "narrow"),
        P("wide", None, None),
        P("wide", None, None),
        P("wide", None, None),
        P("wide", "narrow"),
        P("wide", None),
    )
    return jax.shard_map(
        shards,
        mesh=mesh,
        in_specs=placed,
        out_specs=(P("wide", "narrow"), P("wide", "narrow")),
        check_vma=False,
    )
```

```python
import functools

import jax
import jax.numpy as jnp
from jax import lax
from jax.experimental import pallas as pl
from jax.experimental.pallas import tpu as pltpu
from jax.sharding import PartitionSpec as P

ITERS = 2
damping = 0.5
LANES = 128
CHUNK = 256
VMEM_LIMIT = 32 * 1024 * 1024
f32, bf16, i32 = jnp.float32, jnp.bfloat16, jnp.int32


def dot(a, b):
    return jnp.dot(a, b, preferred_element_type=f32)


def hot_rows(column, first, width):
    offset = column - lax.broadcasted_iota(i32, column.shape, 1)
    tiles = [(offset == first + t).astype(f32).astype(bf16) for t in range(0, width, LANES)]
    return jnp.concatenate(tiles, axis=1)


def hot_cols(row, first, height):
    numbers = lax.broadcasted_iota(i32, (height, row.shape[1]), 0) + first
    return (numbers == row).astype(f32).astype(bf16)


def hot_pairs(column, row):
    tiles = [
        (column == row[:, t : t + LANES]).astype(f32).astype(bf16) for t in range(0, row.shape[1], LANES)
    ]
    return jnp.concatenate(tiles, axis=1)


def chunks(count, body, size=CHUNK):
    for first in range(0, count, size):
        body(pl.ds(first, size), first)


def turned_dot(a, b):
    return lax.dot_general(a, b, (((0,), (0,)), ((), ())), preferred_element_type=f32)


def call(body, grid, in_specs, out_specs, out_shape, scratch, flops, moved, near=(), near_out=()):
    listed = isinstance(out_shape, (list, tuple))
    shapes = [
        (pltpu.VMEM if i in near_out else pltpu.HBM)(x.shape, x.dtype)
        for i, x in enumerate(out_shape if listed else [out_shape])
    ]
    shapes = shapes if listed else shapes[0]
    run = pl.pallas_call(
        body,
        grid=grid,
        in_specs=in_specs,
        out_specs=out_specs,
        out_shape=shapes,
        scratch_shapes=scratch,
        compiler_params=pltpu.CompilerParams(vmem_limit_bytes=VMEM_LIMIT),
        cost_estimate=pl.CostEstimate(flops=int(flops), bytes_accessed=int(moved), transcendentals=0),
    )

    def placed(i, x, spec):
        if spec.memory_space == pltpu.SMEM:
            return x
        return pltpu.with_memory_space_constraint(x, pltpu.VMEM if i in near else pltpu.HBM)

    return lambda *args: run(*(placed(i, x, spec) for i, (x, spec) in enumerate(zip(args, in_specs))))


def whole(shape):
    return pl.BlockSpec(shape, lambda s: (0,) * len(shape))


def open_body(field_ref, matrix_ref, part_ref):
    part_ref[0] = dot(matrix_ref[0], field_ref[...].astype(bf16))


def first_body(row_ref, field_ref, out_ref, column_ref, low):
    same = (
        lax.broadcasted_iota(i32, (LANES, LANES), 0) == lax.broadcasted_iota(i32, (LANES, LANES), 1)
    ).astype(f32)
    ones = jnp.ones((LANES, LANES), bf16)
    for t in range(0, row_ref.shape[1], LANES):
        number = row_ref[:, t : t + LANES]
        number = jnp.where(number < 0, -2, number) + 2
        high = number // LANES
        column = dot((same * high.astype(f32)).astype(bf16), ones) * LANES
        column += dot((same * (number - high * LANES).astype(f32)).astype(bf16), ones)
        column_ref[pl.ds(t, LANES), :] = column.astype(i32) - 2
    low[...] = field_ref[...].astype(bf16)

    def rows(at, _):
        out_ref[at, :] = dot(hot_rows(column_ref[at, :], 0, low.shape[0]), low[...]).astype(bf16)

    chunks(out_ref.shape[0], rows)


def settle_body(sign, has_modes, base_ref, in_ref, row_ref, matrix_ref, *rest):
    if has_modes:
        modes_ref, part_ref, proj_ref, low = rest
    else:
        field_ref, part_ref, low = rest
    core = base_ref.shape[0]
    first = pl.program_id(0) * core

    def fields(at, c):
        added = dot(hot_cols(row_ref[...], first + c, CHUNK), in_ref[...])
        value = base_ref[at, :] + sign * added
        if not has_modes:
            field_ref[at, :] = value
        low[at, :] = value.astype(bf16)

    chunks(core, fields)
    if has_modes:
        proj_ref[...] = dot(modes_ref[0], low[...])
    part_ref[0] = dot(matrix_ref[0], low[...])


def finish_body(sign, base_ref, in_ref, row_ref, field_ref):
    core = field_ref.shape[0]
    first = pl.program_id(0) * core

    def fields(at, c):
        added = dot(hot_cols(row_ref[...], first + c, CHUNK), in_ref[...])
        field_ref[at, :] = base_ref[at, :] + sign * added

    chunks(core, fields)


def take_margin(in_ref, column_ref, margin_ref, s, margins):
    at = pl.ds(s * margins, margins)
    taken = dot(hot_rows(column_ref[at, :], 0, in_ref.shape[0]), in_ref[...]).astype(bf16)
    margin_ref[at, :] = taken
    return taken


def pack(place_ref, outer, out_ref):
    def rows(at, c):
        out_ref[at, :] = dot(hot_cols(place_ref[...], c, CHUNK), outer[...]).astype(bf16)

    chunks(out_ref.shape[0], rows)


def outer_body(in_ref, column_ref, place_ref, matrix_ref, part_ref, margin_ref, out_ref, outer):
    subs, margins, _ = matrix_ref.shape
    for s in range(subs):
        taken = take_margin(in_ref, column_ref, margin_ref, s, margins)
        outer[pl.ds(s * margins, margins), :] = (part_ref[s] + dot(matrix_ref[s], taken)).astype(bf16)
    pack(place_ref, outer, out_ref)


def project_body(in_ref, column_ref, modes_ref, proj_ref, margin_ref, out_ref):
    subs, count, margins = modes_ref.shape
    for s in range(subs):
        taken = take_margin(in_ref, column_ref, margin_ref, s, margins)
        made = (proj_ref[pl.ds(s * count, count), :] + dot(modes_ref[s], taken)).astype(bf16)
        for first in range(0, out_ref.shape[0], subs * count):
            out_ref[pl.ds(first + s * count, count), :] = made


def split(x):
    high = x.astype(bf16)
    return jnp.concatenate([high, (x - high.astype(f32)).astype(bf16)], axis=1)


def both(x):
    half = x.shape[1] // 2
    return x[:, :half] + x[:, half:]


def coarse_body(side, here_ref, all_ref, *rest):
    inverse_refs = rest[:side]
    margin_ref, place_ref, matrix_ref, part_ref, modes_ref, coarse_ref, out_ref, outer = rest[side:]
    subs, count, margins = modes_ref.shape
    made = 0.0
    for k, inverse_ref in enumerate(inverse_refs):
        width = inverse_ref.shape[1]
        first = pl.multiple_of((here_ref[0] ^ k) * width, width)
        made += dot(inverse_ref[...], all_ref[pl.ds(first, width), :])
    coarse_ref[...] = made
    halves = split(made)
    for s in range(subs):
        at = pl.ds(s * margins, margins)
        solved = part_ref[s] + dot(matrix_ref[s], margin_ref[at, :])
        lifted = both(turned_dot(modes_ref[s], halves[s * count : (s + 1) * count]))
        outer[at, :] = (damping * solved + lifted).astype(bf16)
    pack(place_ref, outer, out_ref)


def inner_body(sign, has_modes, part_ref, matrix_ref, margin_ref, base_ref, column_ref, *rest):
    if has_modes:
        coarse_ref, modes_ref, new_ref, sent_ref, halves, total = rest
    else:
        new_ref, sent_ref, halves, total = rest
    s = pl.program_id(0)
    core = new_ref.shape[0]
    made = part_ref[0] + dot(matrix_ref[0], margin_ref[...])
    if has_modes:
        made = damping * made + both(turned_dot(modes_ref[0], split(coarse_ref[...])))
    value = base_ref[...] + sign * made
    new_ref[...] = value
    halves[...] = split(value)

    @pl.when(s == 0)
    def _():
        total[...] = jnp.zeros_like(total)

    def rows(at, _):
        total[at, :] += dot(hot_rows(column_ref[at, :], s * core, core), halves[...])

    chunks(total.shape[0], rows)

    @pl.when(s == pl.num_programs(0) - 1)
    def _():
        sent_ref[...] = both(total[...])


def relay_body(sign, sent_ref, in_ref, column_ref, row_ref, out_ref):
    def rows(at, _):
        added = dot(hot_pairs(column_ref[at, :], row_ref[...]), in_ref[...])
        out_ref[at, :] = (sent_ref[at, :] + sign * added).astype(bf16)

    chunks(out_ref.shape[0], rows)


def shards(loads, start, stiffness, local_inverse, modes, coarse_inverse, margin_rows):
    owners = lax.axis_size("wide")
    subs, margins = margin_rows.shape
    order = stiffness.shape[1]
    core = order - margins
    held, cols = loads.shape
    count = modes.shape[2]
    coarse_rows = subs * count
    capacity = 3 * subs * margins // (2 * owners)
    slots = owners * capacity
    many = subs * margins
    m_at = core // margins

    flat = margin_rows.reshape(-1)
    source = flat // held
    row = flat - source * held
    onehot = (source[:, None] == jnp.arange(owners, dtype=i32)[None, :]).astype(bf16)
    earlier = (jnp.arange(many)[:, None] > jnp.arange(many)[None, :]).astype(bf16)
    rank = jnp.sum(dot(earlier, onehot) * onehot.astype(f32), axis=1).astype(i32)
    place = source * capacity + rank
    hit = place[:, None] == jnp.arange(slots, dtype=i32)[None, :]
    asked = jnp.sum(jnp.where(hit, row[:, None] + 1, 0), axis=0) - 1

    def trade(x):
        blocks = x.reshape((owners, x.shape[0] // owners) + x.shape[1:])
        got = lax.all_to_all(blocks, "wide", split_axis=0, concat_axis=0, tiled=True)
        return got.reshape(x.shape)

    wanted = trade(asked)
    wanted_row = wanted[None, :]
    place_row = place[None, :]
    place_column = jnp.broadcast_to(place[:, None], (many, LANES))
    modes_turned = jnp.swapaxes(modes, 1, 2)

    rows_spec = pl.BlockSpec((core, cols), lambda s: (s, 0))
    left_spec = pl.BlockSpec((1, order, core), lambda s: (s, 0, 0))
    part_spec = pl.BlockSpec((1, order, cols), lambda s: (s, 0, 0))
    slots_spec = whole((slots, cols))
    held_shape = jax.ShapeDtypeStruct((held, cols), f32)
    part_shape = jax.ShapeDtypeStruct((subs, order, cols), f32)
    slots_low = jax.ShapeDtypeStruct((slots, cols), bf16)
    margin_shape = jax.ShapeDtypeStruct((many, cols), bf16)
    matrix_flops = 2 * subs * order * core * cols
    slot_flops = 2 * held * slots * cols

    going, wanted_column = call(
        first_body, (1,), [whole((1, slots)), whole((held, cols))], [slots_spec, whole((slots, LANES))],
        [slots_low, jax.ShapeDtypeStruct((slots, LANES), i32)], [pltpu.VMEM((held, cols), bf16)],
        slot_flops, 2e6, (0,), (1,),
    )(wanted_row, start)
    begun, own, going = lax.optimization_barrier((start, coarse_inverse.astype(bf16), going))
    part = call(
        open_body, (subs,), [rows_spec, left_spec], part_spec, part_shape, [], matrix_flops, 10e6, (), (0,),
    )(begun, stiffness)

    side = lax.axis_size("narrow")
    here = lax.axis_index("narrow").reshape(1).astype(i32)
    pieces = [own] + [
        lax.ppermute(own, "narrow", [(i, i ^ k) for i in range(side)]) for k in range(1, side)
    ]
    core_modes_spec = pl.BlockSpec((1, count, core), lambda s: (s, 0, 0))
    outer_modes_spec = pl.BlockSpec((subs, count, margins), lambda s: (0, 0, m_at))

    def settle(sign, base, came, matrices, has_modes):
        specs = [rows_spec, slots_spec, whole((1, slots)), left_spec]
        args = [base, came, wanted_row, matrices]
        outs, shapes = [rows_spec, part_spec], [held_shape, part_shape]
        if has_modes:
            specs.append(core_modes_spec)
            args.append(modes_turned)
            outs = [part_spec, pl.BlockSpec((count, cols), lambda s: (s, 0))]
            shapes = [part_shape, jax.ShapeDtypeStruct((coarse_rows, cols), f32)]
        return call(
            functools.partial(settle_body, sign, has_modes), (subs,), specs, outs, shapes,
            [pltpu.VMEM((core, cols), bf16)], slot_flops + matrix_flops, 14e6, (1, 2),
            () if has_modes else (1,),
        )(*args)

    corner_spec = pl.BlockSpec((subs, margins, margins), lambda s: (0, m_at, m_at))
    part_outer_spec = pl.BlockSpec((subs, margins, cols), lambda s: (0, m_at, 0))
    outer_scratch = [pltpu.VMEM((many, cols), bf16)]

    def inner(sign, base, margin, part, matrices, coarse):
        specs = [
            pl.BlockSpec((1, core, cols), lambda s: (s, 0, 0)),
            pl.BlockSpec((1, core, margins), lambda s: (s, 0, m_at)),
            pl.BlockSpec((margins, cols), lambda s: (s, 0)),
            rows_spec,
            whole((slots, LANES)),
        ]
        args = [part, matrices, margin, base, wanted_column]
        if coarse is not None:
            specs += [
                pl.BlockSpec((count, cols), lambda s: (s, 0)),
                core_modes_spec,
            ]
            args += [coarse, modes_turned]
        return call(
            functools.partial(inner_body, sign, coarse is not None), (subs,), specs, [rows_spec, slots_spec],
            [held_shape, jax.ShapeDtypeStruct((slots, cols), f32)],
            [pltpu.VMEM((core, 2 * cols), bf16), pltpu.VMEM((slots, 2 * cols), f32)], 2 * slot_flops, 8e6,
            (4,) if coarse is not None else (0, 4), (1,),
        )(*args)

    def relay(sign, sent, came):
        return call(
            functools.partial(relay_body, sign), (1,),
            [slots_spec, slots_spec, whole((slots, LANES)), whole((1, slots))], slots_spec, slots_low, [],
            slot_flops // 2, 3e6, (0, 1, 2, 3),
        )(sent, came, wanted_column, wanted_row)

    def stiffness_outer(came, part):
        return call(
            outer_body, (1,),
            [slots_spec, whole((many, LANES)), whole((1, many)), corner_spec, part_outer_spec],
            [whole((many, cols)), slots_spec], [margin_shape, slots_low], outer_scratch, slot_flops, 3e6,
            (0, 4),
        )(came, place_column, place_row, stiffness, part)

    field = start
    for step in range(ITERS + 1):
        came = trade(going)
        if step == 0:
            pieces, came = lax.optimization_barrier((pieces, came))
        else:
            field, part = settle(1.0, base, back, stiffness, False)
        margin, going = stiffness_outer(came, part)
        back = trade(going)
        base, sent = inner(-1.0, loads, margin, part, stiffness, None)
        if step == ITERS:
            break

        going = relay(-1.0, sent, back)
        came = trade(going)
        part, proj = settle(-1.0, base, back, local_inverse, True)
        margin, projection = call(
            project_body, (1,),
            [slots_spec, whole((many, LANES)), outer_modes_spec, whole((coarse_rows, cols))],
            [whole((many, cols)), whole((owners * coarse_rows, cols))],
            [margin_shape, jax.ShapeDtypeStruct((owners * coarse_rows, cols), bf16)], [], slot_flops // 2, 2e6,
            (0,),
        )(came, place_column, modes_turned, proj)
        everyone = trade(projection)
        coarse, going = call(
            functools.partial(coarse_body, side), (1,),
            [pl.BlockSpec(memory_space=pltpu.SMEM), whole((owners * coarse_rows, cols))]
            + [whole(coarse_inverse.shape)] * side
            + [
                whole((many, cols)),
                whole((1, many)),
                corner_spec,
                part_outer_spec,
                outer_modes_spec,
            ],
            [whole((coarse_rows, cols)), slots_spec],
            [jax.ShapeDtypeStruct((coarse_rows, cols), f32), slots_low], outer_scratch, slot_flops, 3e6,
            (1,),
        )(here, everyone, *pieces, margin, place_row, local_inverse, part, modes_turned)
        back = trade(going)
        base, sent = inner(1.0, field, margin, part, local_inverse, coarse)
        going = relay(1.0, sent, back)

    final = call(
        functools.partial(finish_body, -1.0), (subs,), [rows_spec, slots_spec, whole((1, slots))], rows_spec,
        held_shape, [], slot_flops, 4e6, (1, 2),
    )(base, back, wanted_row)
    return field, final


def solution(mesh):
    placed = (
        P("wide", "narrow"),
        P("wide", "narrow"),
        P("wide", None, None),
        P("wide", None, None),
        P("wide", None, None),
        P("wide", "narrow"),
        P("wide", None),
    )
    return jax.shard_map(
        shards,
        mesh=mesh,
        in_specs=placed,
        out_specs=(P("wide", "narrow"), P("wide", "narrow")),
        check_vma=False,
    )
```

```python
import functools

import jax
import jax.numpy as jnp
from jax import lax
from jax.experimental import pallas as pl
from jax.experimental.pallas import tpu as pltpu
from jax.sharding import PartitionSpec as P

ITERS = 2
damping = 0.5
LANES = 128
CHUNK = 256
VMEM_LIMIT = 32 * 1024 * 1024
f32, bf16, i32 = jnp.float32, jnp.bfloat16, jnp.int32


def dot(a, b):
    return jnp.dot(a, b, preferred_element_type=f32)


def hot_rows(column, first, width):
    offset = column - lax.broadcasted_iota(i32, column.shape, 1)
    tiles = [(offset == first + t).astype(f32).astype(bf16) for t in range(0, width, LANES)]
    return jnp.concatenate(tiles, axis=1)


def hot_cols(row, first, height):
    numbers = lax.broadcasted_iota(i32, (height, row.shape[1]), 0) + first
    return (numbers == row).astype(f32).astype(bf16)


def hot_pairs(column, row):
    tiles = [
        (column == row[:, t : t + LANES]).astype(f32).astype(bf16) for t in range(0, row.shape[1], LANES)
    ]
    return jnp.concatenate(tiles, axis=1)


def chunks(count, body, size=CHUNK):
    for first in range(0, count, size):
        body(pl.ds(first, size), first)


def turned_dot(a, b):
    return lax.dot_general(a, b, (((0,), (0,)), ((), ())), preferred_element_type=f32)


def call(body, grid, in_specs, out_specs, out_shape, scratch, flops, moved, near=(), near_out=()):
    listed = isinstance(out_shape, (list, tuple))
    shapes = [
        (pltpu.VMEM if i in near_out else pltpu.HBM)(x.shape, x.dtype)
        for i, x in enumerate(out_shape if listed else [out_shape])
    ]
    shapes = shapes if listed else shapes[0]
    run = pl.pallas_call(
        body,
        grid=grid,
        in_specs=in_specs,
        out_specs=out_specs,
        out_shape=shapes,
        scratch_shapes=scratch,
        compiler_params=pltpu.CompilerParams(vmem_limit_bytes=VMEM_LIMIT),
        cost_estimate=pl.CostEstimate(flops=int(flops), bytes_accessed=int(moved), transcendentals=0),
    )

    def placed(i, x, spec):
        if spec.memory_space == pltpu.SMEM:
            return x
        return pltpu.with_memory_space_constraint(x, pltpu.VMEM if i in near else pltpu.HBM)

    return lambda *args: run(*(placed(i, x, spec) for i, (x, spec) in enumerate(zip(args, in_specs))))


def whole(shape):
    return pl.BlockSpec(shape, lambda s: (0,) * len(shape))


def open_body(field_ref, matrix_ref, part_ref):
    part_ref[0] = dot(matrix_ref[0], field_ref[...].astype(bf16))


def first_body(row_ref, field_ref, modes_ref, out_ref, column_ref, own_ref, low):
    same = (
        lax.broadcasted_iota(i32, (LANES, LANES), 0) == lax.broadcasted_iota(i32, (LANES, LANES), 1)
    ).astype(f32)
    ones = jnp.ones((LANES, LANES), bf16)
    for t in range(0, row_ref.shape[1], LANES):
        number = row_ref[:, t : t + LANES]
        number = jnp.where(number < 0, -2, number) + 2
        high = number // LANES
        column = dot((same * high.astype(f32)).astype(bf16), ones) * LANES
        column += dot((same * (number - high * LANES).astype(f32)).astype(bf16), ones)
        column_ref[pl.ds(t, LANES), :] = column.astype(i32) - 2
    cols = field_ref.shape[1]
    low[:, :cols] = field_ref[...].astype(bf16)
    low[:, cols:] = modes_ref[...]

    def rows(at, _):
        both_parts = dot(hot_rows(column_ref[at, :], 0, low.shape[0]), low[...]).astype(bf16)
        out_ref[at, :] = both_parts[:, :cols]
        own_ref[at, :] = both_parts[:, cols:]

    chunks(out_ref.shape[0], rows)


def slots_in(in_ref, capacity, held):
    if in_ref.shape[1] == capacity:
        return in_ref[...].reshape(-1, in_ref.shape[2])
    for k in range(in_ref.shape[0]):
        held[pl.ds(k * capacity, capacity), :] = in_ref[k, :capacity, :]
    return held[...]


def split(x):
    high = x.astype(bf16)
    return jnp.concatenate([high, (x - high.astype(f32)).astype(bf16)], axis=1)


def both(x):
    half = x.shape[1] // 2
    return x[:, :half] + x[:, half:]


def residual_body(capacity, base_ref, in_ref, row_ref, matrix_ref, modes_ref, part_ref, proj_ref, low, held):
    core = base_ref.shape[0]
    s = pl.program_id(0)

    @pl.when(s == 0)
    def _():
        held[...] = slots_in(in_ref, capacity, held)

    def fields(at, c):
        added = dot(hot_cols(row_ref[...], s * core + c, CHUNK), held[...])
        low[at, :] = (base_ref[at, :] - added).astype(bf16)

    chunks(core, fields)
    proj_ref[...] = dot(modes_ref[0], low[...])
    part_ref[0] = dot(matrix_ref[0], low[...])


def update_body(base_ref, in_ref, row_ref, matrix_ref, modes_ref, coarse_ref, field_ref, part_ref, low):
    core = base_ref.shape[0]
    s = pl.program_id(0)
    halves = split(coarse_ref[...])

    def fields(at, c):
        added = dot(hot_cols(row_ref[...], s * core + c, CHUNK), in_ref[...])
        added += turned_dot(modes_ref[0, :, at], halves)
        value = base_ref[at, :] + both(added)
        field_ref[at, :] = value
        low[at, :] = value.astype(bf16)

    chunks(core, fields)
    part_ref[0] = dot(matrix_ref[0], low[...])


def finish_body(base_ref, in_ref, row_ref, field_ref):
    core = field_ref.shape[0]
    first = pl.program_id(0) * core

    def fields(at, c):
        added = dot(hot_cols(row_ref[...], first + c, CHUNK), in_ref[...])
        field_ref[at, :] = base_ref[at, :] - added

    chunks(core, fields)


def take_margin(in_ref, column_ref, margin_ref, s, margins):
    at = pl.ds(s * margins, margins)
    taken = dot(hot_rows(column_ref[at, :], 0, in_ref.shape[0]), in_ref[...]).astype(bf16)
    margin_ref[at, :] = taken
    return taken


def pack(place_ref, outer, packed):
    def rows(at, c):
        packed[at, :] = dot(hot_cols(place_ref[...], c, CHUNK), outer[...]).astype(bf16)

    chunks(packed.shape[0], rows)


def outer_body(in_ref, column_ref, place_ref, matrix_ref, part_ref, *rest):
    subs, margins, _ = matrix_ref.shape
    cols = in_ref.shape[1]
    if len(rest) > 4:
        modes_ref, margin_ref, out_ref, outer, packed = rest
        outer[:, cols:] = modes_ref[...]
    else:
        margin_ref, out_ref, outer, packed = rest
    for s in range(subs):
        taken = take_margin(in_ref, column_ref, margin_ref, s, margins)
        outer[pl.ds(s * margins, margins), :cols] = (part_ref[s] + dot(matrix_ref[s], taken)).astype(bf16)
    pack(place_ref, outer, packed)
    owners = out_ref.shape[0]
    capacity = packed.shape[0] // owners
    for k in range(owners):
        out_ref[k, :capacity, :] = packed[pl.ds(k * capacity, capacity), :cols]
        if len(rest) > 4:
            out_ref[k, capacity:, :] = packed[pl.ds(k * capacity, capacity), cols:]


def solve_body(
    in_ref, column_ref, place_ref, matrix_ref, part_ref, modes_ref, proj_ref, margin_ref, out_ref, outer, packed
):
    subs, count, margins = modes_ref.shape
    owners = out_ref.shape[0]
    capacity = packed.shape[0] // owners
    for s in range(subs):
        taken = take_margin(in_ref, column_ref, margin_ref, s, margins)
        made = (proj_ref[pl.ds(s * count, count), :] + dot(modes_ref[s], taken)).astype(bf16)
        for k in range(owners):
            out_ref[k, pl.ds(capacity + s * count, count), :] = made
        solved = damping * (part_ref[s] + dot(matrix_ref[s], taken))
        outer[pl.ds(s * margins, margins), :] = solved.astype(bf16)
    pack(place_ref, outer, packed)
    for k in range(owners):
        out_ref[k, :capacity, :] = packed[pl.ds(k * capacity, capacity), :]


def inner_body(sign, scale, part_ref, matrix_ref, margin_ref, base_ref, column_ref, new_ref, sent_ref, halves, total):
    s = pl.program_id(0)
    core = new_ref.shape[0]
    value = base_ref[...] + sign * scale * (part_ref[0] + dot(matrix_ref[0], margin_ref[...]))
    new_ref[...] = value
    halves[...] = split(value)

    @pl.when(s == 0)
    def _():
        total[...] = jnp.zeros_like(total)

    def rows(at, _):
        total[at, :] += dot(hot_rows(column_ref[at, :], s * core, core), halves[...])

    chunks(total.shape[0], rows)

    @pl.when(s == pl.num_programs(0) - 1)
    def _():
        sent_ref[...] = both(total[...])


def relay_body(capacity, sent_ref, in_ref, column_ref, row_ref, out_ref, held):
    held[...] = slots_in(in_ref, capacity, held)

    def rows(at, _):
        added = dot(hot_pairs(column_ref[at, :], row_ref[...]), held[...])
        out_ref[at, :] = (sent_ref[at, :] - added).astype(bf16)

    chunks(out_ref.shape[0], rows)


def lift_body(
    capacity, me_ref, sent_ref, in_ref, column_ref, row_ref, inverse_ref, lifts_ref, own_ref,
    out_ref, added_ref, coarse_ref, gathered, made,
):
    step = pl.program_id(0)
    some, side, count, width = inverse_ref.shape
    owners = in_ref.shape[0]

    @pl.when(step == 0)
    def _():
        for k in range(owners):
            gathered[pl.ds(k * count, count), :] = in_ref[k, capacity:, :]

    total = 0.0
    for n in range(side):
        block = inverse_ref[:, n].reshape(some * count, width)
        total += dot(block, gathered[n * width : (n + 1) * width, :])
    made[pl.ds(pl.multiple_of(step * (some * count), some * count), some * count), :] = total
    halves = split(total)
    for k in range(some):
        at = step * some + k
        lifted = both(dot(lifts_ref[at, capacity:, :], halves[k * count : (k + 1) * count]))
        value = in_ref[at, :capacity, :].astype(f32) + lifted
        added_ref[pl.ds(pl.multiple_of(at * capacity, capacity), capacity), :] = split(value)

    @pl.when(step == pl.num_programs(0) - 1)
    def _():
        mine = made[pl.ds(pl.multiple_of(me_ref[0] * count, count), count), :]
        coarse_ref[...] = mine
        mine_halves = split(mine)

        def rows(at, _):
            value = dot(hot_pairs(column_ref[at, :], row_ref[...]), added_ref[...])
            value += dot(own_ref[at, :], mine_halves)
            out_ref[at, :] = (sent_ref[at, :] + both(value)).astype(bf16)

        chunks(out_ref.shape[0], rows)


def shards(loads, start, stiffness, local_inverse, modes, coarse_inverse, margin_rows):
    owners = lax.axis_size("wide")
    subs, margins = margin_rows.shape
    order = stiffness.shape[1]
    core = order - margins
    held, cols = loads.shape
    count = modes.shape[2]
    coarse_rows = subs * count
    capacity = 3 * subs * margins // (2 * owners)
    slots = owners * capacity
    many = subs * margins
    m_at = core // margins

    flat = margin_rows.reshape(-1)
    source = flat // held
    row = flat - source * held
    onehot = (source[:, None] == jnp.arange(owners, dtype=i32)[None, :]).astype(bf16)
    earlier = (jnp.arange(many)[:, None] > jnp.arange(many)[None, :]).astype(bf16)
    rank = jnp.sum(dot(earlier, onehot) * onehot.astype(f32), axis=1).astype(i32)
    place = source * capacity + rank
    hit = place[:, None] == jnp.arange(slots, dtype=i32)[None, :]
    asked = jnp.sum(jnp.where(hit, row[:, None] + 1, 0), axis=0) - 1

    def trade(blocks):
        return lax.all_to_all(blocks, "wide", split_axis=0, concat_axis=0, tiled=True)

    wanted = trade(asked.reshape(owners, capacity)).reshape(slots)
    wanted_row = wanted[None, :]
    place_row = place[None, :]
    place_column = jnp.broadcast_to(place[:, None], (many, LANES))
    modes_turned = jnp.swapaxes(modes, 1, 2)

    def spread(block):
        shown = [
            jnp.pad(block[s], ((0, 0), (s * count, coarse_rows - (s + 1) * count))) for s in range(subs)
        ]
        return jnp.concatenate(shown, axis=0)

    core_modes = spread(modes[:, :core])
    outer_modes = spread(modes[:, core:])

    side = lax.axis_size("narrow")
    me = lax.axis_index("wide").reshape(1).astype(i32)
    width = coarse_inverse.shape[1]
    if owners <= 8:
        inverse = lax.all_gather(coarse_inverse.astype(bf16), ("wide", "narrow"), axis=0)
        inverse = inverse.reshape(owners, side, coarse_rows, width)
    else:
        inverse = lax.all_gather(coarse_inverse.astype(bf16), "narrow", axis=0)
        inverse = lax.all_gather(inverse, "wide", axis=0)

    rows_spec = pl.BlockSpec((core, cols), lambda s: (s, 0))
    left_spec = pl.BlockSpec((1, order, core), lambda s: (s, 0, 0))
    part_spec = pl.BlockSpec((1, order, cols), lambda s: (s, 0, 0))
    slots_spec = whole((slots, cols))
    column_spec = whole((slots, LANES))
    row_spec = whole((1, slots))
    held_shape = jax.ShapeDtypeStruct((held, cols), f32)
    part_shape = jax.ShapeDtypeStruct((subs, order, cols), f32)
    slots_low = jax.ShapeDtypeStruct((slots, cols), bf16)
    margin_shape = jax.ShapeDtypeStruct((many, cols), bf16)
    coarse_shape = jax.ShapeDtypeStruct((coarse_rows, cols), f32)
    matrix_flops = 2 * subs * order * core * cols
    slot_flops = 2 * held * slots * cols
    low_scratch = pltpu.VMEM((core, cols), bf16)
    held_scratch = pltpu.VMEM((slots, cols), bf16)

    going, wanted_column, own_lifts = call(
        first_body, (1,), [row_spec, whole((held, cols)), whole((held, coarse_rows))],
        [slots_spec, column_spec, whole((slots, coarse_rows))],
        [slots_low, jax.ShapeDtypeStruct((slots, LANES), i32), jax.ShapeDtypeStruct((slots, coarse_rows), bf16)],
        [pltpu.VMEM((held, cols + coarse_rows), bf16)], slot_flops, 2e6, (0,), (1,),
    )(wanted_row, start, core_modes)
    begun, going = lax.optimization_barrier((start, going))
    part = call(
        open_body, (subs,), [rows_spec, left_spec], part_spec, part_shape, [], matrix_flops, 10e6, (), (0,),
    )(begun, stiffness)

    core_modes_spec = pl.BlockSpec((1, count, core), lambda s: (s, 0, 0))
    outer_modes_spec = pl.BlockSpec((subs, count, margins), lambda s: (0, 0, m_at))
    coarse_spec = pl.BlockSpec((count, cols), lambda s: (s, 0))
    corner_spec = pl.BlockSpec((subs, margins, margins), lambda s: (0, m_at, m_at))
    part_outer_spec = pl.BlockSpec((subs, margins, cols), lambda s: (0, m_at, 0))

    def inner(sign, scale, base, margin, part, matrices):
        return call(
            functools.partial(inner_body, sign, scale), (subs,),
            [
                pl.BlockSpec((1, core, cols), lambda s: (s, 0, 0)),
                pl.BlockSpec((1, core, margins), lambda s: (s, 0, m_at)),
                pl.BlockSpec((margins, cols), lambda s: (s, 0)),
                rows_spec,
                column_spec,
            ],
            [rows_spec, slots_spec], [held_shape, jax.ShapeDtypeStruct((slots, cols), f32)],
            [pltpu.VMEM((core, 2 * cols), bf16), pltpu.VMEM((slots, 2 * cols), f32)], 2 * slot_flops, 8e6,
            (0, 4) if matrices is stiffness else (4,), () if matrices is stiffness else (1,),
        )(part, matrices, margin, base, wanted_column)

    def outer(came, part, extra):
        rows = capacity * (1 if extra is None else 2)
        wide = cols if extra is None else cols + coarse_rows
        specs = [slots_spec, whole((many, LANES)), whole((1, many)), corner_spec, part_outer_spec]
        args = [came.reshape(slots, cols), place_column, place_row, stiffness, part]
        if extra is not None:
            specs.append(whole((many, coarse_rows)))
            args.append(extra)
        return call(
            outer_body, (1,), specs, [whole((many, cols)), whole((owners, rows, cols))],
            [margin_shape, jax.ShapeDtypeStruct((owners, rows, cols), bf16)],
            [pltpu.VMEM((many, wide), bf16), pltpu.VMEM((slots, wide), bf16)], slot_flops, 3e6, (0, 4),
        )(*args)

    field, lifts = start, None
    for step in range(ITERS + 1):
        came = trade(going.reshape(owners, capacity, cols))
        if step > 0:
            field, part = call(
                update_body, (subs,),
                [rows_spec, whole((slots, 2 * cols)), row_spec, left_spec, core_modes_spec, coarse_spec],
                [rows_spec, part_spec], [held_shape, part_shape], [low_scratch],
                slot_flops + matrix_flops, 14e6, (2,), (1,),
            )(base, added, wanted_row, stiffness, modes_turned, coarse)
        margin, going = outer(came, part, outer_modes if step == 0 else None)
        back = trade(going)
        if step == 0:
            lifts = back
        base, sent = inner(-1.0, 1.0, loads, margin, part, stiffness)
        if step == ITERS:
            break

        back_spec = whole(back.shape)
        going = call(
            functools.partial(relay_body, capacity), (1,), [slots_spec, back_spec, column_spec, row_spec],
            slots_spec, slots_low, [held_scratch], slot_flops // 2, 3e6, (1, 2, 3),
        )(sent, back, wanted_column, wanted_row)
        came = trade(going.reshape(owners, capacity, cols))
        part, proj = call(
            functools.partial(residual_body, capacity), (subs,),
            [rows_spec, back_spec, row_spec, left_spec, core_modes_spec], [part_spec, coarse_spec],
            [part_shape, coarse_shape], [low_scratch, held_scratch], slot_flops + matrix_flops, 14e6, (1, 2), (0,),
        )(base, back, wanted_row, local_inverse, modes_turned)
        sent_rows = capacity + coarse_rows
        margin, going = call(
            solve_body, (1,),
            [
                slots_spec, whole((many, LANES)), whole((1, many)), corner_spec, part_outer_spec,
                outer_modes_spec, whole((coarse_rows, cols)),
            ],
            [whole((many, cols)), whole((owners, sent_rows, cols))],
            [margin_shape, jax.ShapeDtypeStruct((owners, sent_rows, cols), bf16)],
            [pltpu.VMEM((many, cols), bf16), pltpu.VMEM((slots, cols), bf16)], slot_flops, 3e6, (0, 4),
        )(came.reshape(slots, cols), place_column, place_row, local_inverse, part, modes_turned, proj)
        back = trade(going)
        base, sent = inner(1.0, damping, field, margin, part, local_inverse)
        some = min(owners, 8)
        going, added, coarse = call(
            functools.partial(lift_body, capacity), (owners // some,),
            [
                pl.BlockSpec(memory_space=pltpu.SMEM), slots_spec, whole(back.shape), column_spec, row_spec,
                pl.BlockSpec((some, side, coarse_rows, width), lambda j: (j, 0, 0, 0)),
                whole(lifts.shape), whole((slots, coarse_rows)),
            ],
            [slots_spec, whole((slots, 2 * cols)), whole((coarse_rows, cols))],
            [slots_low, jax.ShapeDtypeStruct((slots, 2 * cols), bf16), coarse_shape],
            [pltpu.VMEM((owners * coarse_rows, cols), bf16), pltpu.VMEM((owners * coarse_rows, cols), f32)],
            slot_flops, 6e6, (1, 2, 3, 4),
        )(me, sent, back, wanted_column, wanted_row, inverse, lifts, own_lifts)

    final = call(
        finish_body, (subs,), [rows_spec, slots_spec, row_spec], rows_spec, held_shape, [], slot_flops, 4e6, (1, 2),
    )(base, back.reshape(slots, cols), wanted_row)
    return field, final


def solution(mesh):
    placed = (
        P("wide", "narrow"),
        P("wide", "narrow"),
        P("wide", None, None),
        P("wide", None, None),
        P("wide", None, None),
        P("wide", "narrow"),
        P("wide", None),
    )
    return jax.shard_map(
        shards,
        mesh=mesh,
        in_specs=placed,
        out_specs=(P("wide", "narrow"), P("wide", "narrow")),
        check_vma=False,
    )
```

```python
import functools

import jax
import jax.numpy as jnp
from jax import lax
from jax.experimental import pallas as pl
from jax.experimental.pallas import tpu as pltpu
from jax.sharding import PartitionSpec as P

ITERS = 2
damping = 0.5
LANES = 128
VMEM_LIMIT = 32 * 1024 * 1024
f32, bf16, i32 = jnp.float32, jnp.bfloat16, jnp.int32


def dot(a, b):
    return jnp.dot(a, b, preferred_element_type=f32)


def hot_rows(column, first, width):
    offset = column - lax.broadcasted_iota(i32, column.shape, 1)
    tiles = [(offset == first + t).astype(f32).astype(bf16) for t in range(0, width, LANES)]
    return jnp.concatenate(tiles, axis=1)


def hot_cols(row, first, height):
    numbers = lax.broadcasted_iota(i32, (height, row.shape[1]), 0) + first
    return (numbers == row).astype(f32).astype(bf16)


def hot_pairs(column, row):
    tiles = [
        (column == row[:, t : t + LANES]).astype(f32).astype(bf16) for t in range(0, row.shape[1], LANES)
    ]
    return jnp.concatenate(tiles, axis=1)


def chunks(count, body, parts):
    size = count // parts
    for first in range(0, count, size):
        body(pl.ds(first, size), first)


def product(matrix_ref, vectors, out_ref):
    def rows(at, _):
        out_ref[0, at, :] = dot(matrix_ref[0, at, :], vectors)

    chunks(out_ref.shape[1], rows, 2)


def turned_dot(a, b):
    return lax.dot_general(a, b, (((0,), (0,)), ((), ())), preferred_element_type=f32)


def call(body, grid, in_specs, out_specs, out_shape, scratch, flops, moved, near=(), near_out=()):
    listed = isinstance(out_shape, (list, tuple))
    shapes = [
        (pltpu.VMEM if i in near_out else pltpu.HBM)(x.shape, x.dtype)
        for i, x in enumerate(out_shape if listed else [out_shape])
    ]
    shapes = shapes if listed else shapes[0]
    run = pl.pallas_call(
        body,
        grid=grid,
        in_specs=in_specs,
        out_specs=out_specs,
        out_shape=shapes,
        scratch_shapes=scratch,
        compiler_params=pltpu.CompilerParams(vmem_limit_bytes=VMEM_LIMIT),
        cost_estimate=pl.CostEstimate(flops=int(flops), bytes_accessed=int(moved), transcendentals=0),
    )

    def placed(i, x, spec):
        if spec.memory_space == pltpu.SMEM:
            return x
        return pltpu.with_memory_space_constraint(x, pltpu.VMEM if i in near else pltpu.HBM)

    return lambda *args: run(*(placed(i, x, spec) for i, (x, spec) in enumerate(zip(args, in_specs))))


def whole(shape):
    return pl.BlockSpec(shape, lambda s: (0,) * len(shape))


def open_body(field_ref, matrix_ref, part_ref):
    product(matrix_ref, field_ref[...].astype(bf16), part_ref)


def first_body(row_ref, field_ref, out_ref, column_ref, low):
    same = (
        lax.broadcasted_iota(i32, (LANES, LANES), 0) == lax.broadcasted_iota(i32, (LANES, LANES), 1)
    ).astype(f32)
    ones = jnp.ones((LANES, LANES), bf16)
    for t in range(0, row_ref.shape[1], LANES):
        number = row_ref[:, t : t + LANES]
        number = jnp.where(number < 0, -2, number) + 2
        high = number // LANES
        column = dot((same * high.astype(f32)).astype(bf16), ones) * LANES
        column += dot((same * (number - high * LANES).astype(f32)).astype(bf16), ones)
        column_ref[pl.ds(t, LANES), :] = column.astype(i32) - 2
    low[...] = field_ref[...].astype(bf16)

    def rows(at, _):
        out_ref[at, :] = dot(hot_rows(column_ref[at, :], 0, low.shape[0]), low[...]).astype(bf16)

    chunks(out_ref.shape[0], rows, 3)


def settle_body(sign, has_modes, base_ref, in_ref, row_ref, matrix_ref, *rest):
    if has_modes:
        modes_ref, part_ref, proj_ref, low = rest
    else:
        field_ref, part_ref, low = rest
    core = base_ref.shape[0]
    first = pl.program_id(0) * core

    def fields(at, c):
        added = dot(hot_cols(row_ref[...], first + c, at.size), in_ref[...])
        value = base_ref[at, :] + sign * added
        if not has_modes:
            field_ref[at, :] = value
        low[at, :] = value.astype(bf16)

    chunks(core, fields, 2)
    if has_modes:
        proj_ref[...] = dot(modes_ref[0], low[...])
    product(matrix_ref, low[...], part_ref)


def finish_body(sign, base_ref, in_ref, row_ref, field_ref):
    core = field_ref.shape[0]
    first = pl.program_id(0) * core

    def fields(at, c):
        added = dot(hot_cols(row_ref[...], first + c, at.size), in_ref[...])
        field_ref[at, :] = base_ref[at, :] + sign * added

    chunks(core, fields, 2)


def take_margins(in_ref, column_ref, margin_ref):
    def rows(at, _):
        hot = hot_rows(column_ref[at, :], 0, in_ref.shape[0])
        margin_ref[at, :] = dot(hot, in_ref[...]).astype(bf16)

    chunks(margin_ref.shape[0], rows, 2)


def pack(place_ref, outer, out_ref):
    def rows(at, c):
        out_ref[at, :] = dot(hot_cols(place_ref[...], c, at.size), outer[...]).astype(bf16)

    chunks(out_ref.shape[0], rows, 2)


def outer_body(in_ref, column_ref, place_ref, matrix_ref, part_ref, margin_ref, out_ref, outer):
    subs, margins, _ = matrix_ref.shape
    take_margins(in_ref, column_ref, margin_ref)
    for s in range(subs):
        taken = margin_ref[pl.ds(s * margins, margins), :]
        outer[pl.ds(s * margins, margins), :] = (part_ref[s] + dot(matrix_ref[s], taken)).astype(bf16)
    pack(place_ref, outer, out_ref)


def project_body(in_ref, column_ref, modes_ref, proj_ref, margin_ref, out_ref):
    subs, count, margins = modes_ref.shape
    take_margins(in_ref, column_ref, margin_ref)
    for s in range(subs):
        taken = margin_ref[pl.ds(s * margins, margins), :]
        at = pl.ds(s * count, count)
        out_ref[at, :] = (proj_ref[at, :] + dot(modes_ref[s], taken)).astype(bf16)


def split(x):
    high = x.astype(bf16)
    return jnp.concatenate([high, (x - high.astype(f32)).astype(bf16)], axis=1)


def both(x):
    half = x.shape[1] // 2
    return x[:, :half] + x[:, half:]


def coarse_body(side, here_ref, all_ref, *rest):
    inverse_refs = rest[:side]
    margin_ref, place_ref, matrix_ref, part_ref, modes_ref, coarse_ref, out_ref, outer = rest[side:]
    subs, count, margins = modes_ref.shape
    made = 0.0
    for k, inverse_ref in enumerate(inverse_refs):
        width = inverse_ref.shape[1]
        first = pl.multiple_of((here_ref[0] ^ k) * width, width)
        made += dot(inverse_ref[...], all_ref[pl.ds(first, width), :])
    coarse_ref[...] = made
    halves = split(made)
    for s in range(subs):
        at = pl.ds(s * margins, margins)
        solved = part_ref[s] + dot(matrix_ref[s], margin_ref[at, :])
        lifted = both(turned_dot(modes_ref[s], halves[s * count : (s + 1) * count]))
        outer[at, :] = (damping * solved + lifted).astype(bf16)
    pack(place_ref, outer, out_ref)


def inner_body(sign, has_modes, part_ref, matrix_ref, margin_ref, base_ref, column_ref, *rest):
    if has_modes:
        coarse_ref, modes_ref, new_ref, sent_ref, halves, total = rest
    else:
        new_ref, sent_ref, halves, total = rest
    s = pl.program_id(0)
    core = new_ref.shape[0]
    made = part_ref[0] + dot(matrix_ref[0], margin_ref[...])
    if has_modes:
        made = damping * made + both(turned_dot(modes_ref[0], split(coarse_ref[...])))
    value = base_ref[...] + sign * made
    new_ref[...] = value
    halves[...] = split(value)

    @pl.when(s == 0)
    def _():
        total[...] = jnp.zeros_like(total)

    def rows(at, _):
        total[at, :] += dot(hot_rows(column_ref[at, :], s * core, core), halves[...])

    chunks(total.shape[0], rows, 2)

    @pl.when(s == pl.num_programs(0) - 1)
    def _():
        sent_ref[...] = both(total[...])


def relay_body(sign, sent_ref, in_ref, column_ref, row_ref, out_ref):
    def rows(at, _):
        added = dot(hot_pairs(column_ref[at, :], row_ref[...]), in_ref[...])
        out_ref[at, :] = (sent_ref[at, :] + sign * added).astype(bf16)

    chunks(out_ref.shape[0], rows, 2)


def shards(loads, start, stiffness, local_inverse, modes, coarse_inverse, margin_rows):
    owners = lax.axis_size("wide")
    subs, margins = margin_rows.shape
    order = stiffness.shape[1]
    core = order - margins
    held, cols = loads.shape
    count = modes.shape[2]
    coarse_rows = subs * count
    capacity = 3 * subs * margins // (2 * owners)
    slots = owners * capacity
    many = subs * margins
    m_at = core // margins

    flat = margin_rows.reshape(-1)
    source = flat // held
    row = flat - source * held
    onehot = (source[:, None] == jnp.arange(owners, dtype=i32)[None, :]).astype(bf16)
    earlier = (jnp.arange(many)[:, None] > jnp.arange(many)[None, :]).astype(bf16)
    rank = jnp.sum(dot(earlier, onehot) * onehot.astype(f32), axis=1).astype(i32)
    place = source * capacity + rank
    hit = place[:, None] == jnp.arange(slots, dtype=i32)[None, :]
    asked = jnp.sum(jnp.where(hit, row[:, None] + 1, 0), axis=0) - 1

    def trade(x):
        blocks = x.reshape((owners, x.shape[0] // owners) + x.shape[1:])
        got = lax.all_to_all(blocks, "wide", split_axis=0, concat_axis=0, tiled=True)
        return got.reshape(x.shape)

    wanted = trade(asked)
    wanted_row = wanted[None, :]
    place_row = place[None, :]
    place_column = jnp.broadcast_to(place[:, None], (many, LANES))
    wanted_row, place_column = lax.optimization_barrier((wanted_row, place_column))
    modes_turned = jnp.swapaxes(modes, 1, 2)

    rows_spec = pl.BlockSpec((core, cols), lambda s: (s, 0))
    left_spec = pl.BlockSpec((1, order, core), lambda s: (s, 0, 0))
    part_spec = pl.BlockSpec((1, order, cols), lambda s: (s, 0, 0))
    slots_spec = whole((slots, cols))
    held_shape = jax.ShapeDtypeStruct((held, cols), f32)
    part_shape = jax.ShapeDtypeStruct((subs, order, cols), f32)
    slots_low = jax.ShapeDtypeStruct((slots, cols), bf16)
    margin_shape = jax.ShapeDtypeStruct((many, cols), bf16)
    matrix_flops = 2 * subs * order * core * cols
    slot_flops = 2 * held * slots * cols

    going, wanted_column = call(
        first_body, (1,), [whole((1, slots)), whole((held, cols))], [slots_spec, whole((slots, LANES))],
        [slots_low, jax.ShapeDtypeStruct((slots, LANES), i32)], [pltpu.VMEM((held, cols), bf16)],
        slot_flops, 2e6, (0,), (1,),
    )(wanted_row, start)
    begun, own, going = lax.optimization_barrier((start, coarse_inverse.astype(bf16), going))
    part = call(
        open_body, (subs,), [rows_spec, left_spec], part_spec, part_shape, [], matrix_flops, 10e6,
    )(begun, stiffness)

    side = lax.axis_size("narrow")
    here = lax.axis_index("narrow").reshape(1).astype(i32)
    pieces = [own] + [
        lax.ppermute(own, "narrow", [(i, i ^ k) for i in range(side)]) for k in range(1, side)
    ]
    core_modes_spec = pl.BlockSpec((1, count, core), lambda s: (s, 0, 0))
    outer_modes_spec = pl.BlockSpec((subs, count, margins), lambda s: (0, 0, m_at))

    def settle(sign, base, came, matrices, has_modes):
        specs = [rows_spec, slots_spec, whole((1, slots)), left_spec]
        args = [base, came, wanted_row, matrices]
        outs, shapes = [rows_spec, part_spec], [held_shape, part_shape]
        if has_modes:
            specs.append(core_modes_spec)
            args.append(modes_turned)
            outs = [part_spec, pl.BlockSpec((count, cols), lambda s: (s, 0))]
            shapes = [part_shape, jax.ShapeDtypeStruct((coarse_rows, cols), f32)]
        return call(
            functools.partial(settle_body, sign, has_modes), (subs,), specs, outs, shapes,
            [pltpu.VMEM((core, cols), bf16)], slot_flops + matrix_flops, 14e6, (1, 2),
            (),
        )(*args)

    corner_spec = pl.BlockSpec((subs, margins, margins), lambda s: (0, m_at, m_at))
    part_outer_spec = pl.BlockSpec((subs, margins, cols), lambda s: (0, m_at, 0))
    outer_scratch = [pltpu.VMEM((many, cols), bf16)]

    def inner(sign, base, margin, part, matrices, coarse):
        specs = [
            pl.BlockSpec((1, core, cols), lambda s: (s, 0, 0)),
            pl.BlockSpec((1, core, margins), lambda s: (s, 0, m_at)),
            pl.BlockSpec((margins, cols), lambda s: (s, 0)),
            rows_spec,
            whole((slots, LANES)),
        ]
        args = [part, matrices, margin, base, wanted_column]
        if coarse is not None:
            specs += [
                pl.BlockSpec((count, cols), lambda s: (s, 0)),
                core_modes_spec,
            ]
            args += [coarse, modes_turned]
        return call(
            functools.partial(inner_body, sign, coarse is not None), (subs,), specs, [rows_spec, slots_spec],
            [held_shape, jax.ShapeDtypeStruct((slots, cols), f32)],
            [pltpu.VMEM((core, 2 * cols), bf16), pltpu.VMEM((slots, 2 * cols), f32)], 2 * slot_flops, 8e6,
            (4,), (1,),
        )(*args)

    def relay(sign, sent, came):
        return call(
            functools.partial(relay_body, sign), (1,),
            [slots_spec, slots_spec, whole((slots, LANES)), whole((1, slots))], slots_spec, slots_low, [],
            slot_flops // 2, 3e6, (0, 1, 2, 3),
        )(sent, came, wanted_column, wanted_row)

    def stiffness_outer(came, part):
        return call(
            outer_body, (1,),
            [slots_spec, whole((many, LANES)), whole((1, many)), corner_spec, part_outer_spec],
            [whole((many, cols)), slots_spec], [margin_shape, slots_low], outer_scratch, slot_flops, 3e6,
            (0,),
        )(came, place_column, place_row, stiffness, part)

    field = start
    for step in range(ITERS + 1):
        came = trade(going)
        if step == 0:
            pieces, came = lax.optimization_barrier((pieces, came))
        else:
            field, part = settle(1.0, base, back, stiffness, False)
        margin, going = stiffness_outer(came, part)
        back = trade(going)
        base, sent = inner(-1.0, loads, margin, part, stiffness, None)
        if step == ITERS:
            break

        going = relay(-1.0, sent, back)
        came = trade(going)
        part, proj = settle(-1.0, base, back, local_inverse, True)
        margin, projection = call(
            project_body, (1,),
            [slots_spec, whole((many, LANES)), outer_modes_spec, whole((coarse_rows, cols))],
            [whole((many, cols)), whole((coarse_rows, cols))],
            [margin_shape, jax.ShapeDtypeStruct((coarse_rows, cols), bf16)], [], slot_flops // 2, 2e6,
            (0,),
        )(came, place_column, modes_turned, proj)
        everyone = lax.all_gather(projection, "wide", axis=0, tiled=True)
        coarse, going = call(
            functools.partial(coarse_body, side), (1,),
            [pl.BlockSpec(memory_space=pltpu.SMEM), whole((owners * coarse_rows, cols))]
            + [whole(coarse_inverse.shape)] * side
            + [
                whole((many, cols)),
                whole((1, many)),
                corner_spec,
                part_outer_spec,
                outer_modes_spec,
            ],
            [whole((coarse_rows, cols)), slots_spec],
            [jax.ShapeDtypeStruct((coarse_rows, cols), f32), slots_low], outer_scratch, slot_flops, 3e6,
            (1,),
        )(here, everyone, *pieces, margin, place_row, local_inverse, part, modes_turned)
        back = trade(going)
        base, sent = inner(1.0, field, margin, part, local_inverse, coarse)
        going = relay(1.0, sent, back)

    final = call(
        functools.partial(finish_body, -1.0), (subs,), [rows_spec, slots_spec, whole((1, slots))], rows_spec,
        held_shape, [], slot_flops, 4e6, (1, 2),
    )(base, back, wanted_row)
    return field, final


def solution(mesh):
    placed = (
        P("wide", "narrow"),
        P("wide", "narrow"),
        P("wide", None, None),
        P("wide", None, None),
        P("wide", None, None),
        P("wide", "narrow"),
        P("wide", None),
    )
    return jax.shard_map(
        shards,
        mesh=mesh,
        in_specs=placed,
        out_specs=(P("wide", "narrow"), P("wide", "narrow")),
        check_vma=False,
    )
```

```python
import functools

import jax
import jax.numpy as jnp
from jax import lax
from jax.experimental import pallas as pl
from jax.experimental.pallas import tpu as pltpu
from jax.sharding import PartitionSpec as P

ITERS = 2
damping = 0.5
LANES = 128
VMEM_LIMIT = 32 * 1024 * 1024
f32, bf16, i32 = jnp.float32, jnp.bfloat16, jnp.int32


def dot(a, b):
    return jnp.dot(a, b, preferred_element_type=f32)


def hot_rows(column, first, width):
    offset = column - lax.broadcasted_iota(i32, column.shape, 1)
    tiles = [(offset == first + t).astype(f32).astype(bf16) for t in range(0, width, LANES)]
    return jnp.concatenate(tiles, axis=1)


def hot_cols(row, first, height):
    numbers = lax.broadcasted_iota(i32, (height, row.shape[1]), 0) + first
    return (numbers == row).astype(f32).astype(bf16)


def hot_pairs(column, row):
    tiles = [
        (column == row[:, t : t + LANES]).astype(f32).astype(bf16) for t in range(0, row.shape[1], LANES)
    ]
    return jnp.concatenate(tiles, axis=1)


def chunks(count, body, parts):
    size = count // parts
    for first in range(0, count, size):
        body(pl.ds(first, size), first)


def product(matrix_ref, vectors, out_ref):
    def rows(at, _):
        out_ref[0, at, :] = dot(matrix_ref[0, at, :], vectors)

    chunks(out_ref.shape[1], rows, 2)


def turned_dot(a, b):
    return lax.dot_general(a, b, (((0,), (0,)), ((), ())), preferred_element_type=f32)


def call(body, grid, in_specs, out_specs, out_shape, scratch, flops, moved, near=(), near_out=()):
    listed = isinstance(out_shape, (list, tuple))
    shapes = [
        (pltpu.VMEM if i in near_out else pltpu.HBM)(x.shape, x.dtype)
        for i, x in enumerate(out_shape if listed else [out_shape])
    ]
    shapes = shapes if listed else shapes[0]
    run = pl.pallas_call(
        body,
        grid=grid,
        in_specs=in_specs,
        out_specs=out_specs,
        out_shape=shapes,
        scratch_shapes=scratch,
        compiler_params=pltpu.CompilerParams(vmem_limit_bytes=VMEM_LIMIT),
        cost_estimate=pl.CostEstimate(flops=int(flops), bytes_accessed=int(moved), transcendentals=0),
    )

    def placed(i, x, spec):
        if spec.memory_space == pltpu.SMEM:
            return x
        return pltpu.with_memory_space_constraint(x, pltpu.VMEM if i in near else pltpu.HBM)

    return lambda *args: run(*(placed(i, x, spec) for i, (x, spec) in enumerate(zip(args, in_specs))))


def flat_call(body, near, out_shape, near_out, scratch, copies, flops, moved, scalar=()):
    def run(*args):
        places = [
            pltpu.SMEM if i in scalar else pltpu.VMEM if i in near else pltpu.HBM for i in range(len(args))
        ]
        out_places = [pltpu.VMEM if i in near_out else pltpu.HBM for i in range(len(out_shape))]
        return pl.pallas_call(
            body,
            in_specs=[pl.BlockSpec(memory_space=p) for p in places],
            out_specs=[pl.BlockSpec(memory_space=p) for p in out_places],
            out_shape=[p(x.shape, x.dtype) for p, x in zip(out_places, out_shape)],
            scratch_shapes=list(scratch) + [pltpu.SemaphoreType.DMA((copies,))],
            compiler_params=pltpu.CompilerParams(vmem_limit_bytes=VMEM_LIMIT),
            cost_estimate=pl.CostEstimate(flops=int(flops), bytes_accessed=int(moved), transcendentals=0),
        )(*(x if i in scalar else pltpu.with_memory_space_constraint(x, p) for i, (x, p) in enumerate(zip(args, places))))

    return run


def begin(sems, first, pairs):
    started = [pltpu.make_async_copy(a, b, sems.at[first + i]) for i, (a, b) in enumerate(pairs)]
    for copy in started:
        copy.start()
    return started


def finish(copies):
    for copy in copies:
        copy.wait()


def whole(shape):
    return pl.BlockSpec(shape, lambda s: (0,) * len(shape))


def open_body(field_ref, matrix_ref, part_ref):
    product(matrix_ref, field_ref[...].astype(bf16), part_ref)


def turn(row_ref, column_ref):
    same = (
        lax.broadcasted_iota(i32, (LANES, LANES), 0) == lax.broadcasted_iota(i32, (LANES, LANES), 1)
    ).astype(f32)
    ones = jnp.ones((LANES, LANES), bf16)
    for t in range(0, row_ref.shape[1], LANES):
        number = row_ref[:, t : t + LANES]
        number = jnp.where(number < 0, -2, number) + 2
        high = number // LANES
        column = dot((same * high.astype(f32)).astype(bf16), ones) * LANES
        column += dot((same * (number - high * LANES).astype(f32)).astype(bf16), ones)
        column_ref[pl.ds(t, LANES), :] = column.astype(i32) - 2


def first_body(row_ref, place_ref, field_ref, out_ref, column_ref, placed_ref, field, low, made, turned, sems):
    parts = 3
    size = field.shape[0] // parts
    loads = begin(
        sems, 0, [(field_ref.at[pl.ds(k * size, size)], field.at[pl.ds(k * size, size)]) for k in range(parts)]
    )
    turn(row_ref, column_ref)
    turn(place_ref, turned)
    stores = begin(sems, parts, [(turned, placed_ref)])
    for k in range(parts):
        loads[k].wait()
        low[pl.ds(k * size, size), :] = field[pl.ds(k * size, size), :].astype(bf16)
    size = made.shape[0] // parts
    for k in range(parts):
        at = pl.ds(k * size, size)
        made[at, :] = dot(hot_rows(column_ref[at, :], 0, low.shape[0]), low[...]).astype(bf16)
        stores += begin(sems, parts + 1 + k, [(made.at[at], out_ref.at[at])])
    finish(stores)


def settle_body(sign, has_modes, base_ref, in_ref, row_ref, matrix_ref, *rest):
    if has_modes:
        modes_ref, part_ref, proj_ref, low = rest
    else:
        field_ref, part_ref, low = rest
    core = base_ref.shape[0]
    first = pl.program_id(0) * core

    def fields(at, c):
        added = dot(hot_cols(row_ref[...], first + c, at.size), in_ref[...])
        value = base_ref[at, :] + sign * added
        if not has_modes:
            field_ref[at, :] = value
        low[at, :] = value.astype(bf16)

    chunks(core, fields, 2)
    if has_modes:
        proj_ref[...] = dot(modes_ref[0], low[...])
    product(matrix_ref, low[...], part_ref)


def last_body(sign, base_ref, in_ref, row_ref, field_ref):
    core = field_ref.shape[0]
    first = pl.program_id(0) * core

    def fields(at, c):
        added = dot(hot_cols(row_ref[...], first + c, at.size), in_ref[...])
        field_ref[at, :] = base_ref[at, :] + sign * added

    chunks(core, fields, 2)


def take_margins(in_ref, column_ref, margin_ref):
    def rows(at, _):
        hot = hot_rows(column_ref[at, :], 0, in_ref.shape[0])
        margin_ref[at, :] = dot(hot, in_ref[...]).astype(bf16)

    chunks(margin_ref.shape[0], rows, 2)


def pack(place_ref, outer, packed, out_ref, sems, first):
    stores = []
    size = packed.shape[0] // 2
    for k in range(2):
        at = pl.ds(k * size, size)
        packed[at, :] = dot(hot_cols(place_ref[...], k * size, size), outer[...]).astype(bf16)
        stores += begin(sems, first + k, [(packed.at[at], out_ref.at[at])])
    return stores


def outer_body(
    in_ref, placed_ref, place_ref, matrix_ref, part_ref, margin_ref, out_ref,
    placed, place, matrix, part, margin, outer, packed, sems,
):
    subs, margins, _ = matrix.shape
    core = matrix_ref.shape[1] - margins
    loads = begin(
        sems, 0,
        [
            (placed_ref, placed),
            (place_ref, place),
            (matrix_ref.at[:, core:, core:], matrix),
            (part_ref.at[:, core:, :], part),
        ],
    )
    loads[0].wait()
    take_margins(in_ref, placed, margin)
    stores = begin(sems, 4, [(margin, margin_ref)])
    finish(loads[1:])
    for s in range(subs):
        at = pl.ds(s * margins, margins)
        outer[at, :] = (part[s] + dot(matrix[s], margin[at, :])).astype(bf16)
    finish(stores + pack(place, outer, packed, out_ref, sems, 5))


def project_body(in_ref, placed_ref, modes_ref, proj_ref, margin_ref, out_ref, placed, modes, proj, margin, made, sems):
    subs, count, margins = modes.shape
    core = modes_ref.shape[2] - margins
    loads = begin(sems, 0, [(placed_ref, placed), (modes_ref.at[:, :, core:], modes), (proj_ref, proj)])
    loads[0].wait()
    take_margins(in_ref, placed, margin)
    stores = begin(sems, 3, [(margin, margin_ref)])
    finish(loads[1:])
    for s in range(subs):
        at = pl.ds(s * count, count)
        made[at, :] = (proj[at, :] + dot(modes[s], margin[pl.ds(s * margins, margins), :])).astype(bf16)
    finish(stores + begin(sems, 4, [(made, out_ref)]))


def split(x):
    high = x.astype(bf16)
    return jnp.concatenate([high, (x - high.astype(f32)).astype(bf16)], axis=1)


def both(x):
    half = x.shape[1] // 2
    return x[:, :half] + x[:, half:]


def coarse_body(side, here_ref, all_ref, *rest):
    inverse_refs = rest[:side]
    margin_ref, place_ref, matrix_ref, part_ref, modes_ref, coarse_ref, out_ref = rest[side : side + 7]
    inverse, margin, place, matrix, part, modes, made, outer, packed, sems = rest[side + 7 :]
    subs, count, margins = modes.shape
    core = matrix_ref.shape[1] - margins
    loads = begin(
        sems, 0,
        [(inverse_refs[k], inverse.at[k]) for k in range(side)]
        + [
            (modes_ref.at[:, :, core:], modes),
            (margin_ref, margin),
            (matrix_ref.at[:, core:, core:], matrix),
            (part_ref.at[:, core:, :], part),
            (place_ref, place),
        ],
    )
    finish(loads[:side])
    value = 0.0
    for k in range(side):
        width = inverse.shape[2]
        at = pl.multiple_of((here_ref[0] ^ k) * width, width)
        value += dot(inverse[k], all_ref[pl.ds(at, width), :])
    made[...] = value
    stores = begin(sems, side + 5, [(made, coarse_ref)])
    halves = split(value)
    finish(loads[side:])
    for s in range(subs):
        at = pl.ds(s * margins, margins)
        solved = part[s] + dot(matrix[s], margin[at, :])
        lifted = both(turned_dot(modes[s], halves[s * count : (s + 1) * count]))
        outer[at, :] = (damping * solved + lifted).astype(bf16)
    finish(stores + pack(place, outer, packed, out_ref, sems, side + 6))


def inner_body(sign, has_modes, part_ref, matrix_ref, margin_ref, base_ref, column_ref, *rest):
    if has_modes:
        coarse_ref, modes_ref, new_ref, sent_ref, halves, total = rest
    else:
        new_ref, sent_ref, halves, total = rest
    s = pl.program_id(0)
    core = new_ref.shape[0]
    made = part_ref[0] + dot(matrix_ref[0], margin_ref[...])
    if has_modes:
        made = damping * made + both(turned_dot(modes_ref[0], split(coarse_ref[...])))
    value = base_ref[...] + sign * made
    new_ref[...] = value
    halves[...] = split(value)

    @pl.when(s == 0)
    def _():
        total[...] = jnp.zeros_like(total)

    def rows(at, _):
        total[at, :] += dot(hot_rows(column_ref[at, :], s * core, core), halves[...])

    chunks(total.shape[0], rows, 2)

    @pl.when(s == pl.num_programs(0) - 1)
    def _():
        sent_ref[...] = both(total[...])


def relay_body(sign, sent_ref, in_ref, column_ref, row_ref, out_ref, made, sems):
    stores = []
    size = made.shape[0] // 2
    for k in range(2):
        at = pl.ds(k * size, size)
        added = dot(hot_pairs(column_ref[at, :], row_ref[...]), in_ref[...])
        made[at, :] = (sent_ref[at, :] + sign * added).astype(bf16)
        stores += begin(sems, k, [(made.at[at], out_ref.at[at])])
    finish(stores)


def shards(loads, start, stiffness, local_inverse, modes, coarse_inverse, margin_rows):
    owners = lax.axis_size("wide")
    subs, margins = margin_rows.shape
    order = stiffness.shape[1]
    core = order - margins
    held, cols = loads.shape
    count = modes.shape[2]
    coarse_rows = subs * count
    capacity = 3 * subs * margins // (2 * owners)
    slots = owners * capacity
    many = subs * margins
    m_at = core // margins

    flat = margin_rows.reshape(-1)
    source = flat // held
    row = flat - source * held
    onehot = (source[:, None] == jnp.arange(owners, dtype=i32)[None, :]).astype(bf16)
    earlier = (jnp.arange(many)[:, None] > jnp.arange(many)[None, :]).astype(bf16)
    rank = jnp.sum(dot(earlier, onehot) * onehot.astype(f32), axis=1).astype(i32)
    place = source * capacity + rank
    hit = place[:, None] == jnp.arange(slots, dtype=i32)[None, :]
    asked = jnp.sum(jnp.where(hit, row[:, None] + 1, 0), axis=0) - 1

    def trade(x):
        blocks = x.reshape((owners, x.shape[0] // owners) + x.shape[1:])
        got = lax.all_to_all(blocks, "wide", split_axis=0, concat_axis=0, tiled=True)
        return got.reshape(x.shape)

    wanted = trade(asked)
    wanted_row = wanted[None, :]
    place_row = place[None, :]
    modes_turned = jnp.swapaxes(modes, 1, 2)

    rows_spec = pl.BlockSpec((core, cols), lambda s: (s, 0))
    left_spec = pl.BlockSpec((1, order, core), lambda s: (s, 0, 0))
    part_spec = pl.BlockSpec((1, order, cols), lambda s: (s, 0, 0))
    slots_spec = whole((slots, cols))
    held_shape = jax.ShapeDtypeStruct((held, cols), f32)
    part_shape = jax.ShapeDtypeStruct((subs, order, cols), f32)
    slots_low = jax.ShapeDtypeStruct((slots, cols), bf16)
    margin_shape = jax.ShapeDtypeStruct((many, cols), bf16)
    matrix_flops = 2 * subs * order * core * cols
    slot_flops = 2 * held * slots * cols

    going, wanted_column, place_column = flat_call(
        first_body, (0, 1),
        [slots_low, jax.ShapeDtypeStruct((slots, LANES), i32), jax.ShapeDtypeStruct((many, LANES), i32)], (1,),
        [
            pltpu.VMEM((held, cols), f32), pltpu.VMEM((held, cols), bf16), pltpu.VMEM((slots, cols), bf16),
            pltpu.VMEM((many, LANES), i32),
        ],
        7, slot_flops, 4e6,
    )(wanted_row, place_row, start)
    side = lax.axis_size("narrow")
    here = lax.axis_index("narrow").reshape(1).astype(i32)
    own = coarse_inverse.astype(bf16)
    pieces = [own] + [
        lax.ppermute(own, "narrow", [(i, i ^ k) for i in range(side)]) for k in range(1, side)
    ]
    begun, pieces, going = lax.optimization_barrier((start, pieces, going))
    part = call(
        open_body, (subs,), [rows_spec, left_spec], part_spec, part_shape, [], matrix_flops, 10e6,
    )(begun, stiffness)

    core_modes_spec = pl.BlockSpec((1, count, core), lambda s: (s, 0, 0))
    outer_modes_spec = pl.BlockSpec((subs, count, margins), lambda s: (0, 0, m_at))

    def settle(sign, base, came, matrices, has_modes):
        specs = [rows_spec, slots_spec, whole((1, slots)), left_spec]
        args = [base, came, wanted_row, matrices]
        outs, shapes = [rows_spec, part_spec], [held_shape, part_shape]
        if has_modes:
            specs.append(core_modes_spec)
            args.append(modes_turned)
            outs = [part_spec, pl.BlockSpec((count, cols), lambda s: (s, 0))]
            shapes = [part_shape, jax.ShapeDtypeStruct((coarse_rows, cols), f32)]
        return call(
            functools.partial(settle_body, sign, has_modes), (subs,), specs, outs, shapes,
            [pltpu.VMEM((core, cols), bf16)], slot_flops + matrix_flops, 14e6, (1, 2),
            (),
        )(*args)

    corner_spec = pl.BlockSpec((subs, margins, margins), lambda s: (0, m_at, m_at))
    part_outer_spec = pl.BlockSpec((subs, margins, cols), lambda s: (0, m_at, 0))
    outer_scratch = [pltpu.VMEM((many, cols), bf16)]

    def inner(sign, base, margin, part, matrices, coarse):
        specs = [
            pl.BlockSpec((1, core, cols), lambda s: (s, 0, 0)),
            pl.BlockSpec((1, core, margins), lambda s: (s, 0, m_at)),
            pl.BlockSpec((margins, cols), lambda s: (s, 0)),
            rows_spec,
            whole((slots, LANES)),
        ]
        args = [part, matrices, margin, base, wanted_column]
        if coarse is not None:
            specs += [
                pl.BlockSpec((count, cols), lambda s: (s, 0)),
                core_modes_spec,
            ]
            args += [coarse, modes_turned]
        return call(
            functools.partial(inner_body, sign, coarse is not None), (subs,), specs, [rows_spec, slots_spec],
            [held_shape, jax.ShapeDtypeStruct((slots, cols), f32)],
            [pltpu.VMEM((core, 2 * cols), bf16), pltpu.VMEM((slots, 2 * cols), f32)], 2 * slot_flops, 8e6,
            (4,), (1,),
        )(*args)

    def relay(sign, sent, came):
        return flat_call(
            functools.partial(relay_body, sign), (0, 1, 2, 3), [slots_low], (), [pltpu.VMEM((slots, cols), bf16)], 2,
            slot_flops // 2, 3e6,
        )(sent, came, wanted_column, wanted_row)[0]

    column_scratch = pltpu.VMEM((many, LANES), i32)
    corner_scratch = [
        pltpu.VMEM((subs, margins, margins), bf16), pltpu.VMEM((subs, margins, cols), f32),
    ]
    margin_scratch = pltpu.VMEM((many, cols), bf16)
    packed_scratch = pltpu.VMEM((slots, cols), bf16)
    modes_scratch = pltpu.VMEM((subs, count, margins), bf16)

    def stiffness_outer(came, part):
        return flat_call(
            outer_body, (0,), [margin_shape, slots_low], (),
            [column_scratch, pltpu.VMEM((1, many), i32)] + corner_scratch
            + [margin_scratch, margin_scratch, packed_scratch],
            7, slot_flops, 3e6,
        )(came, place_column, place_row, stiffness, part)

    field = start
    for step in range(ITERS + 1):
        came = trade(going)
        if step > 0:
            field, part = settle(1.0, base, back, stiffness, False)
        margin, going = stiffness_outer(came, part)
        back = trade(going)
        base, sent = inner(-1.0, loads, margin, part, stiffness, None)
        if step == ITERS:
            break

        going = relay(-1.0, sent, back)
        came = trade(going)
        part, proj = settle(-1.0, base, back, local_inverse, True)
        margin, projection = flat_call(
            project_body, (0,), [margin_shape, jax.ShapeDtypeStruct((coarse_rows, cols), bf16)], (),
            [
                column_scratch, modes_scratch, pltpu.VMEM((coarse_rows, cols), f32), margin_scratch,
                pltpu.VMEM((coarse_rows, cols), bf16),
            ],
            5, slot_flops // 2, 2e6,
        )(came, place_column, modes_turned, proj)
        everyone = lax.all_gather(projection, "wide", axis=0, tiled=True)
        coarse, going = flat_call(
            functools.partial(coarse_body, side), (1,), [jax.ShapeDtypeStruct((coarse_rows, cols), f32), slots_low], (),
            [pltpu.VMEM((side,) + coarse_inverse.shape, bf16), margin_scratch, pltpu.VMEM((1, many), i32)]
            + corner_scratch
            + [modes_scratch, pltpu.VMEM((coarse_rows, cols), f32), margin_scratch, packed_scratch],
            side + 8, slot_flops, 3e6, (0,),
        )(here, everyone, *pieces, margin, place_row, local_inverse, part, modes_turned)
        back = trade(going)
        base, sent = inner(1.0, field, margin, part, local_inverse, coarse)
        going = relay(1.0, sent, back)

    final = call(
        functools.partial(last_body, -1.0), (subs,), [rows_spec, slots_spec, whole((1, slots))], rows_spec,
        held_shape, [], slot_flops, 4e6, (1, 2),
    )(base, back, wanted_row)
    return field, final


def solution(mesh):
    placed = (
        P("wide", "narrow"),
        P("wide", "narrow"),
        P("wide", None, None),
        P("wide", None, None),
        P("wide", None, None),
        P("wide", "narrow"),
        P("wide", None),
    )
    return jax.shard_map(
        shards,
        mesh=mesh,
        in_specs=placed,
        out_specs=(P("wide", "narrow"), P("wide", "narrow")),
        check_vma=False,
    )
```

```python
import functools

import jax
import jax.numpy as jnp
from jax import lax
from jax.experimental import pallas as pl
from jax.experimental.pallas import tpu as pltpu
from jax.sharding import PartitionSpec as P

ITERS = 2
damping = 0.5
LANES = 128
VMEM_LIMIT = 32 * 1024 * 1024
f32, bf16, i32 = jnp.float32, jnp.bfloat16, jnp.int32


def dot(a, b):
    return jnp.dot(a, b, preferred_element_type=f32)


def hot_rows(column, first, width):
    offset = column - lax.broadcasted_iota(i32, column.shape, 1)
    tiles = [(offset == first + t).astype(f32).astype(bf16) for t in range(0, width, LANES)]
    return jnp.concatenate(tiles, axis=1)


def hot_cols(row, first, height):
    numbers = lax.broadcasted_iota(i32, (height, row.shape[1]), 0) + first
    return (numbers == row).astype(f32).astype(bf16)


def hot_pairs(column, row):
    tiles = [
        (column == row[:, t : t + LANES]).astype(f32).astype(bf16) for t in range(0, row.shape[1], LANES)
    ]
    return jnp.concatenate(tiles, axis=1)


def chunks(count, body, parts):
    size = count // parts
    for first in range(0, count, size):
        body(pl.ds(first, size), first)


def product(matrix_ref, vectors, out_ref):
    def rows(at, _):
        out_ref[0, at, :] = dot(matrix_ref[0, at, :], vectors)

    chunks(out_ref.shape[1], rows, 2)


def turned_dot(a, b):
    return lax.dot_general(a, b, (((0,), (0,)), ((), ())), preferred_element_type=f32)


def call(body, grid, in_specs, out_specs, out_shape, scratch, flops, moved, near=(), near_out=()):
    listed = isinstance(out_shape, (list, tuple))
    shapes = [
        (pltpu.VMEM if i in near_out else pltpu.HBM)(x.shape, x.dtype)
        for i, x in enumerate(out_shape if listed else [out_shape])
    ]
    shapes = shapes if listed else shapes[0]
    run = pl.pallas_call(
        body,
        grid=grid,
        in_specs=in_specs,
        out_specs=out_specs,
        out_shape=shapes,
        scratch_shapes=scratch,
        compiler_params=pltpu.CompilerParams(vmem_limit_bytes=VMEM_LIMIT),
        cost_estimate=pl.CostEstimate(flops=int(flops), bytes_accessed=int(moved), transcendentals=0),
    )

    def placed(i, x, spec):
        if spec.memory_space == pltpu.SMEM:
            return x
        return pltpu.with_memory_space_constraint(x, pltpu.VMEM if i in near else pltpu.HBM)

    return lambda *args: run(*(placed(i, x, spec) for i, (x, spec) in enumerate(zip(args, in_specs))))


def flat_call(body, near, out_shape, near_out, scratch, copies, flops, moved, scalar=()):
    def run(*args):
        places = [
            pltpu.SMEM if i in scalar else pltpu.VMEM if i in near else pltpu.HBM for i in range(len(args))
        ]
        out_places = [pltpu.VMEM if i in near_out else pltpu.HBM for i in range(len(out_shape))]
        return pl.pallas_call(
            body,
            in_specs=[pl.BlockSpec(memory_space=p) for p in places],
            out_specs=[pl.BlockSpec(memory_space=p) for p in out_places],
            out_shape=[p(x.shape, x.dtype) for p, x in zip(out_places, out_shape)],
            scratch_shapes=list(scratch) + [pltpu.SemaphoreType.DMA((copies,))],
            compiler_params=pltpu.CompilerParams(vmem_limit_bytes=VMEM_LIMIT),
            cost_estimate=pl.CostEstimate(flops=int(flops), bytes_accessed=int(moved), transcendentals=0),
        )(*(x if i in scalar else pltpu.with_memory_space_constraint(x, p) for i, (x, p) in enumerate(zip(args, places))))

    return run


def begin(sems, first, pairs):
    started = [pltpu.make_async_copy(a, b, sems.at[first + i]) for i, (a, b) in enumerate(pairs)]
    for copy in started:
        copy.start()
    return started


def finish(copies):
    for copy in copies:
        copy.wait()


def whole(shape):
    return pl.BlockSpec(shape, lambda s: (0,) * len(shape))


def open_body(field_ref, matrix_ref, part_ref):
    product(matrix_ref, field_ref[...].astype(bf16), part_ref)


def turn(row_ref, column_ref):
    same = (
        lax.broadcasted_iota(i32, (LANES, LANES), 0) == lax.broadcasted_iota(i32, (LANES, LANES), 1)
    ).astype(f32)
    ones = jnp.ones((LANES, LANES), bf16)
    for t in range(0, row_ref.shape[1], LANES):
        number = row_ref[:, t : t + LANES]
        number = jnp.where(number < 0, -2, number) + 2
        high = number // LANES
        column = dot((same * high.astype(f32)).astype(bf16), ones) * LANES
        column += dot((same * (number - high * LANES).astype(f32)).astype(bf16), ones)
        column_ref[pl.ds(t, LANES), :] = column.astype(i32) - 2


def first_body(row_ref, place_ref, field_ref, out_ref, column_ref, placed_ref, field, low, made, turned, sems):
    parts = 3
    size = field.shape[0] // parts
    loads = begin(
        sems, 0, [(field_ref.at[pl.ds(k * size, size)], field.at[pl.ds(k * size, size)]) for k in range(parts)]
    )
    turn(row_ref, column_ref)
    turn(place_ref, turned)
    stores = begin(sems, parts, [(turned, placed_ref)])
    for k in range(parts):
        loads[k].wait()
        low[pl.ds(k * size, size), :] = field[pl.ds(k * size, size), :].astype(bf16)
    size = made.shape[0] // parts
    for k in range(parts):
        at = pl.ds(k * size, size)
        made[at, :] = dot(hot_rows(column_ref[at, :], 0, low.shape[0]), low[...]).astype(bf16)
        stores += begin(sems, parts + 1 + k, [(made.at[at], out_ref.at[at])])
    finish(stores)


def settle_body(sign, has_modes, base_ref, in_ref, row_ref, matrix_ref, *rest):
    if has_modes:
        modes_ref, part_ref, proj_ref, low = rest
    else:
        field_ref, part_ref, low = rest
    core = base_ref.shape[0]
    first = pl.program_id(0) * core

    def fields(at, c):
        added = dot(hot_cols(row_ref[...], first + c, at.size), in_ref[...])
        value = base_ref[at, :] + sign * added
        if not has_modes:
            field_ref[at, :] = value
        low[at, :] = value.astype(bf16)

    chunks(core, fields, 2)
    if has_modes:
        proj_ref[...] = dot(modes_ref[0], low[...])
    product(matrix_ref, low[...], part_ref)


def last_body(sign, base_ref, in_ref, row_ref, field_ref, made, sems):
    stores = []
    parts = sems.shape[0]
    size = made.shape[0] // parts
    for k in range(parts):
        at = pl.ds(k * size, size)
        added = dot(hot_cols(row_ref[...], k * size, size), in_ref[...])
        made[at, :] = base_ref[at, :] + sign * added
        stores += begin(sems, k, [(made.at[at], field_ref.at[at])])
    finish(stores)


def take_margins(in_ref, column_ref, margin_ref):
    def rows(at, _):
        hot = hot_rows(column_ref[at, :], 0, in_ref.shape[0])
        margin_ref[at, :] = dot(hot, in_ref[...]).astype(bf16)

    chunks(margin_ref.shape[0], rows, 2)


def pack(place_ref, outer, packed, out_ref, sems, first):
    stores = []
    size = packed.shape[0] // 2
    for k in range(2):
        at = pl.ds(k * size, size)
        packed[at, :] = dot(hot_cols(place_ref[...], k * size, size), outer[...]).astype(bf16)
        stores += begin(sems, first + k, [(packed.at[at], out_ref.at[at])])
    return stores


def outer_body(
    in_ref, placed_ref, place_ref, matrix_ref, part_ref, margin_ref, out_ref,
    placed, place, matrix, part, margin, outer, packed, sems,
):
    subs, margins, _ = matrix.shape
    core = matrix_ref.shape[1] - margins
    loads = begin(
        sems, 0,
        [
            (placed_ref, placed),
            (place_ref, place),
            (matrix_ref.at[:, core:, core:], matrix),
            (part_ref.at[:, core:, :], part),
        ],
    )
    loads[0].wait()
    take_margins(in_ref, placed, margin)
    stores = begin(sems, 4, [(margin, margin_ref)])
    finish(loads[1:])
    for s in range(subs):
        at = pl.ds(s * margins, margins)
        outer[at, :] = (part[s] + dot(matrix[s], margin[at, :])).astype(bf16)
    finish(stores + pack(place, outer, packed, out_ref, sems, 5))


def project_body(in_ref, placed_ref, modes_ref, proj_ref, margin_ref, out_ref, placed, modes, proj, margin, made, sems):
    subs, count, margins = modes.shape
    core = modes_ref.shape[2] - margins
    loads = begin(sems, 0, [(placed_ref, placed), (modes_ref.at[:, :, core:], modes), (proj_ref, proj)])
    loads[0].wait()
    take_margins(in_ref, placed, margin)
    stores = begin(sems, 3, [(margin, margin_ref)])
    finish(loads[1:])
    for s in range(subs):
        at = pl.ds(s * count, count)
        made[at, :] = (proj[at, :] + dot(modes[s], margin[pl.ds(s * margins, margins), :])).astype(bf16)
    finish(stores + begin(sems, 4, [(made, out_ref)]))


def split(x):
    high = x.astype(bf16)
    return jnp.concatenate([high, (x - high.astype(f32)).astype(bf16)], axis=1)


def both(x):
    half = x.shape[1] // 2
    return x[:, :half] + x[:, half:]


def coarse_body(side, place_count, here_ref, *rest):
    pairs, rest = rest[:place_count], rest[place_count:]
    inverse_refs = rest[:side]
    margin_ref, place_ref, matrix_ref, part_ref, modes_ref, coarse_ref, out_ref = rest[side : side + 7]
    inverse, everyone, margin, place, matrix, part, modes, made, outer, packed, sems = rest[side + 7 :]
    subs, count, margins = modes.shape
    core = matrix_ref.shape[1] - margins
    loads = begin(
        sems, 0,
        [(inverse_refs[k], inverse.at[k]) for k in range(side)]
        + [
            (modes_ref.at[:, :, core:], modes),
            (margin_ref, margin),
            (matrix_ref.at[:, core:, core:], matrix),
            (part_ref.at[:, core:, :], part),
            (place_ref, place),
        ],
    )
    height = made.shape[0]
    for k, pair_ref in enumerate(pairs):
        for j in range(2):
            at = pl.multiple_of((here_ref[1] ^ (2 * k + j)) * height, height)
            everyone[pl.ds(at, height), :] = pair_ref[j * height : (j + 1) * height, :]
    finish(loads[:side])
    value = 0.0
    for k in range(side):
        width = inverse.shape[2]
        at = pl.multiple_of((here_ref[0] ^ k) * width, width)
        value += dot(inverse[k], everyone[pl.ds(at, width), :])
    made[...] = value
    stores = begin(sems, side + 5, [(made, coarse_ref)])
    halves = split(value)
    finish(loads[side:])
    for s in range(subs):
        at = pl.ds(s * margins, margins)
        solved = part[s] + dot(matrix[s], margin[at, :])
        lifted = both(turned_dot(modes[s], halves[s * count : (s + 1) * count]))
        outer[at, :] = (damping * solved + lifted).astype(bf16)
    finish(stores + pack(place, outer, packed, out_ref, sems, side + 6))


def inner_body(sign, has_modes, part_ref, matrix_ref, margin_ref, base_ref, column_ref, *rest):
    if has_modes:
        coarse_ref, modes_ref, new_ref, sent_ref, halves, total = rest
    else:
        new_ref, sent_ref, halves, total = rest
    s = pl.program_id(0)
    core = new_ref.shape[0]
    made = part_ref[0] + dot(matrix_ref[0], margin_ref[...])
    if has_modes:
        made = damping * made + both(turned_dot(modes_ref[0], split(coarse_ref[...])))
    value = base_ref[...] + sign * made
    new_ref[...] = value
    halves[...] = split(value)

    @pl.when(s == 0)
    def _():
        total[...] = jnp.zeros_like(total)

    def rows(at, _):
        total[at, :] += dot(hot_rows(column_ref[at, :], s * core, core), halves[...])

    chunks(total.shape[0], rows, 2)

    @pl.when(s == pl.num_programs(0) - 1)
    def _():
        sent_ref[...] = both(total[...])


def relay_body(sign, sent_ref, in_ref, column_ref, row_ref, out_ref, made, sems):
    stores = []
    size = made.shape[0] // 2
    for k in range(2):
        at = pl.ds(k * size, size)
        added = dot(hot_pairs(column_ref[at, :], row_ref[...]), in_ref[...])
        made[at, :] = (sent_ref[at, :] + sign * added).astype(bf16)
        stores += begin(sems, k, [(made.at[at], out_ref.at[at])])
    finish(stores)


def shards(loads, start, stiffness, local_inverse, modes, coarse_inverse, margin_rows):
    owners = lax.axis_size("wide")
    subs, margins = margin_rows.shape
    order = stiffness.shape[1]
    core = order - margins
    held, cols = loads.shape
    count = modes.shape[2]
    coarse_rows = subs * count
    capacity = 3 * subs * margins // (2 * owners)
    slots = owners * capacity
    many = subs * margins
    m_at = core // margins

    flat = margin_rows.reshape(-1)
    source = flat // held
    row = flat - source * held
    onehot = (source[:, None] == jnp.arange(owners, dtype=i32)[None, :]).astype(bf16)
    earlier = (jnp.arange(many)[:, None] > jnp.arange(many)[None, :]).astype(bf16)
    rank = jnp.sum(dot(earlier, onehot) * onehot.astype(f32), axis=1).astype(i32)
    place = source * capacity + rank
    hit = place[:, None] == jnp.arange(slots, dtype=i32)[None, :]
    asked = jnp.sum(jnp.where(hit, row[:, None] + 1, 0), axis=0) - 1

    def trade(x):
        blocks = x.reshape((owners, x.shape[0] // owners) + x.shape[1:])
        got = lax.all_to_all(blocks, "wide", split_axis=0, concat_axis=0, tiled=True)
        return got.reshape(x.shape)

    wanted = trade(asked)
    wanted_row = wanted[None, :]
    place_row = place[None, :]
    modes_turned = jnp.swapaxes(modes, 1, 2)

    rows_spec = pl.BlockSpec((core, cols), lambda s: (s, 0))
    left_spec = pl.BlockSpec((1, order, core), lambda s: (s, 0, 0))
    part_spec = pl.BlockSpec((1, order, cols), lambda s: (s, 0, 0))
    slots_spec = whole((slots, cols))
    held_shape = jax.ShapeDtypeStruct((held, cols), f32)
    part_shape = jax.ShapeDtypeStruct((subs, order, cols), f32)
    slots_low = jax.ShapeDtypeStruct((slots, cols), bf16)
    margin_shape = jax.ShapeDtypeStruct((many, cols), bf16)
    matrix_flops = 2 * subs * order * core * cols
    slot_flops = 2 * held * slots * cols

    going, wanted_column, place_column = flat_call(
        first_body, (0, 1),
        [slots_low, jax.ShapeDtypeStruct((slots, LANES), i32), jax.ShapeDtypeStruct((many, LANES), i32)], (1,),
        [
            pltpu.VMEM((held, cols), f32), pltpu.VMEM((held, cols), bf16), pltpu.VMEM((slots, cols), bf16),
            pltpu.VMEM((many, LANES), i32),
        ],
        7, slot_flops, 4e6,
    )(wanted_row, place_row, start)
    side = lax.axis_size("narrow")
    here = jnp.stack([lax.axis_index("narrow"), lax.axis_index("wide")]).astype(i32)
    begun, own, going = lax.optimization_barrier((start, coarse_inverse.astype(bf16), going))
    pieces = [own] + [
        lax.ppermute(own, "narrow", [(i, i ^ k) for i in range(side)]) for k in range(1, side)
    ]
    part = call(
        open_body, (subs,), [rows_spec, left_spec], part_spec, part_shape, [], matrix_flops, 10e6,
    )(begun, stiffness)

    core_modes_spec = pl.BlockSpec((1, count, core), lambda s: (s, 0, 0))
    outer_modes_spec = pl.BlockSpec((subs, count, margins), lambda s: (0, 0, m_at))

    def settle(sign, base, came, matrices, has_modes):
        specs = [rows_spec, slots_spec, whole((1, slots)), left_spec]
        args = [base, came, wanted_row, matrices]
        outs, shapes = [rows_spec, part_spec], [held_shape, part_shape]
        if has_modes:
            specs.append(core_modes_spec)
            args.append(modes_turned)
            outs = [part_spec, pl.BlockSpec((count, cols), lambda s: (s, 0))]
            shapes = [part_shape, jax.ShapeDtypeStruct((coarse_rows, cols), f32)]
        return call(
            functools.partial(settle_body, sign, has_modes), (subs,), specs, outs, shapes,
            [pltpu.VMEM((core, cols), bf16)], slot_flops + matrix_flops, 14e6, (1, 2),
            (),
        )(*args)

    corner_spec = pl.BlockSpec((subs, margins, margins), lambda s: (0, m_at, m_at))
    part_outer_spec = pl.BlockSpec((subs, margins, cols), lambda s: (0, m_at, 0))
    outer_scratch = [pltpu.VMEM((many, cols), bf16)]

    def inner(sign, base, margin, part, matrices, coarse, near_out=(1,)):
        specs = [
            pl.BlockSpec((1, core, cols), lambda s: (s, 0, 0)),
            pl.BlockSpec((1, core, margins), lambda s: (s, 0, m_at)),
            pl.BlockSpec((margins, cols), lambda s: (s, 0)),
            rows_spec,
            whole((slots, LANES)),
        ]
        args = [part, matrices, margin, base, wanted_column]
        if coarse is not None:
            specs += [
                pl.BlockSpec((count, cols), lambda s: (s, 0)),
                core_modes_spec,
            ]
            args += [coarse, modes_turned]
        return call(
            functools.partial(inner_body, sign, coarse is not None), (subs,), specs, [rows_spec, slots_spec],
            [held_shape, jax.ShapeDtypeStruct((slots, cols), f32)],
            [pltpu.VMEM((core, 2 * cols), bf16), pltpu.VMEM((slots, 2 * cols), f32)], 2 * slot_flops, 8e6,
            (4,), near_out,
        )(*args)

    def relay(sign, sent, came):
        return flat_call(
            functools.partial(relay_body, sign), (0, 1, 2, 3), [slots_low], (), [pltpu.VMEM((slots, cols), bf16)], 2,
            slot_flops // 2, 3e6,
        )(sent, came, wanted_column, wanted_row)[0]

    column_scratch = pltpu.VMEM((many, LANES), i32)
    corner_scratch = [
        pltpu.VMEM((subs, margins, margins), bf16), pltpu.VMEM((subs, margins, cols), f32),
    ]
    margin_scratch = pltpu.VMEM((many, cols), bf16)
    packed_scratch = pltpu.VMEM((slots, cols), bf16)
    modes_scratch = pltpu.VMEM((subs, count, margins), bf16)

    def stiffness_outer(came, part):
        return flat_call(
            outer_body, (0,), [margin_shape, slots_low], (),
            [column_scratch, pltpu.VMEM((1, many), i32)] + corner_scratch
            + [margin_scratch, margin_scratch, packed_scratch],
            7, slot_flops, 3e6,
        )(came, place_column, place_row, stiffness, part)

    field = start
    for step in range(ITERS + 1):
        came = trade(going)
        if step == 0:
            pieces, came = lax.optimization_barrier((pieces, came))
        else:
            field, part = settle(1.0, base, back, stiffness, False)
        margin, going = stiffness_outer(came, part)
        back = trade(going)
        base, sent = inner(-1.0, loads, margin, part, stiffness, None, (0,) if step == ITERS else (1,))
        if step == ITERS:
            break

        going = relay(-1.0, sent, back)
        came = trade(going)
        part, proj = settle(-1.0, base, back, local_inverse, True)
        margin, projection = flat_call(
            project_body, (0,), [margin_shape, jax.ShapeDtypeStruct((coarse_rows, cols), bf16)], (),
            [
                column_scratch, modes_scratch, pltpu.VMEM((coarse_rows, cols), f32), margin_scratch,
                pltpu.VMEM((coarse_rows, cols), bf16),
            ],
            5, slot_flops // 2, 2e6,
        )(came, place_column, modes_turned, proj)
        partner = lax.ppermute(projection, "wide", [(i, i ^ 1) for i in range(owners)])
        pair = jnp.concatenate([projection, partner], axis=0)
        pairs = [pair] + [
            lax.ppermute(pair, "wide", [(i, i ^ k) for i in range(owners)]) for k in range(2, owners, 2)
        ]
        coarse, going = flat_call(
            functools.partial(coarse_body, side, len(pairs)), tuple(range(1, len(pairs) + 1)), [jax.ShapeDtypeStruct((coarse_rows, cols), f32), slots_low], (),
            [
                pltpu.VMEM((side,) + coarse_inverse.shape, bf16), pltpu.VMEM((owners * coarse_rows, cols), bf16),
                margin_scratch, pltpu.VMEM((1, many), i32),
            ]
            + corner_scratch
            + [modes_scratch, pltpu.VMEM((coarse_rows, cols), f32), margin_scratch, packed_scratch],
            side + 8, slot_flops, 3e6, (0,),
        )(here, *pairs, *pieces, margin, place_row, local_inverse, part, modes_turned)
        back = trade(going)
        base, sent = inner(1.0, field, margin, part, local_inverse, coarse)
        going = relay(1.0, sent, back)

    final = flat_call(
        functools.partial(last_body, -1.0), (0, 1, 2), [held_shape], (), [pltpu.VMEM((held, cols), f32)], 2 * subs,
        slot_flops, 4e6,
    )(base, back, wanted_row)[0]
    return field, final


def solution(mesh):
    placed = (
        P("wide", "narrow"),
        P("wide", "narrow"),
        P("wide", None, None),
        P("wide", None, None),
        P("wide", None, None),
        P("wide", "narrow"),
        P("wide", None),
    )
    return jax.shard_map(
        shards,
        mesh=mesh,
        in_specs=placed,
        out_specs=(P("wide", "narrow"), P("wide", "narrow")),
        check_vma=False,
    )
```

```python
import functools

import jax
import jax.numpy as jnp
from jax import lax
from jax.experimental import pallas as pl
from jax.experimental.pallas import tpu as pltpu
from jax.sharding import PartitionSpec as P

ITERS = 2
damping = 0.5
LANES = 128
VMEM_LIMIT = 32 * 1024 * 1024
f32, bf16, i32 = jnp.float32, jnp.bfloat16, jnp.int32


def dot(a, b):
    return jnp.dot(a, b, preferred_element_type=f32)


def hot_rows(column, first, width):
    offset = column - lax.broadcasted_iota(i32, column.shape, 1)
    tiles = [(offset == first + t).astype(f32).astype(bf16) for t in range(0, width, LANES)]
    return jnp.concatenate(tiles, axis=1)


def hot_cols(row, first, height):
    numbers = lax.broadcasted_iota(i32, (height, row.shape[1]), 0) + first
    return (numbers == row).astype(f32).astype(bf16)


def hot_pairs(column, row):
    tiles = [
        (column == row[:, t : t + LANES]).astype(f32).astype(bf16) for t in range(0, row.shape[1], LANES)
    ]
    return jnp.concatenate(tiles, axis=1)


def chunks(count, body, parts):
    size = count // parts
    for first in range(0, count, size):
        body(pl.ds(first, size), first)


def product(matrix_ref, vectors, out_ref):
    def rows(at, _):
        out_ref[0, at, :] = dot(matrix_ref[0, at, :], vectors)

    chunks(out_ref.shape[1], rows, 2)


def turned_dot(a, b):
    return lax.dot_general(a, b, (((0,), (0,)), ((), ())), preferred_element_type=f32)


def call(body, grid, in_specs, out_specs, out_shape, scratch, flops, moved, near=(), near_out=()):
    listed = isinstance(out_shape, (list, tuple))
    shapes = [
        (pltpu.VMEM if i in near_out else pltpu.HBM)(x.shape, x.dtype)
        for i, x in enumerate(out_shape if listed else [out_shape])
    ]
    shapes = shapes if listed else shapes[0]
    run = pl.pallas_call(
        body,
        grid=grid,
        in_specs=in_specs,
        out_specs=out_specs,
        out_shape=shapes,
        scratch_shapes=scratch,
        compiler_params=pltpu.CompilerParams(vmem_limit_bytes=VMEM_LIMIT),
        cost_estimate=pl.CostEstimate(flops=int(flops), bytes_accessed=int(moved), transcendentals=0),
    )

    def placed(i, x, spec):
        if spec.memory_space == pltpu.SMEM:
            return x
        return pltpu.with_memory_space_constraint(x, pltpu.VMEM if i in near else pltpu.HBM)

    return lambda *args: run(*(placed(i, x, spec) for i, (x, spec) in enumerate(zip(args, in_specs))))


def flat_call(body, near, out_shape, near_out, scratch, copies, flops, moved, scalar=()):
    def run(*args):
        places = [
            pltpu.SMEM if i in scalar else pltpu.VMEM if i in near else pltpu.HBM for i in range(len(args))
        ]
        out_places = [pltpu.VMEM if i in near_out else pltpu.HBM for i in range(len(out_shape))]
        return pl.pallas_call(
            body,
            in_specs=[pl.BlockSpec(memory_space=p) for p in places],
            out_specs=[pl.BlockSpec(memory_space=p) for p in out_places],
            out_shape=[p(x.shape, x.dtype) for p, x in zip(out_places, out_shape)],
            scratch_shapes=list(scratch) + [pltpu.SemaphoreType.DMA((copies,))],
            compiler_params=pltpu.CompilerParams(vmem_limit_bytes=VMEM_LIMIT),
            cost_estimate=pl.CostEstimate(flops=int(flops), bytes_accessed=int(moved), transcendentals=0),
        )(*(x if i in scalar else pltpu.with_memory_space_constraint(x, p) for i, (x, p) in enumerate(zip(args, places))))

    return run


def begin(sems, first, pairs):
    started = [pltpu.make_async_copy(a, b, sems.at[first + i]) for i, (a, b) in enumerate(pairs)]
    for copy in started:
        copy.start()
    return started


def finish(copies):
    for copy in copies:
        copy.wait()


def whole(shape):
    return pl.BlockSpec(shape, lambda s: (0,) * len(shape))


def open_body(field_ref, matrix_ref, part_ref):
    product(matrix_ref, field_ref[...].astype(bf16), part_ref)


def turn(row_ref, column_ref):
    same = (
        lax.broadcasted_iota(i32, (LANES, LANES), 0) == lax.broadcasted_iota(i32, (LANES, LANES), 1)
    ).astype(f32)
    ones = jnp.ones((LANES, LANES), bf16)
    for t in range(0, row_ref.shape[1], LANES):
        number = row_ref[:, t : t + LANES]
        number = jnp.where(number < 0, -2, number) + 2
        high = number // LANES
        column = dot((same * high.astype(f32)).astype(bf16), ones) * LANES
        column += dot((same * (number - high * LANES).astype(f32)).astype(bf16), ones)
        column_ref[pl.ds(t, LANES), :] = column.astype(i32) - 2


def first_body(row_ref, place_ref, field_ref, out_ref, column_ref, placed_ref, field, low, made, turned, sems):
    parts = 3
    size = field.shape[0] // parts
    loads = begin(
        sems, 0, [(field_ref.at[pl.ds(k * size, size)], field.at[pl.ds(k * size, size)]) for k in range(parts)]
    )
    turn(row_ref, column_ref)
    turn(place_ref, turned)
    stores = begin(sems, parts, [(turned, placed_ref)])
    for k in range(parts):
        loads[k].wait()
        low[pl.ds(k * size, size), :] = field[pl.ds(k * size, size), :].astype(bf16)
    size = made.shape[0] // 2
    for k in range(2):
        at = pl.ds(k * size, size)
        made[at, :] = dot(hot_rows(column_ref[at, :], 0, low.shape[0]), low[...]).astype(bf16)
        stores += begin(sems, parts + 1 + k, [(made.at[at], out_ref.at[at])])
    finish(stores)


def settle_body(sign, has_modes, base_ref, in_ref, row_ref, matrix_ref, *rest):
    if has_modes:
        modes_ref, part_ref, proj_ref, low = rest
    else:
        field_ref, part_ref, low = rest
    core = base_ref.shape[0]
    first = pl.program_id(0) * core

    def fields(at, c):
        added = dot(hot_cols(row_ref[...], first + c, at.size), in_ref[...])
        value = base_ref[at, :] + sign * added
        if not has_modes:
            field_ref[at, :] = value
        low[at, :] = value.astype(bf16)

    chunks(core, fields, 2)
    if has_modes:
        proj_ref[...] = dot(modes_ref[0], low[...])
    product(matrix_ref, low[...], part_ref)


def last_body(sign, base_ref, in_ref, row_ref, field_ref, made, sems):
    stores = []
    parts = sems.shape[0]
    size = made.shape[0] // parts
    for k in range(parts):
        at = pl.ds(k * size, size)
        added = dot(hot_cols(row_ref[...], k * size, size), in_ref[...])
        made[at, :] = base_ref[at, :] + sign * added
        stores += begin(sems, k, [(made.at[at], field_ref.at[at])])
    finish(stores)


def take_margins(in_ref, column_ref, margin_ref):
    def rows(at, _):
        hot = hot_rows(column_ref[at, :], 0, in_ref.shape[0])
        margin_ref[at, :] = dot(hot, in_ref[...]).astype(bf16)

    chunks(margin_ref.shape[0], rows, 2)


def pack(place_ref, outer, packed, out_ref, sems, first):
    stores = []
    size = packed.shape[0] // 2
    for k in range(2):
        at = pl.ds(k * size, size)
        packed[at, :] = dot(hot_cols(place_ref[...], k * size, size), outer[...]).astype(bf16)
        stores += begin(sems, first + k, [(packed.at[at], out_ref.at[at])])
    return stores


def outer_body(
    in_ref, placed_ref, place_ref, matrix_ref, part_ref, margin_ref, out_ref,
    placed, place, matrix, part, margin, outer, packed, sems,
):
    subs, margins, _ = matrix.shape
    core = matrix_ref.shape[1] - margins
    loads = begin(
        sems, 0,
        [
            (placed_ref, placed),
            (place_ref, place),
            (matrix_ref.at[:, core:, core:], matrix),
            (part_ref.at[:, core:, :], part),
        ],
    )
    loads[0].wait()
    take_margins(in_ref, placed, margin)
    stores = begin(sems, 4, [(margin, margin_ref)])
    finish(loads[1:])
    for s in range(subs):
        at = pl.ds(s * margins, margins)
        outer[at, :] = (part[s] + dot(matrix[s], margin[at, :])).astype(bf16)
    finish(stores + pack(place, outer, packed, out_ref, sems, 5))


def project_body(in_ref, placed_ref, modes_ref, proj_ref, margin_ref, out_ref, placed, modes, proj, margin, made, sems):
    subs, count, margins = modes.shape
    core = modes_ref.shape[2] - margins
    loads = begin(sems, 0, [(placed_ref, placed), (modes_ref.at[:, :, core:], modes), (proj_ref, proj)])
    loads[0].wait()
    take_margins(in_ref, placed, margin)
    stores = begin(sems, 3, [(margin, margin_ref)])
    finish(loads[1:])
    for s in range(subs):
        at = pl.ds(s * count, count)
        made[at, :] = (proj[at, :] + dot(modes[s], margin[pl.ds(s * margins, margins), :])).astype(bf16)
    finish(stores + begin(sems, 4, [(made, out_ref)]))


def split(x):
    high = x.astype(bf16)
    return jnp.concatenate([high, (x - high.astype(f32)).astype(bf16)], axis=1)


def both(x):
    half = x.shape[1] // 2
    return x[:, :half] + x[:, half:]


def ready_body(
    margin_ref, place_ref, matrix_ref, part_ref, modes_ref, solved_ref, lift_ref,
    margin, place, matrix, part, modes, outer, solved, lift, sems,
):
    subs, count, margins = modes.shape
    core = matrix_ref.shape[1] - margins
    cols = part.shape[2]
    finish(
        begin(
            sems, 0,
            [
                (margin_ref, margin),
                (matrix_ref.at[:, core:, core:], matrix),
                (part_ref.at[:, core:, :], part),
                (modes_ref.at[:, :, core:], modes),
                (place_ref, place),
            ],
        )
    )
    width = lift.shape[1]
    rows = lax.broadcasted_iota(i32, (count, width), 0)
    lanes = lax.broadcasted_iota(i32, (count, width), 1)
    for s in range(subs):
        at = pl.ds(s * margins, margins)
        outer[at, : 2 * cols] = split(damping * (part[s] + dot(matrix[s], margin[at, :])))
        own = (rows + s * count == lanes).astype(f32).astype(bf16)
        outer[at, 2 * cols :] = turned_dot(modes[s], own).astype(bf16)
    stores = []
    size = solved.shape[0] // 2
    for k in range(2):
        at = pl.ds(k * size, size)
        packed = dot(hot_cols(place[...], k * size, size), outer[...])
        solved[at, :] = both(packed[:, : 2 * cols])
        lift[at, :] = packed[:, 2 * cols :].astype(bf16)
        stores += begin(
            sems, 5 + 2 * k, [(solved.at[at], solved_ref.at[at]), (lift.at[at], lift_ref.at[at])]
        )
    finish(stores)


def coarse_body(side, pair_count, here_ref, *rest):
    pairs, rest = rest[:pair_count], rest[pair_count:]
    inverse_refs = rest[:side]
    solved_ref, lift_ref, coarse_ref, out_ref = rest[side : side + 4]
    inverse, everyone, solved, lift, made, packed, sems = rest[side + 4 :]
    loads = begin(
        sems, 0,
        [(inverse_refs[k], inverse.at[k]) for k in range(side)] + [(lift_ref, lift), (solved_ref, solved)],
    )
    height = made.shape[0]
    for k, pair_ref in enumerate(pairs):
        for j in range(2):
            at = pl.multiple_of((here_ref[1] ^ (2 * k + j)) * height, height)
            everyone[pl.ds(at, height), :] = pair_ref[j * height : (j + 1) * height, :]
    finish(loads[:side])
    value = 0.0
    for k in range(side):
        width = inverse.shape[2]
        at = pl.multiple_of((here_ref[0] ^ k) * width, width)
        value += dot(inverse[k], everyone[pl.ds(at, width), :])
    made[...] = value
    stores = begin(sems, side + 2, [(made, coarse_ref)])
    halves = split(value)
    finish(loads[side:])
    size = packed.shape[0] // 2
    for k in range(2):
        at = pl.ds(k * size, size)
        packed[at, :] = (solved[at, :] + both(dot(lift[at, :], halves))).astype(bf16)
        stores += begin(sems, side + 3 + k, [(packed.at[at], out_ref.at[at])])
    finish(stores)


def inner_body(sign, has_modes, part_ref, matrix_ref, margin_ref, base_ref, column_ref, *rest):
    if has_modes:
        coarse_ref, modes_ref, new_ref, sent_ref, halves, total = rest
    else:
        new_ref, sent_ref, halves, total = rest
    s = pl.program_id(0)
    core = new_ref.shape[0]
    made = part_ref[0] + dot(matrix_ref[0], margin_ref[...])
    if has_modes:
        made = damping * made + both(turned_dot(modes_ref[0], split(coarse_ref[...])))
    value = base_ref[...] + sign * made
    new_ref[...] = value
    halves[...] = split(value)

    @pl.when(s == 0)
    def _():
        total[...] = jnp.zeros_like(total)

    def rows(at, _):
        total[at, :] += dot(hot_rows(column_ref[at, :], s * core, core), halves[...])

    chunks(total.shape[0], rows, 2)

    @pl.when(s == pl.num_programs(0) - 1)
    def _():
        sent_ref[...] = both(total[...])


def relay_body(sign, sent_ref, in_ref, column_ref, row_ref, out_ref, made, sems):
    stores = []
    size = made.shape[0] // 2
    for k in range(2):
        at = pl.ds(k * size, size)
        added = dot(hot_pairs(column_ref[at, :], row_ref[...]), in_ref[...])
        made[at, :] = (sent_ref[at, :] + sign * added).astype(bf16)
        stores += begin(sems, k, [(made.at[at], out_ref.at[at])])
    finish(stores)


def shards(loads, start, stiffness, local_inverse, modes, coarse_inverse, margin_rows):
    owners = lax.axis_size("wide")
    subs, margins = margin_rows.shape
    order = stiffness.shape[1]
    core = order - margins
    held, cols = loads.shape
    count = modes.shape[2]
    coarse_rows = subs * count
    capacity = 3 * subs * margins // (2 * owners)
    slots = owners * capacity
    many = subs * margins
    m_at = core // margins

    flat = margin_rows.reshape(-1)
    source = flat // held
    row = flat - source * held
    onehot = (source[:, None] == jnp.arange(owners, dtype=i32)[None, :]).astype(bf16)
    earlier = (jnp.arange(many)[:, None] > jnp.arange(many)[None, :]).astype(bf16)
    rank = jnp.sum(dot(earlier, onehot) * onehot.astype(f32), axis=1).astype(i32)
    place = source * capacity + rank
    hit = place[:, None] == jnp.arange(slots, dtype=i32)[None, :]
    asked = jnp.sum(jnp.where(hit, row[:, None] + 1, 0), axis=0) - 1

    def trade(x):
        blocks = x.reshape((owners, x.shape[0] // owners) + x.shape[1:])
        got = lax.all_to_all(blocks, "wide", split_axis=0, concat_axis=0, tiled=True)
        return got.reshape(x.shape)

    wanted = trade(asked)
    wanted_row = wanted[None, :]
    place_row = place[None, :]
    modes_turned = jnp.swapaxes(modes, 1, 2)

    rows_spec = pl.BlockSpec((core, cols), lambda s: (s, 0))
    left_spec = pl.BlockSpec((1, order, core), lambda s: (s, 0, 0))
    part_spec = pl.BlockSpec((1, order, cols), lambda s: (s, 0, 0))
    slots_spec = whole((slots, cols))
    held_shape = jax.ShapeDtypeStruct((held, cols), f32)
    part_shape = jax.ShapeDtypeStruct((subs, order, cols), f32)
    slots_low = jax.ShapeDtypeStruct((slots, cols), bf16)
    margin_shape = jax.ShapeDtypeStruct((many, cols), bf16)
    matrix_flops = 2 * subs * order * core * cols
    slot_flops = 2 * held * slots * cols

    going, wanted_column, place_column = flat_call(
        first_body, (0, 1),
        [slots_low, jax.ShapeDtypeStruct((slots, LANES), i32), jax.ShapeDtypeStruct((many, LANES), i32)], (1,),
        [
            pltpu.VMEM((held, cols), f32), pltpu.VMEM((held, cols), bf16), pltpu.VMEM((slots, cols), bf16),
            pltpu.VMEM((many, LANES), i32),
        ],
        6, slot_flops, 4e6,
    )(wanted_row, place_row, start)
    side = lax.axis_size("narrow")
    here = jnp.stack([lax.axis_index("narrow"), lax.axis_index("wide")]).astype(i32)
    begun, own, going = lax.optimization_barrier((start, coarse_inverse.astype(bf16), going))
    pieces = [own] + [
        lax.ppermute(own, "narrow", [(i, i ^ k) for i in range(side)]) for k in range(1, side)
    ]
    part = call(
        open_body, (subs,), [rows_spec, left_spec], part_spec, part_shape, [], matrix_flops, 10e6,
    )(begun, stiffness)

    core_modes_spec = pl.BlockSpec((1, count, core), lambda s: (s, 0, 0))
    outer_modes_spec = pl.BlockSpec((subs, count, margins), lambda s: (0, 0, m_at))

    def settle(sign, base, came, matrices, has_modes):
        specs = [rows_spec, slots_spec, whole((1, slots)), left_spec]
        args = [base, came, wanted_row, matrices]
        outs, shapes = [rows_spec, part_spec], [held_shape, part_shape]
        if has_modes:
            specs.append(core_modes_spec)
            args.append(modes_turned)
            outs = [part_spec, pl.BlockSpec((count, cols), lambda s: (s, 0))]
            shapes = [part_shape, jax.ShapeDtypeStruct((coarse_rows, cols), f32)]
        return call(
            functools.partial(settle_body, sign, has_modes), (subs,), specs, outs, shapes,
            [pltpu.VMEM((core, cols), bf16)], slot_flops + matrix_flops, 14e6, (1, 2),
            (),
        )(*args)

    corner_spec = pl.BlockSpec((subs, margins, margins), lambda s: (0, m_at, m_at))
    part_outer_spec = pl.BlockSpec((subs, margins, cols), lambda s: (0, m_at, 0))
    outer_scratch = [pltpu.VMEM((many, cols), bf16)]

    def inner(sign, base, margin, part, matrices, coarse, near_out=(1,)):
        specs = [
            pl.BlockSpec((1, core, cols), lambda s: (s, 0, 0)),
            pl.BlockSpec((1, core, margins), lambda s: (s, 0, m_at)),
            pl.BlockSpec((margins, cols), lambda s: (s, 0)),
            rows_spec,
            whole((slots, LANES)),
        ]
        args = [part, matrices, margin, base, wanted_column]
        if coarse is not None:
            specs += [
                pl.BlockSpec((count, cols), lambda s: (s, 0)),
                core_modes_spec,
            ]
            args += [coarse, modes_turned]
        return call(
            functools.partial(inner_body, sign, coarse is not None), (subs,), specs, [rows_spec, slots_spec],
            [held_shape, jax.ShapeDtypeStruct((slots, cols), f32)],
            [pltpu.VMEM((core, 2 * cols), bf16), pltpu.VMEM((slots, 2 * cols), f32)], 2 * slot_flops, 8e6,
            (4,), near_out,
        )(*args)

    def relay(sign, sent, came):
        return flat_call(
            functools.partial(relay_body, sign), (0, 1, 2, 3), [slots_low], (), [pltpu.VMEM((slots, cols), bf16)], 2,
            slot_flops // 2, 3e6,
        )(sent, came, wanted_column, wanted_row)[0]

    column_scratch = pltpu.VMEM((many, LANES), i32)
    corner_scratch = [
        pltpu.VMEM((subs, margins, margins), bf16), pltpu.VMEM((subs, margins, cols), f32),
    ]
    margin_scratch = pltpu.VMEM((many, cols), bf16)
    packed_scratch = pltpu.VMEM((slots, cols), bf16)
    modes_scratch = pltpu.VMEM((subs, count, margins), bf16)

    def stiffness_outer(came, part):
        return flat_call(
            outer_body, (0,), [margin_shape, slots_low], (),
            [column_scratch, pltpu.VMEM((1, many), i32)] + corner_scratch
            + [margin_scratch, margin_scratch, packed_scratch],
            7, slot_flops, 3e6,
        )(came, place_column, place_row, stiffness, part)

    field = start
    for step in range(ITERS + 1):
        came = trade(going)
        if step == 0:
            pieces, came = lax.optimization_barrier((pieces, came))
        else:
            field, part = settle(1.0, base, back, stiffness, False)
        margin, going = stiffness_outer(came, part)
        back = trade(going)
        base, sent = inner(-1.0, loads, margin, part, stiffness, None, (0,) if step == ITERS else (1,))
        if step == ITERS:
            break

        going = relay(-1.0, sent, back)
        came = trade(going)
        part, proj = settle(-1.0, base, back, local_inverse, True)
        margin, projection = flat_call(
            project_body, (0,), [margin_shape, jax.ShapeDtypeStruct((coarse_rows, cols), bf16)], (),
            [
                column_scratch, modes_scratch, pltpu.VMEM((coarse_rows, cols), f32), margin_scratch,
                pltpu.VMEM((coarse_rows, cols), bf16),
            ],
            5, slot_flops // 2, 2e6,
        )(came, place_column, modes_turned, proj)
        partner = lax.ppermute(projection, "wide", [(i, i ^ 1) for i in range(owners)])
        pair = jnp.concatenate([projection, partner], axis=0)
        pairs = [pair] + [
            lax.ppermute(pair, "wide", [(i, i ^ k) for i in range(owners)]) for k in range(2, owners, 2)
        ]
        solved, lift = flat_call(
            ready_body, (),
            [jax.ShapeDtypeStruct((slots, cols), f32), jax.ShapeDtypeStruct((slots, coarse_rows), bf16)], (),
            [margin_scratch, pltpu.VMEM((1, many), i32)] + corner_scratch
            + [
                modes_scratch, pltpu.VMEM((many, 2 * cols + coarse_rows), bf16), pltpu.VMEM((slots, cols), f32),
                pltpu.VMEM((slots, coarse_rows), bf16),
            ],
            9, slot_flops, 3e6,
        )(margin, place_row, local_inverse, part, modes_turned)
        coarse, going = flat_call(
            functools.partial(coarse_body, side, len(pairs)), tuple(range(1, len(pairs) + 1)),
            [jax.ShapeDtypeStruct((coarse_rows, cols), f32), slots_low], (),
            [
                pltpu.VMEM((side,) + coarse_inverse.shape, bf16), pltpu.VMEM((owners * coarse_rows, cols), bf16),
                pltpu.VMEM((slots, cols), f32), pltpu.VMEM((slots, coarse_rows), bf16),
                pltpu.VMEM((coarse_rows, cols), f32), packed_scratch,
            ],
            side + 5, slot_flops // 4, 3e6, (0,),
        )(here, *pairs, *pieces, solved, lift)
        back = trade(going)
        base, sent = inner(1.0, field, margin, part, local_inverse, coarse)
        going = relay(1.0, sent, back)

    final = flat_call(
        functools.partial(last_body, -1.0), (0, 1, 2), [held_shape], (), [pltpu.VMEM((held, cols), f32)], 2 * subs,
        slot_flops, 4e6,
    )(base, back, wanted_row)[0]
    return field, final


def solution(mesh):
    placed = (
        P("wide", "narrow"),
        P("wide", "narrow"),
        P("wide", None, None),
        P("wide", None, None),
        P("wide", None, None),
        P("wide", "narrow"),
        P("wide", None),
    )
    return jax.shard_map(
        shards,
        mesh=mesh,
        in_specs=placed,
        out_specs=(P("wide", "narrow"), P("wide", "narrow")),
        check_vma=False,
    )
```

```python
import functools

import jax
import jax.numpy as jnp
from jax import lax
from jax.experimental import pallas as pl
from jax.experimental.pallas import tpu as pltpu
from jax.sharding import PartitionSpec as P

ITERS = 2
damping = 0.5
LANES = 128
VMEM_LIMIT = 32 * 1024 * 1024
f32, bf16, i32 = jnp.float32, jnp.bfloat16, jnp.int32


def dot(a, b):
    return jnp.dot(a, b, preferred_element_type=f32)


def hot_rows(column, first, width):
    offset = column - lax.broadcasted_iota(i32, column.shape, 1)
    tiles = [(offset == first + t).astype(f32).astype(bf16) for t in range(0, width, LANES)]
    return jnp.concatenate(tiles, axis=1)


def hot_cols(row, first, height):
    numbers = lax.broadcasted_iota(i32, (height, row.shape[1]), 0) + first
    return (numbers == row).astype(f32).astype(bf16)


def hot_pairs(column, row):
    tiles = [
        (column == row[:, t : t + LANES]).astype(f32).astype(bf16) for t in range(0, row.shape[1], LANES)
    ]
    return jnp.concatenate(tiles, axis=1)


def chunks(count, body, parts):
    size = count // parts
    for first in range(0, count, size):
        body(pl.ds(first, size), first)


def product(matrix_ref, vectors, out_ref):
    def rows(at, _):
        out_ref[0, at, :] = dot(matrix_ref[0, at, :], vectors)

    chunks(out_ref.shape[1], rows, 2)


def turned_dot(a, b):
    return lax.dot_general(a, b, (((0,), (0,)), ((), ())), preferred_element_type=f32)


def call(body, grid, in_specs, out_specs, out_shape, scratch, flops, moved, near=(), near_out=()):
    listed = isinstance(out_shape, (list, tuple))
    shapes = [
        (pltpu.VMEM if i in near_out else pltpu.HBM)(x.shape, x.dtype)
        for i, x in enumerate(out_shape if listed else [out_shape])
    ]
    shapes = shapes if listed else shapes[0]
    run = pl.pallas_call(
        body,
        grid=grid,
        in_specs=in_specs,
        out_specs=out_specs,
        out_shape=shapes,
        scratch_shapes=scratch,
        compiler_params=pltpu.CompilerParams(vmem_limit_bytes=VMEM_LIMIT),
        cost_estimate=pl.CostEstimate(flops=int(flops), bytes_accessed=int(moved), transcendentals=0),
    )

    def placed(i, x, spec):
        if spec.memory_space == pltpu.SMEM:
            return x
        return pltpu.with_memory_space_constraint(x, pltpu.VMEM if i in near else pltpu.HBM)

    return lambda *args: run(*(placed(i, x, spec) for i, (x, spec) in enumerate(zip(args, in_specs))))


def flat_call(body, near, out_shape, near_out, scratch, copies, flops, moved, scalar=()):
    def run(*args):
        places = [
            pltpu.SMEM if i in scalar else pltpu.VMEM if i in near else pltpu.HBM for i in range(len(args))
        ]
        out_places = [pltpu.VMEM if i in near_out else pltpu.HBM for i in range(len(out_shape))]
        return pl.pallas_call(
            body,
            in_specs=[pl.BlockSpec(memory_space=p) for p in places],
            out_specs=[pl.BlockSpec(memory_space=p) for p in out_places],
            out_shape=[p(x.shape, x.dtype) for p, x in zip(out_places, out_shape)],
            scratch_shapes=list(scratch) + [pltpu.SemaphoreType.DMA((copies,))],
            compiler_params=pltpu.CompilerParams(vmem_limit_bytes=VMEM_LIMIT),
            cost_estimate=pl.CostEstimate(flops=int(flops), bytes_accessed=int(moved), transcendentals=0),
        )(*(x if i in scalar else pltpu.with_memory_space_constraint(x, p) for i, (x, p) in enumerate(zip(args, places))))

    return run


def begin(sems, first, pairs):
    started = [pltpu.make_async_copy(a, b, sems.at[first + i]) for i, (a, b) in enumerate(pairs)]
    for copy in started:
        copy.start()
    return started


def finish(copies):
    for copy in copies:
        copy.wait()


def whole(shape):
    return pl.BlockSpec(shape, lambda s: (0,) * len(shape))


def open_body(field_ref, matrix_ref, part_ref):
    product(matrix_ref, field_ref[...].astype(bf16), part_ref)


def turn(row_ref, column_ref):
    same = (
        lax.broadcasted_iota(i32, (LANES, LANES), 0) == lax.broadcasted_iota(i32, (LANES, LANES), 1)
    ).astype(f32)
    ones = jnp.ones((LANES, LANES), bf16)
    for t in range(0, row_ref.shape[1], LANES):
        number = row_ref[:, t : t + LANES]
        number = jnp.where(number < 0, -2, number) + 2
        high = number // LANES
        column = dot((same * high.astype(f32)).astype(bf16), ones) * LANES
        column += dot((same * (number - high * LANES).astype(f32)).astype(bf16), ones)
        column_ref[pl.ds(t, LANES), :] = column.astype(i32) - 2


def first_body(row_ref, place_ref, field_ref, out_ref, column_ref, placed_ref, field, low, made, turned, sems):
    parts = 3
    size = field.shape[0] // parts
    loads = begin(
        sems, 0, [(field_ref.at[pl.ds(k * size, size)], field.at[pl.ds(k * size, size)]) for k in range(parts)]
    )
    turn(row_ref, column_ref)
    turn(place_ref, turned)
    stores = begin(sems, parts, [(turned, placed_ref)])
    for k in range(parts):
        loads[k].wait()
        low[pl.ds(k * size, size), :] = field[pl.ds(k * size, size), :].astype(bf16)
    size = made.shape[0] // 2
    for k in range(2):
        at = pl.ds(k * size, size)
        made[at, :] = dot(hot_rows(column_ref[at, :], 0, low.shape[0]), low[...]).astype(bf16)
        stores += begin(sems, parts + 1 + k, [(made.at[at], out_ref.at[at])])
    finish(stores)


def settle_body(sign, has_modes, base_ref, in_ref, row_ref, matrix_ref, *rest):
    if has_modes:
        modes_ref, part_ref, proj_ref, low = rest
    else:
        field_ref, part_ref, low = rest
    core = base_ref.shape[0]
    first = pl.program_id(0) * core

    def fields(at, c):
        added = dot(hot_cols(row_ref[...], first + c, at.size), in_ref[...])
        value = base_ref[at, :] + sign * added
        if not has_modes:
            field_ref[at, :] = value
        low[at, :] = value.astype(bf16)

    chunks(core, fields, 2)
    if has_modes:
        proj_ref[...] = dot(modes_ref[0], low[...])
    product(matrix_ref, low[...], part_ref)


def last_body(sign, base_ref, in_ref, row_ref, field_ref, made, sems):
    stores = []
    parts = sems.shape[0]
    size = made.shape[0] // parts
    for k in range(parts):
        at = pl.ds(k * size, size)
        added = dot(hot_cols(row_ref[...], k * size, size), in_ref[...])
        made[at, :] = base_ref[at, :] + sign * added
        stores += begin(sems, k, [(made.at[at], field_ref.at[at])])
    finish(stores)


def take_margins(in_ref, column_ref, margin_ref):
    def rows(at, _):
        hot = hot_rows(column_ref[at, :], 0, in_ref.shape[0])
        margin_ref[at, :] = dot(hot, in_ref[...]).astype(bf16)

    chunks(margin_ref.shape[0], rows, 2)


def pack(place_ref, outer, packed, out_ref, sems, first):
    stores = []
    size = packed.shape[0] // 2
    for k in range(2):
        at = pl.ds(k * size, size)
        packed[at, :] = dot(hot_cols(place_ref[...], k * size, size), outer[...]).astype(bf16)
        stores += begin(sems, first + k, [(packed.at[at], out_ref.at[at])])
    return stores


def outer_body(
    in_ref, placed_ref, place_ref, matrix_ref, part_ref, margin_ref, out_ref,
    placed, place, matrix, part, margin, outer, packed, sems,
):
    subs, margins, _ = matrix.shape
    core = matrix_ref.shape[1] - margins
    loads = begin(
        sems, 0,
        [
            (placed_ref, placed),
            (place_ref, place),
            (matrix_ref.at[:, core:, core:], matrix),
            (part_ref.at[:, core:, :], part),
        ],
    )
    loads[0].wait()
    take_margins(in_ref, placed, margin)
    stores = begin(sems, 4, [(margin, margin_ref)])
    finish(loads[1:])
    for s in range(subs):
        at = pl.ds(s * margins, margins)
        outer[at, :] = (part[s] + dot(matrix[s], margin[at, :])).astype(bf16)
    finish(stores + pack(place, outer, packed, out_ref, sems, 5))


def project_body(in_ref, placed_ref, modes_ref, proj_ref, margin_ref, out_ref, placed, modes, proj, margin, made, sems):
    subs, count, margins = modes.shape
    core = modes_ref.shape[2] - margins
    loads = begin(sems, 0, [(placed_ref, placed), (modes_ref.at[:, :, core:], modes), (proj_ref, proj)])
    loads[0].wait()
    take_margins(in_ref, placed, margin)
    stores = begin(sems, 3, [(margin, margin_ref)])
    finish(loads[1:])
    for s in range(subs):
        at = pl.ds(s * count, count)
        made[at, :] = (proj[at, :] + dot(modes[s], margin[pl.ds(s * margins, margins), :])).astype(bf16)
    finish(stores + begin(sems, 4, [(made, out_ref)]))


def split(x):
    high = x.astype(bf16)
    return jnp.concatenate([high, (x - high.astype(f32)).astype(bf16)], axis=1)


def both(x):
    half = x.shape[1] // 2
    return x[:, :half] + x[:, half:]


def ready_body(
    margin_ref, place_ref, matrix_ref, part_ref, modes_ref, solved_ref, lift_ref,
    margin, place, matrix, part, modes, outer, sems,
):
    subs, count, margins = modes.shape
    core = matrix_ref.shape[1] - margins
    cols = part.shape[2]
    finish(
        begin(
            sems, 0,
            [
                (margin_ref, margin),
                (matrix_ref.at[:, core:, core:], matrix),
                (part_ref.at[:, core:, :], part),
                (modes_ref.at[:, :, core:], modes),
                (place_ref, place),
            ],
        )
    )
    width = lift_ref.shape[1]
    rows = lax.broadcasted_iota(i32, (count, width), 0)
    lanes = lax.broadcasted_iota(i32, (count, width), 1)
    for s in range(subs):
        at = pl.ds(s * margins, margins)
        outer[at, : 2 * cols] = split(damping * (part[s] + dot(matrix[s], margin[at, :])))
        own = (rows + s * count == lanes).astype(f32).astype(bf16)
        outer[at, 2 * cols :] = turned_dot(modes[s], own).astype(bf16)
    size = solved_ref.shape[0] // 2
    for k in range(2):
        at = pl.ds(k * size, size)
        packed = dot(hot_cols(place[...], k * size, size), outer[...])
        solved_ref[at, :] = both(packed[:, : 2 * cols])
        lift_ref[at, :] = packed[:, 2 * cols :].astype(bf16)


def coarse_body(side, pair_count, here_ref, *rest):
    pairs, rest = rest[:pair_count], rest[pair_count:]
    inverse_refs = rest[:side]
    solved_ref, lift_ref, coarse_ref, out_ref = rest[side : side + 4]
    inverse, everyone, made, packed, sems = rest[side + 4 :]
    loads = begin(sems, 0, [(inverse_refs[k], inverse.at[k]) for k in range(side)])
    height = made.shape[0]
    for k, pair_ref in enumerate(pairs):
        for j in range(2):
            at = pl.multiple_of((here_ref[1] ^ (2 * k + j)) * height, height)
            everyone[pl.ds(at, height), :] = pair_ref[j * height : (j + 1) * height, :]
    finish(loads)
    value = 0.0
    for k in range(side):
        width = inverse.shape[2]
        at = pl.multiple_of((here_ref[0] ^ k) * width, width)
        value += dot(inverse[k], everyone[pl.ds(at, width), :])
    made[...] = value
    stores = begin(sems, side, [(made, coarse_ref)])
    halves = split(value)
    size = packed.shape[0] // 2
    for k in range(2):
        at = pl.ds(k * size, size)
        packed[at, :] = (solved_ref[at, :] + both(dot(lift_ref[at, :], halves))).astype(bf16)
        stores += begin(sems, side + 1 + k, [(packed.at[at], out_ref.at[at])])
    finish(stores)


def inner_body(sign, has_modes, part_ref, matrix_ref, margin_ref, base_ref, column_ref, *rest):
    if has_modes:
        coarse_ref, modes_ref, new_ref, sent_ref, halves, total = rest
    else:
        new_ref, sent_ref, halves, total = rest
    s = pl.program_id(0)
    core = new_ref.shape[0]
    made = part_ref[0] + dot(matrix_ref[0], margin_ref[...])
    if has_modes:
        made = damping * made + both(turned_dot(modes_ref[0], split(coarse_ref[...])))
    value = base_ref[...] + sign * made
    new_ref[...] = value
    halves[...] = split(value)

    @pl.when(s == 0)
    def _():
        total[...] = jnp.zeros_like(total)

    def rows(at, _):
        total[at, :] += dot(hot_rows(column_ref[at, :], s * core, core), halves[...])

    chunks(total.shape[0], rows, 2)

    @pl.when(s == pl.num_programs(0) - 1)
    def _():
        sent_ref[...] = both(total[...])


def relay_body(sign, sent_ref, in_ref, column_ref, row_ref, out_ref, made, sems):
    stores = []
    size = made.shape[0] // 2
    for k in range(2):
        at = pl.ds(k * size, size)
        added = dot(hot_pairs(column_ref[at, :], row_ref[...]), in_ref[...])
        made[at, :] = (sent_ref[at, :] + sign * added).astype(bf16)
        stores += begin(sems, k, [(made.at[at], out_ref.at[at])])
    finish(stores)


def shards(loads, start, stiffness, local_inverse, modes, coarse_inverse, margin_rows):
    owners = lax.axis_size("wide")
    subs, margins = margin_rows.shape
    order = stiffness.shape[1]
    core = order - margins
    held, cols = loads.shape
    count = modes.shape[2]
    coarse_rows = subs * count
    capacity = 3 * subs * margins // (2 * owners)
    slots = owners * capacity
    many = subs * margins
    m_at = core // margins

    flat = margin_rows.reshape(-1)
    source = flat // held
    row = flat - source * held
    onehot = (source[:, None] == jnp.arange(owners, dtype=i32)[None, :]).astype(bf16)
    earlier = (jnp.arange(many)[:, None] > jnp.arange(many)[None, :]).astype(bf16)
    rank = jnp.sum(dot(earlier, onehot) * onehot.astype(f32), axis=1).astype(i32)
    place = source * capacity + rank
    hit = place[:, None] == jnp.arange(slots, dtype=i32)[None, :]
    asked = jnp.sum(jnp.where(hit, row[:, None] + 1, 0), axis=0) - 1

    def trade(x):
        blocks = x.reshape((owners, x.shape[0] // owners) + x.shape[1:])
        got = lax.all_to_all(blocks, "wide", split_axis=0, concat_axis=0, tiled=True)
        return got.reshape(x.shape)

    wanted = trade(asked)
    wanted_row = wanted[None, :]
    place_row = place[None, :]
    modes_turned = jnp.swapaxes(modes, 1, 2)

    rows_spec = pl.BlockSpec((core, cols), lambda s: (s, 0))
    left_spec = pl.BlockSpec((1, order, core), lambda s: (s, 0, 0))
    part_spec = pl.BlockSpec((1, order, cols), lambda s: (s, 0, 0))
    slots_spec = whole((slots, cols))
    held_shape = jax.ShapeDtypeStruct((held, cols), f32)
    part_shape = jax.ShapeDtypeStruct((subs, order, cols), f32)
    slots_low = jax.ShapeDtypeStruct((slots, cols), bf16)
    margin_shape = jax.ShapeDtypeStruct((many, cols), bf16)
    matrix_flops = 2 * subs * order * core * cols
    slot_flops = 2 * held * slots * cols

    going, wanted_column, place_column = flat_call(
        first_body, (0, 1),
        [slots_low, jax.ShapeDtypeStruct((slots, LANES), i32), jax.ShapeDtypeStruct((many, LANES), i32)], (1,),
        [
            pltpu.VMEM((held, cols), f32), pltpu.VMEM((held, cols), bf16), pltpu.VMEM((slots, cols), bf16),
            pltpu.VMEM((many, LANES), i32),
        ],
        6, slot_flops, 4e6,
    )(wanted_row, place_row, start)
    side = lax.axis_size("narrow")
    here = jnp.stack([lax.axis_index("narrow"), lax.axis_index("wide")]).astype(i32)
    begun, own, going = lax.optimization_barrier((start, coarse_inverse.astype(bf16), going))
    pieces = [own] + [
        lax.ppermute(own, "narrow", [(i, i ^ k) for i in range(side)]) for k in range(1, side)
    ]
    part = call(
        open_body, (subs,), [rows_spec, left_spec], part_spec, part_shape, [], matrix_flops, 10e6,
    )(begun, stiffness)

    core_modes_spec = pl.BlockSpec((1, count, core), lambda s: (s, 0, 0))
    outer_modes_spec = pl.BlockSpec((subs, count, margins), lambda s: (0, 0, m_at))

    def settle(sign, base, came, matrices, has_modes):
        specs = [rows_spec, slots_spec, whole((1, slots)), left_spec]
        args = [base, came, wanted_row, matrices]
        outs, shapes = [rows_spec, part_spec], [held_shape, part_shape]
        if has_modes:
            specs.append(core_modes_spec)
            args.append(modes_turned)
            outs = [part_spec, pl.BlockSpec((count, cols), lambda s: (s, 0))]
            shapes = [part_shape, jax.ShapeDtypeStruct((coarse_rows, cols), f32)]
        return call(
            functools.partial(settle_body, sign, has_modes), (subs,), specs, outs, shapes,
            [pltpu.VMEM((core, cols), bf16)], slot_flops + matrix_flops, 14e6, (1, 2),
            (),
        )(*args)

    corner_spec = pl.BlockSpec((subs, margins, margins), lambda s: (0, m_at, m_at))
    part_outer_spec = pl.BlockSpec((subs, margins, cols), lambda s: (0, m_at, 0))
    outer_scratch = [pltpu.VMEM((many, cols), bf16)]

    def inner(sign, base, margin, part, matrices, coarse, near_out=(1,)):
        specs = [
            pl.BlockSpec((1, core, cols), lambda s: (s, 0, 0)),
            pl.BlockSpec((1, core, margins), lambda s: (s, 0, m_at)),
            pl.BlockSpec((margins, cols), lambda s: (s, 0)),
            rows_spec,
            whole((slots, LANES)),
        ]
        args = [part, matrices, margin, base, wanted_column]
        if coarse is not None:
            specs += [
                pl.BlockSpec((count, cols), lambda s: (s, 0)),
                core_modes_spec,
            ]
            args += [coarse, modes_turned]
        return call(
            functools.partial(inner_body, sign, coarse is not None), (subs,), specs, [rows_spec, slots_spec],
            [held_shape, jax.ShapeDtypeStruct((slots, cols), f32)],
            [pltpu.VMEM((core, 2 * cols), bf16), pltpu.VMEM((slots, 2 * cols), f32)], 2 * slot_flops, 8e6,
            (4,), near_out,
        )(*args)

    def relay(sign, sent, came):
        return flat_call(
            functools.partial(relay_body, sign), (0, 1, 2, 3), [slots_low], (), [pltpu.VMEM((slots, cols), bf16)], 2,
            slot_flops // 2, 3e6,
        )(sent, came, wanted_column, wanted_row)[0]

    column_scratch = pltpu.VMEM((many, LANES), i32)
    corner_scratch = [
        pltpu.VMEM((subs, margins, margins), bf16), pltpu.VMEM((subs, margins, cols), f32),
    ]
    margin_scratch = pltpu.VMEM((many, cols), bf16)
    packed_scratch = pltpu.VMEM((slots, cols), bf16)
    modes_scratch = pltpu.VMEM((subs, count, margins), bf16)

    def stiffness_outer(came, part):
        return flat_call(
            outer_body, (0,), [margin_shape, slots_low], (),
            [column_scratch, pltpu.VMEM((1, many), i32)] + corner_scratch
            + [margin_scratch, margin_scratch, packed_scratch],
            7, slot_flops, 3e6,
        )(came, place_column, place_row, stiffness, part)

    field = start
    for step in range(ITERS + 1):
        came = trade(going)
        if step == 0:
            pieces, came = lax.optimization_barrier((pieces, came))
        else:
            field, part = settle(1.0, base, back, stiffness, False)
        margin, going = stiffness_outer(came, part)
        back = trade(going)
        base, sent = inner(-1.0, loads, margin, part, stiffness, None, (0,) if step == ITERS else (1,))
        if step == ITERS:
            break

        going = relay(-1.0, sent, back)
        came = trade(going)
        part, proj = settle(-1.0, base, back, local_inverse, True)
        margin, projection = flat_call(
            project_body, (0,), [margin_shape, jax.ShapeDtypeStruct((coarse_rows, cols), bf16)], (),
            [
                column_scratch, modes_scratch, pltpu.VMEM((coarse_rows, cols), f32), margin_scratch,
                pltpu.VMEM((coarse_rows, cols), bf16),
            ],
            5, slot_flops // 2, 2e6,
        )(came, place_column, modes_turned, proj)
        partner = lax.ppermute(projection, "wide", [(i, i ^ 1) for i in range(owners)])
        pair = jnp.concatenate([projection, partner], axis=0)
        pairs = [pair] + [
            lax.ppermute(pair, "wide", [(i, i ^ k) for i in range(owners)]) for k in range(2, owners, 2)
        ]
        solved, lift = flat_call(
            ready_body, (),
            [jax.ShapeDtypeStruct((slots, cols), f32), jax.ShapeDtypeStruct((slots, coarse_rows), bf16)], (0, 1),
            [margin_scratch, pltpu.VMEM((1, many), i32)] + corner_scratch
            + [modes_scratch, pltpu.VMEM((many, 2 * cols + coarse_rows), bf16)],
            5, slot_flops, 3e6,
        )(margin, place_row, local_inverse, part, modes_turned)
        coarse, going = flat_call(
            functools.partial(coarse_body, side, len(pairs)),
            tuple(range(1, len(pairs) + 1)) + (len(pairs) + side + 1, len(pairs) + side + 2),
            [jax.ShapeDtypeStruct((coarse_rows, cols), f32), slots_low], (),
            [
                pltpu.VMEM((side,) + coarse_inverse.shape, bf16), pltpu.VMEM((owners * coarse_rows, cols), bf16),
                pltpu.VMEM((coarse_rows, cols), f32), packed_scratch,
            ],
            side + 3, slot_flops // 4, 3e6, (0,),
        )(here, *pairs, *pieces, solved, lift)
        back = trade(going)
        base, sent = inner(1.0, field, margin, part, local_inverse, coarse)
        going = relay(1.0, sent, back)

    final = flat_call(
        functools.partial(last_body, -1.0), (0, 1, 2), [held_shape], (), [pltpu.VMEM((held, cols), f32)], 2 * subs,
        slot_flops, 4e6,
    )(base, back, wanted_row)[0]
    return field, final


def solution(mesh):
    placed = (
        P("wide", "narrow"),
        P("wide", "narrow"),
        P("wide", None, None),
        P("wide", None, None),
        P("wide", None, None),
        P("wide", "narrow"),
        P("wide", None),
    )
    return jax.shard_map(
        shards,
        mesh=mesh,
        in_specs=placed,
        out_specs=(P("wide", "narrow"), P("wide", "narrow")),
        check_vma=False,
    )
```

```python
import functools

import jax
import jax.numpy as jnp
from jax import lax
from jax.experimental import pallas as pl
from jax.experimental.pallas import tpu as pltpu
from jax.sharding import PartitionSpec as P

ITERS = 2
damping = 0.5
LANES = 128
VMEM_LIMIT = 32 * 1024 * 1024
f32, bf16, i32 = jnp.float32, jnp.bfloat16, jnp.int32


def dot(a, b):
    return jnp.dot(a, b, preferred_element_type=f32)


def hot_rows(column, first, width):
    offset = column - lax.broadcasted_iota(i32, column.shape, 1)
    tiles = [(offset == first + t).astype(f32).astype(bf16) for t in range(0, width, LANES)]
    return jnp.concatenate(tiles, axis=1)


def hot_cols(row, first, height):
    numbers = lax.broadcasted_iota(i32, (height, row.shape[1]), 0) + first
    return (numbers == row).astype(f32).astype(bf16)


def hot_pairs(column, row):
    tiles = [
        (column == row[:, t : t + LANES]).astype(f32).astype(bf16) for t in range(0, row.shape[1], LANES)
    ]
    return jnp.concatenate(tiles, axis=1)


def chunks(count, body, parts):
    size = count // parts
    for first in range(0, count, size):
        body(pl.ds(first, size), first)


def product(matrix_ref, vectors, out_ref):
    def rows(at, _):
        out_ref[0, at, :] = dot(matrix_ref[0, at, :], vectors)

    chunks(out_ref.shape[1], rows, 2)


def turned_dot(a, b):
    return lax.dot_general(a, b, (((0,), (0,)), ((), ())), preferred_element_type=f32)


def call(body, grid, in_specs, out_specs, out_shape, scratch, flops, moved, near=(), near_out=()):
    listed = isinstance(out_shape, (list, tuple))
    shapes = [
        (pltpu.VMEM if i in near_out else pltpu.HBM)(x.shape, x.dtype)
        for i, x in enumerate(out_shape if listed else [out_shape])
    ]
    shapes = shapes if listed else shapes[0]
    run = pl.pallas_call(
        body,
        grid=grid,
        in_specs=in_specs,
        out_specs=out_specs,
        out_shape=shapes,
        scratch_shapes=scratch,
        compiler_params=pltpu.CompilerParams(vmem_limit_bytes=VMEM_LIMIT),
        cost_estimate=pl.CostEstimate(flops=int(flops), bytes_accessed=int(moved), transcendentals=0),
    )

    def placed(i, x, spec):
        if spec.memory_space == pltpu.SMEM:
            return x
        return pltpu.with_memory_space_constraint(x, pltpu.VMEM if i in near else pltpu.HBM)

    return lambda *args: run(*(placed(i, x, spec) for i, (x, spec) in enumerate(zip(args, in_specs))))


def flat_call(body, near, out_shape, near_out, scratch, copies, flops, moved, scalar=()):
    def run(*args):
        places = [
            pltpu.SMEM if i in scalar else pltpu.VMEM if i in near else pltpu.HBM for i in range(len(args))
        ]
        out_places = [pltpu.VMEM if i in near_out else pltpu.HBM for i in range(len(out_shape))]
        return pl.pallas_call(
            body,
            in_specs=[pl.BlockSpec(memory_space=p) for p in places],
            out_specs=[pl.BlockSpec(memory_space=p) for p in out_places],
            out_shape=[p(x.shape, x.dtype) for p, x in zip(out_places, out_shape)],
            scratch_shapes=list(scratch) + [pltpu.SemaphoreType.DMA((copies,))],
            compiler_params=pltpu.CompilerParams(vmem_limit_bytes=VMEM_LIMIT),
            cost_estimate=pl.CostEstimate(flops=int(flops), bytes_accessed=int(moved), transcendentals=0),
        )(*(x if i in scalar else pltpu.with_memory_space_constraint(x, p) for i, (x, p) in enumerate(zip(args, places))))

    return run


def begin(sems, first, pairs):
    started = [pltpu.make_async_copy(a, b, sems.at[first + i]) for i, (a, b) in enumerate(pairs)]
    for copy in started:
        copy.start()
    return started


def finish(copies):
    for copy in copies:
        copy.wait()


def whole(shape):
    return pl.BlockSpec(shape, lambda s: (0,) * len(shape))


def open_body(field_ref, matrix_ref, part_ref):
    product(matrix_ref, field_ref[...].astype(bf16), part_ref)


def turn(row_ref, column_ref):
    same = (
        lax.broadcasted_iota(i32, (LANES, LANES), 0) == lax.broadcasted_iota(i32, (LANES, LANES), 1)
    ).astype(f32)
    ones = jnp.ones((LANES, LANES), bf16)
    for t in range(0, row_ref.shape[1], LANES):
        number = row_ref[:, t : t + LANES]
        number = jnp.where(number < 0, -2, number) + 2
        high = number // LANES
        column = dot((same * high.astype(f32)).astype(bf16), ones) * LANES
        column += dot((same * (number - high * LANES).astype(f32)).astype(bf16), ones)
        column_ref[pl.ds(t, LANES), :] = column.astype(i32) - 2


def first_body(row_ref, place_ref, field_ref, out_ref, column_ref, placed_ref, field, low, made, turned, sems):
    parts = 3
    size = field.shape[0] // parts
    loads = begin(
        sems, 0, [(field_ref.at[pl.ds(k * size, size)], field.at[pl.ds(k * size, size)]) for k in range(parts)]
    )
    turn(row_ref, column_ref)
    turn(place_ref, turned)
    stores = begin(sems, parts, [(turned, placed_ref)])
    for k in range(parts):
        loads[k].wait()
        low[pl.ds(k * size, size), :] = field[pl.ds(k * size, size), :].astype(bf16)
    size = made.shape[0] // 2
    for k in range(2):
        at = pl.ds(k * size, size)
        made[at, :] = dot(hot_rows(column_ref[at, :], 0, low.shape[0]), low[...]).astype(bf16)
        stores += begin(sems, parts + 1 + k, [(made.at[at], out_ref.at[at])])
    finish(stores)


def settle_body(sign, has_modes, base_ref, in_ref, row_ref, matrix_ref, *rest):
    if has_modes:
        modes_ref, part_ref, proj_ref, low = rest
    else:
        field_ref, part_ref, low = rest
    core = base_ref.shape[0]
    first = pl.program_id(0) * core

    def fields(at, c):
        added = dot(hot_cols(row_ref[...], first + c, at.size), in_ref[...])
        value = base_ref[at, :] + sign * added
        if not has_modes:
            field_ref[at, :] = value
        low[at, :] = value.astype(bf16)

    chunks(core, fields, 2)
    if has_modes:
        proj_ref[...] = dot(modes_ref[0], low[...])
    product(matrix_ref, low[...], part_ref)


def last_body(sign, base_ref, in_ref, row_ref, field_ref, made, sems):
    stores = []
    parts = sems.shape[0]
    size = made.shape[0] // parts
    for k in range(parts):
        at = pl.ds(k * size, size)
        added = dot(hot_cols(row_ref[...], k * size, size), in_ref[...])
        made[at, :] = base_ref[at, :] + sign * added
        stores += begin(sems, k, [(made.at[at], field_ref.at[at])])
    finish(stores)


def take_margins(in_ref, column_ref, margin_ref):
    def rows(at, _):
        hot = hot_rows(column_ref[at, :], 0, in_ref.shape[0])
        margin_ref[at, :] = dot(hot, in_ref[...]).astype(bf16)

    chunks(margin_ref.shape[0], rows, 2)


def pack(place_ref, outer, packed, out_ref, sems, first):
    stores = []
    size = packed.shape[0] // 2
    for k in range(2):
        at = pl.ds(k * size, size)
        packed[at, :] = dot(hot_cols(place_ref[...], k * size, size), outer[...]).astype(bf16)
        stores += begin(sems, first + k, [(packed.at[at], out_ref.at[at])])
    return stores


def outer_body(
    in_ref, placed_ref, place_ref, matrix_ref, part_ref, margin_ref, out_ref,
    placed, place, matrix, part, margin, outer, packed, sems,
):
    subs, margins, _ = matrix.shape
    core = matrix_ref.shape[1] - margins
    loads = begin(
        sems, 0,
        [
            (placed_ref, placed),
            (place_ref, place),
            (matrix_ref.at[:, core:, core:], matrix),
            (part_ref.at[:, core:, :], part),
        ],
    )
    loads[0].wait()
    take_margins(in_ref, placed, margin)
    stores = begin(sems, 4, [(margin, margin_ref)])
    finish(loads[1:])
    for s in range(subs):
        at = pl.ds(s * margins, margins)
        outer[at, :] = (part[s] + dot(matrix[s], margin[at, :])).astype(bf16)
    finish(stores + pack(place, outer, packed, out_ref, sems, 5))


def project_body(in_ref, placed_ref, modes_ref, proj_ref, margin_ref, out_ref, placed, modes, proj, margin, made, sems):
    subs, count, margins = modes.shape
    core = modes_ref.shape[2] - margins
    loads = begin(sems, 0, [(placed_ref, placed), (modes_ref.at[:, :, core:], modes), (proj_ref, proj)])
    loads[0].wait()
    take_margins(in_ref, placed, margin)
    stores = begin(sems, 3, [(margin, margin_ref)])
    finish(loads[1:])
    for s in range(subs):
        at = pl.ds(s * count, count)
        made[at, :] = (proj[at, :] + dot(modes[s], margin[pl.ds(s * margins, margins), :])).astype(bf16)
    finish(stores + begin(sems, 4, [(made, out_ref)]))


def split(x):
    high = x.astype(bf16)
    return jnp.concatenate([high, (x - high.astype(f32)).astype(bf16)], axis=1)


def both(x):
    half = x.shape[1] // 2
    return x[:, :half] + x[:, half:]


def ready_body(
    margin_ref, place_ref, matrix_ref, part_ref, modes_ref, solved_ref, lift_ref,
    margin, place, matrix, part, modes, outer, sems,
):
    subs, count, margins = modes.shape
    core = matrix_ref.shape[1] - margins
    cols = part.shape[2]
    finish(
        begin(
            sems, 0,
            [
                (margin_ref, margin),
                (matrix_ref.at[:, core:, core:], matrix),
                (part_ref.at[:, core:, :], part),
                (modes_ref.at[:, :, core:], modes),
                (place_ref, place),
            ],
        )
    )
    width = lift_ref.shape[1]
    rows = lax.broadcasted_iota(i32, (count, width), 0)
    lanes = lax.broadcasted_iota(i32, (count, width), 1)
    for s in range(subs):
        at = pl.ds(s * margins, margins)
        outer[at, : 2 * cols] = split(damping * (part[s] + dot(matrix[s], margin[at, :])))
        own = (rows + s * count == lanes).astype(f32).astype(bf16)
        outer[at, 2 * cols :] = turned_dot(modes[s], own).astype(bf16)
    size = solved_ref.shape[0] // 2
    for k in range(2):
        at = pl.ds(k * size, size)
        packed = dot(hot_cols(place[...], k * size, size), outer[...])
        solved_ref[at, :] = both(packed[:, : 2 * cols])
        lift_ref[at, :] = packed[:, 2 * cols :].astype(bf16)


def coarse_body(side, share_count, here_ref, *rest):
    shares, rest = rest[:share_count], rest[share_count:]
    inverse_refs = rest[:side]
    solved_ref, lift_ref, coarse_ref, out_ref = rest[side : side + 4]
    inverse, everyone, made, packed, sems = rest[side + 4 :]
    loads = begin(sems, 0, [(inverse_refs[k], inverse.at[k]) for k in range(side)])
    height = made.shape[0]
    for k, share_ref in enumerate(shares):
        at = pl.multiple_of((here_ref[1] ^ k) * height, height)
        everyone[pl.ds(at, height), :] = share_ref[...]
    finish(loads)
    value = 0.0
    for k in range(side):
        width = inverse.shape[2]
        at = pl.multiple_of((here_ref[0] ^ k) * width, width)
        value += dot(inverse[k], everyone[pl.ds(at, width), :])
    made[...] = value
    stores = begin(sems, side, [(made, coarse_ref)])
    halves = split(value)
    size = packed.shape[0] // 2
    for k in range(2):
        at = pl.ds(k * size, size)
        packed[at, :] = (solved_ref[at, :] + both(dot(lift_ref[at, :], halves))).astype(bf16)
        stores += begin(sems, side + 1 + k, [(packed.at[at], out_ref.at[at])])
    finish(stores)


def inner_body(sign, has_modes, part_ref, matrix_ref, margin_ref, base_ref, column_ref, *rest):
    if has_modes:
        coarse_ref, modes_ref, new_ref, sent_ref, halves, total = rest
    else:
        new_ref, sent_ref, halves, total = rest
    s = pl.program_id(0)
    core = new_ref.shape[0]
    made = part_ref[0] + dot(matrix_ref[0], margin_ref[...])
    if has_modes:
        made = damping * made + both(turned_dot(modes_ref[0], split(coarse_ref[...])))
    value = base_ref[...] + sign * made
    new_ref[...] = value
    halves[...] = split(value)

    @pl.when(s == 0)
    def _():
        total[...] = jnp.zeros_like(total)

    def rows(at, _):
        total[at, :] += dot(hot_rows(column_ref[at, :], s * core, core), halves[...])

    chunks(total.shape[0], rows, 2)

    @pl.when(s == pl.num_programs(0) - 1)
    def _():
        sent_ref[...] = both(total[...])


def relay_body(sign, sent_ref, in_ref, column_ref, row_ref, out_ref, made, sems):
    stores = []
    size = made.shape[0] // 2
    for k in range(2):
        at = pl.ds(k * size, size)
        added = dot(hot_pairs(column_ref[at, :], row_ref[...]), in_ref[...])
        made[at, :] = (sent_ref[at, :] + sign * added).astype(bf16)
        stores += begin(sems, k, [(made.at[at], out_ref.at[at])])
    finish(stores)


def shards(loads, start, stiffness, local_inverse, modes, coarse_inverse, margin_rows):
    owners = lax.axis_size("wide")
    subs, margins = margin_rows.shape
    order = stiffness.shape[1]
    core = order - margins
    held, cols = loads.shape
    count = modes.shape[2]
    coarse_rows = subs * count
    capacity = 3 * subs * margins // (2 * owners)
    slots = owners * capacity
    many = subs * margins
    m_at = core // margins

    flat = margin_rows.reshape(-1)
    source = flat // held
    row = flat - source * held
    onehot = (source[:, None] == jnp.arange(owners, dtype=i32)[None, :]).astype(bf16)
    earlier = (jnp.arange(many)[:, None] > jnp.arange(many)[None, :]).astype(bf16)
    rank = jnp.sum(dot(earlier, onehot) * onehot.astype(f32), axis=1).astype(i32)
    place = source * capacity + rank
    slot = jnp.arange(slots, dtype=i32).reshape(1, owners, 1, capacity)
    here_hit = place[:, None, None, None] == slot
    asked = jnp.sum(jnp.where(here_hit, row[:, None, None, None] + 1, 0), axis=0)

    def trade(x):
        blocks = x.reshape((owners, x.shape[0] // owners) + x.shape[1:])
        got = lax.all_to_all(blocks, "wide", split_axis=0, concat_axis=0, tiled=True)
        return got.reshape(x.shape)

    wanted = lax.all_to_all(asked, "wide", split_axis=0, concat_axis=0, tiled=True).reshape(slots) - 1
    wanted_row = wanted[None, :]
    place_row = place[None, :]
    modes_turned = jnp.swapaxes(modes, 1, 2)

    rows_spec = pl.BlockSpec((core, cols), lambda s: (s, 0))
    left_spec = pl.BlockSpec((1, order, core), lambda s: (s, 0, 0))
    part_spec = pl.BlockSpec((1, order, cols), lambda s: (s, 0, 0))
    slots_spec = whole((slots, cols))
    held_shape = jax.ShapeDtypeStruct((held, cols), f32)
    part_shape = jax.ShapeDtypeStruct((subs, order, cols), f32)
    slots_low = jax.ShapeDtypeStruct((slots, cols), bf16)
    margin_shape = jax.ShapeDtypeStruct((many, cols), bf16)
    matrix_flops = 2 * subs * order * core * cols
    slot_flops = 2 * held * slots * cols

    going, wanted_column, place_column = flat_call(
        first_body, (0, 1),
        [slots_low, jax.ShapeDtypeStruct((slots, LANES), i32), jax.ShapeDtypeStruct((many, LANES), i32)], (1,),
        [
            pltpu.VMEM((held, cols), f32), pltpu.VMEM((held, cols), bf16), pltpu.VMEM((slots, cols), bf16),
            pltpu.VMEM((many, LANES), i32),
        ],
        6, slot_flops, 4e6,
    )(wanted_row, place_row, start)
    side = lax.axis_size("narrow")
    here = jnp.stack([lax.axis_index("narrow"), lax.axis_index("wide")]).astype(i32)
    begun, own, going = lax.optimization_barrier((start, coarse_inverse.astype(bf16), going))
    pieces = [own] + [
        lax.ppermute(own, "narrow", [(i, i ^ k) for i in range(side)]) for k in range(1, side)
    ]
    part = call(
        open_body, (subs,), [rows_spec, left_spec], part_spec, part_shape, [], matrix_flops, 10e6,
    )(begun, stiffness)

    core_modes_spec = pl.BlockSpec((1, count, core), lambda s: (s, 0, 0))
    outer_modes_spec = pl.BlockSpec((subs, count, margins), lambda s: (0, 0, m_at))

    def settle(sign, base, came, matrices, has_modes):
        specs = [rows_spec, slots_spec, whole((1, slots)), left_spec]
        args = [base, came, wanted_row, matrices]
        outs, shapes = [rows_spec, part_spec], [held_shape, part_shape]
        if has_modes:
            specs.append(core_modes_spec)
            args.append(modes_turned)
            outs = [part_spec, pl.BlockSpec((count, cols), lambda s: (s, 0))]
            shapes = [part_shape, jax.ShapeDtypeStruct((coarse_rows, cols), f32)]
        return call(
            functools.partial(settle_body, sign, has_modes), (subs,), specs, outs, shapes,
            [pltpu.VMEM((core, cols), bf16)], slot_flops + matrix_flops, 14e6, (1, 2),
            (),
        )(*args)

    corner_spec = pl.BlockSpec((subs, margins, margins), lambda s: (0, m_at, m_at))
    part_outer_spec = pl.BlockSpec((subs, margins, cols), lambda s: (0, m_at, 0))
    outer_scratch = [pltpu.VMEM((many, cols), bf16)]

    def inner(sign, base, margin, part, matrices, coarse, near_out=(1,)):
        specs = [
            pl.BlockSpec((1, core, cols), lambda s: (s, 0, 0)),
            pl.BlockSpec((1, core, margins), lambda s: (s, 0, m_at)),
            pl.BlockSpec((margins, cols), lambda s: (s, 0)),
            rows_spec,
            whole((slots, LANES)),
        ]
        args = [part, matrices, margin, base, wanted_column]
        if coarse is not None:
            specs += [
                pl.BlockSpec((count, cols), lambda s: (s, 0)),
                core_modes_spec,
            ]
            args += [coarse, modes_turned]
        return call(
            functools.partial(inner_body, sign, coarse is not None), (subs,), specs, [rows_spec, slots_spec],
            [held_shape, jax.ShapeDtypeStruct((slots, cols), f32)],
            [pltpu.VMEM((core, 2 * cols), bf16), pltpu.VMEM((slots, 2 * cols), f32)], 2 * slot_flops, 8e6,
            (4,), near_out,
        )(*args)

    def relay(sign, sent, came):
        return flat_call(
            functools.partial(relay_body, sign), (0, 1, 2, 3), [slots_low], (), [pltpu.VMEM((slots, cols), bf16)], 2,
            slot_flops // 2, 3e6,
        )(sent, came, wanted_column, wanted_row)[0]

    column_scratch = pltpu.VMEM((many, LANES), i32)
    corner_scratch = [
        pltpu.VMEM((subs, margins, margins), bf16), pltpu.VMEM((subs, margins, cols), f32),
    ]
    margin_scratch = pltpu.VMEM((many, cols), bf16)
    packed_scratch = pltpu.VMEM((slots, cols), bf16)
    modes_scratch = pltpu.VMEM((subs, count, margins), bf16)

    def stiffness_outer(came, part):
        return flat_call(
            outer_body, (0,), [margin_shape, slots_low], (),
            [column_scratch, pltpu.VMEM((1, many), i32)] + corner_scratch
            + [margin_scratch, margin_scratch, packed_scratch],
            7, slot_flops, 3e6,
        )(came, place_column, place_row, stiffness, part)

    field = start
    for step in range(ITERS + 1):
        came = trade(going)
        if step == 0:
            pieces, came = lax.optimization_barrier((pieces, came))
        else:
            field, part = settle(1.0, base, back, stiffness, False)
        margin, going = stiffness_outer(came, part)
        back = trade(going)
        base, sent = inner(-1.0, loads, margin, part, stiffness, None, (0,) if step == ITERS else (1,))
        if step == ITERS:
            break

        going = relay(-1.0, sent, back)
        came = trade(going)
        part, proj = settle(-1.0, base, back, local_inverse, True)
        margin, projection = flat_call(
            project_body, (0,), [margin_shape, jax.ShapeDtypeStruct((coarse_rows, cols), bf16)], (),
            [
                column_scratch, modes_scratch, pltpu.VMEM((coarse_rows, cols), f32), margin_scratch,
                pltpu.VMEM((coarse_rows, cols), bf16),
            ],
            5, slot_flops // 2, 2e6,
        )(came, place_column, modes_turned, proj)
        partner = lax.ppermute(projection, "wide", [(i, i ^ 1) for i in range(owners)])
        shares = []
        for k in range(0, owners, 2):
            for x in (projection, partner):
                shares.append(lax.ppermute(x, "wide", [(i, i ^ k) for i in range(owners)]) if k > 0 else x)
        solved, lift = flat_call(
            ready_body, (),
            [jax.ShapeDtypeStruct((slots, cols), f32), jax.ShapeDtypeStruct((slots, coarse_rows), bf16)], (0, 1),
            [margin_scratch, pltpu.VMEM((1, many), i32)] + corner_scratch
            + [modes_scratch, pltpu.VMEM((many, 2 * cols + coarse_rows), bf16)],
            5, slot_flops, 3e6,
        )(margin, place_row, local_inverse, part, modes_turned)
        coarse, going = flat_call(
            functools.partial(coarse_body, side, len(shares)),
            tuple(range(1, len(shares) + 1)) + (len(shares) + side + 1, len(shares) + side + 2),
            [jax.ShapeDtypeStruct((coarse_rows, cols), f32), slots_low], (),
            [
                pltpu.VMEM((side,) + coarse_inverse.shape, bf16), pltpu.VMEM((owners * coarse_rows, cols), bf16),
                pltpu.VMEM((coarse_rows, cols), f32), packed_scratch,
            ],
            side + 3, slot_flops // 4, 3e6, (0,),
        )(here, *shares, *pieces, solved, lift)
        back = trade(going)
        base, sent = inner(1.0, field, margin, part, local_inverse, coarse)
        going = relay(1.0, sent, back)

    final = flat_call(
        functools.partial(last_body, -1.0), (0, 1, 2), [held_shape], (), [pltpu.VMEM((held, cols), f32)], 2 * subs,
        slot_flops, 4e6,
    )(base, back, wanted_row)[0]
    return field, final


def solution(mesh):
    placed = (
        P("wide", "narrow"),
        P("wide", "narrow"),
        P("wide", None, None),
        P("wide", None, None),
        P("wide", None, None),
        P("wide", "narrow"),
        P("wide", None),
    )
    return jax.shard_map(
        shards,
        mesh=mesh,
        in_specs=placed,
        out_specs=(P("wide", "narrow"), P("wide", "narrow")),
        check_vma=False,
    )
```

```python
import functools

import jax
import jax.numpy as jnp
from jax import lax
from jax.experimental import pallas as pl
from jax.experimental.pallas import tpu as pltpu
from jax.sharding import PartitionSpec as P

ITERS = 2
damping = 0.5
LANES = 128
VMEM_LIMIT = 32 * 1024 * 1024
f32, bf16, i32 = jnp.float32, jnp.bfloat16, jnp.int32


def dot(a, b):
    return jnp.dot(a, b, preferred_element_type=f32)


def hot_rows(column, first, width):
    offset = column - lax.broadcasted_iota(i32, column.shape, 1)
    tiles = [(offset == first + t).astype(f32).astype(bf16) for t in range(0, width, LANES)]
    return jnp.concatenate(tiles, axis=1)


def hot_cols(row, first, height):
    numbers = lax.broadcasted_iota(i32, (height, row.shape[1]), 0) + first
    return (numbers == row).astype(f32).astype(bf16)


def hot_pairs(column, row):
    tiles = [
        (column == row[:, t : t + LANES]).astype(f32).astype(bf16) for t in range(0, row.shape[1], LANES)
    ]
    return jnp.concatenate(tiles, axis=1)


def chunks(count, body, parts):
    size = count // parts
    for first in range(0, count, size):
        body(pl.ds(first, size), first)


def product(matrix_ref, vectors, out_ref):
    def rows(at, _):
        out_ref[0, at, :] = dot(matrix_ref[0, at, :], vectors)

    chunks(out_ref.shape[1], rows, 2)


def turned_dot(a, b):
    return lax.dot_general(a, b, (((0,), (0,)), ((), ())), preferred_element_type=f32)


def call(body, grid, in_specs, out_specs, out_shape, scratch, flops, moved, near=(), near_out=()):
    listed = isinstance(out_shape, (list, tuple))
    shapes = [
        (pltpu.VMEM if i in near_out else pltpu.HBM)(x.shape, x.dtype)
        for i, x in enumerate(out_shape if listed else [out_shape])
    ]
    shapes = shapes if listed else shapes[0]
    run = pl.pallas_call(
        body,
        grid=grid,
        in_specs=in_specs,
        out_specs=out_specs,
        out_shape=shapes,
        scratch_shapes=scratch,
        compiler_params=pltpu.CompilerParams(vmem_limit_bytes=VMEM_LIMIT),
        cost_estimate=pl.CostEstimate(flops=int(flops), bytes_accessed=int(moved), transcendentals=0),
    )

    def placed(i, x, spec):
        if spec.memory_space == pltpu.SMEM:
            return x
        return pltpu.with_memory_space_constraint(x, pltpu.VMEM if i in near else pltpu.HBM)

    return lambda *args: run(*(placed(i, x, spec) for i, (x, spec) in enumerate(zip(args, in_specs))))


def flat_call(body, near, out_shape, near_out, scratch, copies, flops, moved, scalar=()):
    def run(*args):
        places = [
            pltpu.SMEM if i in scalar else pltpu.VMEM if i in near else pltpu.HBM for i in range(len(args))
        ]
        out_places = [pltpu.VMEM if i in near_out else pltpu.HBM for i in range(len(out_shape))]
        return pl.pallas_call(
            body,
            in_specs=[pl.BlockSpec(memory_space=p) for p in places],
            out_specs=[pl.BlockSpec(memory_space=p) for p in out_places],
            out_shape=[p(x.shape, x.dtype) for p, x in zip(out_places, out_shape)],
            scratch_shapes=list(scratch) + [pltpu.SemaphoreType.DMA((copies,))],
            compiler_params=pltpu.CompilerParams(vmem_limit_bytes=VMEM_LIMIT),
            cost_estimate=pl.CostEstimate(flops=int(flops), bytes_accessed=int(moved), transcendentals=0),
        )(*(x if i in scalar else pltpu.with_memory_space_constraint(x, p) for i, (x, p) in enumerate(zip(args, places))))

    return run


def begin(sems, first, pairs):
    started = [pltpu.make_async_copy(a, b, sems.at[first + i]) for i, (a, b) in enumerate(pairs)]
    for copy in started:
        copy.start()
    return started


def finish(copies):
    for copy in copies:
        copy.wait()


def whole(shape):
    return pl.BlockSpec(shape, lambda s: (0,) * len(shape))


def open_body(field_ref, matrix_ref, part_ref):
    product(matrix_ref, field_ref[...].astype(bf16), part_ref)


def turn(row_ref, column_ref):
    same = (
        lax.broadcasted_iota(i32, (LANES, LANES), 0) == lax.broadcasted_iota(i32, (LANES, LANES), 1)
    ).astype(f32)
    ones = jnp.ones((LANES, LANES), bf16)
    for t in range(0, row_ref.shape[1], LANES):
        number = row_ref[:, t : t + LANES]
        number = jnp.where(number < 0, -2, number) + 2
        high = number // LANES
        column = dot((same * high.astype(f32)).astype(bf16), ones) * LANES
        column += dot((same * (number - high * LANES).astype(f32)).astype(bf16), ones)
        column_ref[pl.ds(t, LANES), :] = column.astype(i32) - 2


def first_body(row_ref, place_ref, field_ref, out_ref, column_ref, placed_ref, field, low, made, turned, sems):
    parts = 3
    size = field.shape[0] // parts
    loads = begin(
        sems, 0, [(field_ref.at[pl.ds(k * size, size)], field.at[pl.ds(k * size, size)]) for k in range(parts)]
    )
    turn(row_ref, column_ref)
    turn(place_ref, turned)
    stores = begin(sems, parts, [(turned, placed_ref)])
    for k in range(parts):
        loads[k].wait()
        low[pl.ds(k * size, size), :] = field[pl.ds(k * size, size), :].astype(bf16)
    size = made.shape[0] // 2
    for k in range(2):
        at = pl.ds(k * size, size)
        made[at, :] = dot(hot_rows(column_ref[at, :], 0, low.shape[0]), low[...]).astype(bf16)
        stores += begin(sems, parts + 1 + k, [(made.at[at], out_ref.at[at])])
    finish(stores)


def settle_body(sign, has_modes, base_ref, in_ref, row_ref, matrix_ref, *rest):
    if has_modes:
        modes_ref, part_ref, proj_ref, low = rest
    else:
        field_ref, part_ref, low = rest
    core = base_ref.shape[0]
    first = pl.program_id(0) * core

    def fields(at, c):
        added = dot(hot_cols(row_ref[...], first + c, at.size), in_ref[...])
        value = base_ref[at, :] + sign * added
        if not has_modes:
            field_ref[at, :] = value
        low[at, :] = value.astype(bf16)

    chunks(core, fields, 2)
    if has_modes:
        proj_ref[...] = dot(modes_ref[0], low[...])
    product(matrix_ref, low[...], part_ref)


def last_body(sign, base_ref, in_ref, row_ref, field_ref, made, sems):
    stores = []
    parts = sems.shape[0]
    size = made.shape[0] // parts
    for k in range(parts):
        at = pl.ds(k * size, size)
        added = dot(hot_cols(row_ref[...], k * size, size), in_ref[...])
        made[at, :] = base_ref[at, :] + sign * added
        stores += begin(sems, k, [(made.at[at], field_ref.at[at])])
    finish(stores)


def take_margins(in_ref, column_ref, margin_ref):
    def rows(at, _):
        hot = hot_rows(column_ref[at, :], 0, in_ref.shape[0])
        margin_ref[at, :] = dot(hot, in_ref[...]).astype(bf16)

    chunks(margin_ref.shape[0], rows, 2)


def pack(place_ref, outer, packed, out_ref, sems, first):
    stores = []
    size = packed.shape[0] // 2
    for k in range(2):
        at = pl.ds(k * size, size)
        packed[at, :] = dot(hot_cols(place_ref[...], k * size, size), outer[...]).astype(bf16)
        stores += begin(sems, first + k, [(packed.at[at], out_ref.at[at])])
    return stores


def outer_body(
    in_ref, placed_ref, place_ref, matrix_ref, part_ref, margin_ref, out_ref,
    placed, place, matrix, part, margin, outer, packed, sems,
):
    subs, margins, _ = matrix.shape
    core = matrix_ref.shape[1] - margins
    loads = begin(
        sems, 0,
        [
            (placed_ref, placed),
            (place_ref, place),
            (matrix_ref.at[:, core:, core:], matrix),
            (part_ref.at[:, core:, :], part),
        ],
    )
    loads[0].wait()
    take_margins(in_ref, placed, margin)
    stores = begin(sems, 4, [(margin, margin_ref)])
    finish(loads[1:])
    for s in range(subs):
        at = pl.ds(s * margins, margins)
        outer[at, :] = (part[s] + dot(matrix[s], margin[at, :])).astype(bf16)
    finish(stores + pack(place, outer, packed, out_ref, sems, 5))


def project_body(in_ref, placed_ref, modes_ref, proj_ref, margin_ref, out_ref, placed, modes, proj, margin, sems):
    subs, count, margins = modes.shape
    core = modes_ref.shape[2] - margins
    loads = begin(sems, 0, [(placed_ref, placed), (modes_ref.at[:, :, core:], modes), (proj_ref, proj)])
    loads[0].wait()
    take_margins(in_ref, placed, margin)
    stores = begin(sems, 3, [(margin, margin_ref)])
    finish(loads[1:])
    for s in range(subs):
        at = pl.ds(s * count, count)
        out_ref[at, :] = (proj[at, :] + dot(modes[s], margin[pl.ds(s * margins, margins), :])).astype(bf16)
    finish(stores)


def split(x):
    high = x.astype(bf16)
    return jnp.concatenate([high, (x - high.astype(f32)).astype(bf16)], axis=1)


def both(x):
    half = x.shape[1] // 2
    return x[:, :half] + x[:, half:]


def ready_body(
    margin_ref, place_ref, matrix_ref, part_ref, modes_ref, solved_ref, lift_ref,
    margin, place, matrix, part, modes, outer, sems,
):
    subs, count, margins = modes.shape
    core = matrix_ref.shape[1] - margins
    cols = part.shape[2]
    finish(
        begin(
            sems, 0,
            [
                (margin_ref, margin),
                (matrix_ref.at[:, core:, core:], matrix),
                (part_ref.at[:, core:, :], part),
                (modes_ref.at[:, :, core:], modes),
                (place_ref, place),
            ],
        )
    )
    width = lift_ref.shape[1]
    rows = lax.broadcasted_iota(i32, (count, width), 0)
    lanes = lax.broadcasted_iota(i32, (count, width), 1)
    for s in range(subs):
        at = pl.ds(s * margins, margins)
        outer[at, : 2 * cols] = split(damping * (part[s] + dot(matrix[s], margin[at, :])))
        own = (rows + s * count == lanes).astype(f32).astype(bf16)
        outer[at, 2 * cols :] = turned_dot(modes[s], own).astype(bf16)
    size = solved_ref.shape[0] // 2
    for k in range(2):
        at = pl.ds(k * size, size)
        packed = dot(hot_cols(place[...], k * size, size), outer[...])
        solved_ref[at, :] = both(packed[:, : 2 * cols])
        lift_ref[at, :] = packed[:, 2 * cols :].astype(bf16)


def coarse_body(side, pair_count, here_ref, *rest):
    pairs, rest = rest[:pair_count], rest[pair_count:]
    inverse_refs = rest[:side]
    solved_ref, lift_ref, coarse_ref, out_ref = rest[side : side + 4]
    inverse, everyone, made, packed, sems = rest[side + 4 :]
    loads = begin(sems, 0, [(inverse_refs[k], inverse.at[k]) for k in range(side)])
    height = made.shape[0]
    for k, pair_ref in enumerate(pairs):
        for j in range(2):
            at = pl.multiple_of((here_ref[1] ^ (2 * k + j)) * height, height)
            everyone[pl.ds(at, height), :] = pair_ref[j * height : (j + 1) * height, :]
    finish(loads)
    value = 0.0
    for k in range(side):
        width = inverse.shape[2]
        at = pl.multiple_of((here_ref[0] ^ k) * width, width)
        value += dot(inverse[k], everyone[pl.ds(at, width), :])
    made[...] = value
    stores = begin(sems, side, [(made, coarse_ref)])
    halves = split(value)
    size = packed.shape[0] // 2
    for k in range(2):
        at = pl.ds(k * size, size)
        packed[at, :] = (solved_ref[at, :] + both(dot(lift_ref[at, :], halves))).astype(bf16)
        stores += begin(sems, side + 1 + k, [(packed.at[at], out_ref.at[at])])
    finish(stores)


def inner_body(sign, has_modes, part_ref, matrix_ref, margin_ref, base_ref, column_ref, *rest):
    if has_modes:
        coarse_ref, modes_ref, new_ref, sent_ref, halves, total = rest
    else:
        new_ref, sent_ref, halves, total = rest
    s = pl.program_id(0)
    core = new_ref.shape[0]
    made = part_ref[0] + dot(matrix_ref[0], margin_ref[...])
    if has_modes:
        made = damping * made + both(turned_dot(modes_ref[0], split(coarse_ref[...])))
    value = base_ref[...] + sign * made
    new_ref[...] = value
    halves[...] = split(value)

    @pl.when(s == 0)
    def _():
        total[...] = jnp.zeros_like(total)

    def rows(at, _):
        total[at, :] += dot(hot_rows(column_ref[at, :], s * core, core), halves[...])

    chunks(total.shape[0], rows, 2)

    @pl.when(s == pl.num_programs(0) - 1)
    def _():
        sent_ref[...] = both(total[...])


def relay_body(sign, sent_ref, in_ref, column_ref, row_ref, out_ref, made, sems):
    stores = []
    size = made.shape[0] // 2
    for k in range(2):
        at = pl.ds(k * size, size)
        added = dot(hot_pairs(column_ref[at, :], row_ref[...]), in_ref[...])
        made[at, :] = (sent_ref[at, :] + sign * added).astype(bf16)
        stores += begin(sems, k, [(made.at[at], out_ref.at[at])])
    finish(stores)


def shards(loads, start, stiffness, local_inverse, modes, coarse_inverse, margin_rows):
    owners = lax.axis_size("wide")
    subs, margins = margin_rows.shape
    order = stiffness.shape[1]
    core = order - margins
    held, cols = loads.shape
    count = modes.shape[2]
    coarse_rows = subs * count
    capacity = 3 * subs * margins // (2 * owners)
    slots = owners * capacity
    many = subs * margins
    m_at = core // margins

    flat = margin_rows.reshape(-1)
    source = flat // held
    row = flat - source * held
    onehot = (source[:, None] == jnp.arange(owners, dtype=i32)[None, :]).astype(bf16)
    earlier = (jnp.arange(many)[:, None] > jnp.arange(many)[None, :]).astype(bf16)
    rank = jnp.sum(dot(earlier, onehot) * onehot.astype(f32), axis=1).astype(i32)
    place = source * capacity + rank
    hit = place[:, None] == jnp.arange(slots, dtype=i32)[None, :]
    asked = jnp.sum(jnp.where(hit, row[:, None] + 1, 0), axis=0) - 1

    def trade(x):
        blocks = x.reshape((owners, x.shape[0] // owners) + x.shape[1:])
        got = lax.all_to_all(blocks, "wide", split_axis=0, concat_axis=0, tiled=True)
        return got.reshape(x.shape)

    wanted = trade(asked)
    wanted_row = wanted[None, :]
    place_row = place[None, :]
    modes_turned = jnp.swapaxes(modes, 1, 2)

    rows_spec = pl.BlockSpec((core, cols), lambda s: (s, 0))
    left_spec = pl.BlockSpec((1, order, core), lambda s: (s, 0, 0))
    part_spec = pl.BlockSpec((1, order, cols), lambda s: (s, 0, 0))
    slots_spec = whole((slots, cols))
    held_shape = jax.ShapeDtypeStruct((held, cols), f32)
    part_shape = jax.ShapeDtypeStruct((subs, order, cols), f32)
    slots_low = jax.ShapeDtypeStruct((slots, cols), bf16)
    margin_shape = jax.ShapeDtypeStruct((many, cols), bf16)
    matrix_flops = 2 * subs * order * core * cols
    slot_flops = 2 * held * slots * cols

    going, wanted_column, place_column = flat_call(
        first_body, (0, 1),
        [slots_low, jax.ShapeDtypeStruct((slots, LANES), i32), jax.ShapeDtypeStruct((many, LANES), i32)], (1,),
        [
            pltpu.VMEM((held, cols), f32), pltpu.VMEM((held, cols), bf16), pltpu.VMEM((slots, cols), bf16),
            pltpu.VMEM((many, LANES), i32),
        ],
        6, slot_flops, 4e6,
    )(wanted_row, place_row, start)
    side = lax.axis_size("narrow")
    here = jnp.stack([lax.axis_index("narrow"), lax.axis_index("wide")]).astype(i32)
    begun, own, going = lax.optimization_barrier((start, coarse_inverse.astype(bf16), going))
    pieces = [own] + [
        lax.ppermute(own, "narrow", [(i, i ^ k) for i in range(side)]) for k in range(1, side)
    ]
    part = call(
        open_body, (subs,), [rows_spec, left_spec], part_spec, part_shape, [], matrix_flops, 10e6,
    )(begun, stiffness)

    core_modes_spec = pl.BlockSpec((1, count, core), lambda s: (s, 0, 0))
    outer_modes_spec = pl.BlockSpec((subs, count, margins), lambda s: (0, 0, m_at))

    def settle(sign, base, came, matrices, has_modes):
        specs = [rows_spec, slots_spec, whole((1, slots)), left_spec]
        args = [base, came, wanted_row, matrices]
        outs, shapes = [rows_spec, part_spec], [held_shape, part_shape]
        if has_modes:
            specs.append(core_modes_spec)
            args.append(modes_turned)
            outs = [part_spec, pl.BlockSpec((count, cols), lambda s: (s, 0))]
            shapes = [part_shape, jax.ShapeDtypeStruct((coarse_rows, cols), f32)]
        return call(
            functools.partial(settle_body, sign, has_modes), (subs,), specs, outs, shapes,
            [pltpu.VMEM((core, cols), bf16)], slot_flops + matrix_flops, 14e6, (1, 2),
            (),
        )(*args)

    corner_spec = pl.BlockSpec((subs, margins, margins), lambda s: (0, m_at, m_at))
    part_outer_spec = pl.BlockSpec((subs, margins, cols), lambda s: (0, m_at, 0))
    outer_scratch = [pltpu.VMEM((many, cols), bf16)]

    def inner(sign, base, margin, part, matrices, coarse, near_out=(1,)):
        specs = [
            pl.BlockSpec((1, core, cols), lambda s: (s, 0, 0)),
            pl.BlockSpec((1, core, margins), lambda s: (s, 0, m_at)),
            pl.BlockSpec((margins, cols), lambda s: (s, 0)),
            rows_spec,
            whole((slots, LANES)),
        ]
        args = [part, matrices, margin, base, wanted_column]
        if coarse is not None:
            specs += [
                pl.BlockSpec((count, cols), lambda s: (s, 0)),
                core_modes_spec,
            ]
            args += [coarse, modes_turned]
        return call(
            functools.partial(inner_body, sign, coarse is not None), (subs,), specs, [rows_spec, slots_spec],
            [held_shape, jax.ShapeDtypeStruct((slots, cols), f32)],
            [pltpu.VMEM((core, 2 * cols), bf16), pltpu.VMEM((slots, 2 * cols), f32)], 2 * slot_flops, 8e6,
            (4,), near_out,
        )(*args)

    def relay(sign, sent, came):
        return flat_call(
            functools.partial(relay_body, sign), (0, 1, 2, 3), [slots_low], (), [pltpu.VMEM((slots, cols), bf16)], 2,
            slot_flops // 2, 3e6,
        )(sent, came, wanted_column, wanted_row)[0]

    column_scratch = pltpu.VMEM((many, LANES), i32)
    corner_scratch = [
        pltpu.VMEM((subs, margins, margins), bf16), pltpu.VMEM((subs, margins, cols), f32),
    ]
    margin_scratch = pltpu.VMEM((many, cols), bf16)
    packed_scratch = pltpu.VMEM((slots, cols), bf16)
    modes_scratch = pltpu.VMEM((subs, count, margins), bf16)

    def stiffness_outer(came, part):
        return flat_call(
            outer_body, (0,), [margin_shape, slots_low], (),
            [column_scratch, pltpu.VMEM((1, many), i32)] + corner_scratch
            + [margin_scratch, margin_scratch, packed_scratch],
            7, slot_flops, 3e6,
        )(came, place_column, place_row, stiffness, part)

    field = start
    for step in range(ITERS + 1):
        came = trade(going)
        if step == 0:
            pieces, came = lax.optimization_barrier((pieces, came))
        else:
            field, part = settle(1.0, base, back, stiffness, False)
        margin, going = stiffness_outer(came, part)
        back = trade(going)
        base, sent = inner(-1.0, loads, margin, part, stiffness, None, (0,) if step == ITERS else (1,))
        if step == ITERS:
            break

        going = relay(-1.0, sent, back)
        came = trade(going)
        part, proj = settle(-1.0, base, back, local_inverse, True)
        margin, projection = flat_call(
            project_body, (0,), [margin_shape, jax.ShapeDtypeStruct((coarse_rows, cols), bf16)], (1,),
            [column_scratch, modes_scratch, pltpu.VMEM((coarse_rows, cols), f32), margin_scratch],
            4, slot_flops // 2, 2e6,
        )(came, place_column, modes_turned, proj)
        partner = lax.ppermute(projection, "wide", [(i, i ^ 1) for i in range(owners)])
        pair = jnp.concatenate([projection, partner], axis=0)
        pairs = [pair] + [
            lax.ppermute(pair, "wide", [(i, i ^ k) for i in range(owners)]) for k in range(2, owners, 2)
        ]
        solved, lift = flat_call(
            ready_body, (),
            [jax.ShapeDtypeStruct((slots, cols), f32), jax.ShapeDtypeStruct((slots, coarse_rows), bf16)], (0, 1),
            [margin_scratch, pltpu.VMEM((1, many), i32)] + corner_scratch
            + [modes_scratch, pltpu.VMEM((many, 2 * cols + coarse_rows), bf16)],
            5, slot_flops, 3e6,
        )(margin, place_row, local_inverse, part, modes_turned)
        coarse, going = flat_call(
            functools.partial(coarse_body, side, len(pairs)),
            tuple(range(1, len(pairs) + 1)) + (len(pairs) + side + 1, len(pairs) + side + 2),
            [jax.ShapeDtypeStruct((coarse_rows, cols), f32), slots_low], (),
            [
                pltpu.VMEM((side,) + coarse_inverse.shape, bf16), pltpu.VMEM((owners * coarse_rows, cols), bf16),
                pltpu.VMEM((coarse_rows, cols), f32), packed_scratch,
            ],
            side + 3, slot_flops // 4, 3e6, (0,),
        )(here, *pairs, *pieces, solved, lift)
        back = trade(going)
        base, sent = inner(1.0, field, margin, part, local_inverse, coarse)
        going = relay(1.0, sent, back)

    final = flat_call(
        functools.partial(last_body, -1.0), (0, 1, 2), [held_shape], (), [pltpu.VMEM((held, cols), f32)], 2 * subs,
        slot_flops, 4e6,
    )(base, back, wanted_row)[0]
    return field, final


def solution(mesh):
    placed = (
        P("wide", "narrow"),
        P("wide", "narrow"),
        P("wide", None, None),
        P("wide", None, None),
        P("wide", None, None),
        P("wide", "narrow"),
        P("wide", None),
    )
    return jax.shard_map(
        shards,
        mesh=mesh,
        in_specs=placed,
        out_specs=(P("wide", "narrow"), P("wide", "narrow")),
        check_vma=False,
    )
```
